32 devices in a mesh: batch: 2 (over x), pos: 8 (over z, core), ch: 2 (over y).
Axes of the slice: x: 2, y: 2, z: 4, core: 2. Of those that a mesh axis runs over, the one named last changes fastest.
Arguments:
- section_input: bfloat16 [2, 2, 8192, 1280], P(None, 'batch', 'pos', 'ch')
- norm1_gain: float32 [1280], P('ch'), may hold values from 0.1 to 1.9
- norm1_bias: float32 [1280], P('ch'), may hold values from -3 to 3
- conv1_weight: bfloat16 [6400, 1536], P(None, 'ch'), may hold values from -0.078125 to 0.078125
- conv1_bias: float32 [1536], P('ch'), may hold values from -3 to 3
- norm2_gain: float32 [1536], P('ch'), may hold values from 0.1 to 1.9
- norm2_bias: float32 [1536], P('ch'), may hold values from -3 to 3
- conv2_weight: bfloat16 [1536, 1536], P(None, 'ch'), may hold values from -0.15625 to 0.15625
- conv2_bias: float32 [1536], P('ch'), may hold values from -3 to 3
- pool_weight: bfloat16 [1536, 1536], P(None, 'ch'), may hold values from -0.3125 to 0.3125
- out_grad: bfloat16 [2, 2, 4096, 1536], P(None, 'batch', 'pos', 'ch'), may hold values from -8 to 8
- clip_table: float32 [8], replicated, may hold values from 0.5 to 3
- clip_index: int32 [2], replicated, may hold values from 0 to 7
Outputs:
- section_output: bfloat16 [2, 2, 4096, 1536], P(None, 'batch', 'pos', 'ch')
- input_grad: bfloat16 [2, 2, 8192, 1280], P(None, 'batch', 'pos', 'ch')
- grad_norm1_gain: float32 [1280], P('ch')
- grad_norm1_bias: float32 [1280], P('ch')
- grad_conv1_weight: float32 [6400, 1536], P(('batch', 'pos'), 'ch')
- grad_conv1_bias: float32 [1536], P('ch')
- grad_norm2_gain: float32 [1536], P('ch')
- grad_norm2_bias: float32 [1536], P('ch')
- grad_conv2_weight: float32 [1536, 1536], P(('batch', 'pos'), 'ch')
- grad_conv2_bias: float32 [1536], P('ch')
- grad_pool_weight: float32 [1536, 1536], P(('batch', 'pos'), 'ch')
The draws below stay inside these ranges and needn't reach their ends.
All inputs are finite; a program needn't handle non-finite values.
Results may differ from the reference program's by a relative error of at most 0.017.
Values may be sent and summed in bfloat16 or wider, within the bound.
A program may use at most 384 MiB of HBM per device.

```python
import math
import jax
import jax.numpy as jnp
from jax import lax

CIN = 1280
COUT = 1536
KW = 5
NT = 8
LEN = 8192
MICRO = 2
SEQS = 2
BINS = 4096


def draw_section_input(key, part):
    key = jax.random.fold_in(key, 7)
    keys = jax.random.split(key, 4)
    full_shape = (MICRO, SEQS, LEN, CIN)
    base = jnp.clip(jax.random.normal(keys[0], full_shape, jnp.float32), -6.0, 6.0)
    offsets = 0.5 * jax.random.normal(keys[1], (CIN,), jnp.float32)
    row_scale = jnp.exp(jax.random.uniform(keys[2], (MICRO, SEQS, LEN, 1), jnp.float32, 0.0, math.log(3.0)))
    trend = jnp.exp(math.log(3.0) * jnp.arange(LEN, dtype=jnp.float32) / (LEN - 1)).reshape(1, 1, LEN, 1)
    col_scale = jnp.exp(jax.random.uniform(keys[3], (CIN,), jnp.float32, math.log(0.5), math.log(2.0)))
    return ((base + offsets) * row_scale * trend * col_scale).astype(jnp.bfloat16)


def block_scale(rng, extent, pieces, smallest, high):
    def one(axis_at, shards_of):
        draws = jax.random.uniform(jax.random.fold_in(jax.random.fold_in(rng, 6), axis_at), (shards_of,), jnp.float32, smallest / len(pieces), high / len(pieces))
        return jnp.repeat(jnp.exp(draws), extent[axis_at] // shards_of).reshape((-1,) + (1,) * (len(extent) - axis_at - 1))

    level = one(*pieces[0])
    for cut in pieces[1:]:
        level = level * one(*cut)
    return level


def normal_values(key, dims, scale, reach, shards=(), kind=jnp.bfloat16):
    factor_of = block_scale(key, dims, shards, -0.22, 0.18) if shards else 1.0
    entries = jax.random.normal(key, dims, jnp.float32) * scale * factor_of
    return jnp.minimum(jnp.maximum(entries, -reach), reach).astype(kind)


def setup_inputs(seed: int = 0) -> dict:
    key_list = jax.random.split(jax.random.key(seed), 14)
    return {
        "section_input": draw_section_input(jax.random.fold_in(key_list[13], 71), 0),
        "norm1_gain": jnp.clip(1.0 + 0.18 * jax.random.normal(key_list[1], (CIN,), jnp.float32), 0.1, 1.9),
        "norm1_bias": normal_values(key_list[2], (CIN,), 0.5, 3.0, ((0, 2),), jnp.float32),
        "conv1_weight": normal_values(key_list[3], (KW * CIN, COUT), (KW * CIN) ** -0.5, 0.078125, ((1, 2),)),
        "conv1_bias": normal_values(key_list[4], (COUT,), 0.5, 3.0, ((0, 2),), jnp.float32),
        "norm2_gain": jnp.clip(1.0 + 0.18 * jax.random.normal(key_list[5], (COUT,), jnp.float32), 0.1, 1.9),
        "norm2_bias": normal_values(key_list[6], (COUT,), 0.5, 3.0, ((0, 2),), jnp.float32),
        "conv2_weight": normal_values(key_list[7], (COUT, COUT), COUT ** -0.5, 0.15625, ((1, 2),)),
        "conv2_bias": normal_values(key_list[8], (COUT,), 0.5, 3.0, ((0, 2),), jnp.float32),
        "pool_weight": normal_values(key_list[9], (COUT, COUT), (COUT // 4) ** -0.5, 0.3125, ((1, 2),)),
        "out_grad": normal_values(key_list[10], (MICRO, SEQS, BINS, COUT), 1.5, 8.0, ((1, 2), (2, 8), (3, 2))),
        "clip_table": jnp.clip(jnp.exp(jax.random.uniform(key_list[11], (NT,), jnp.float32, math.log(0.5), math.log(3.0))), 0.5, 3.0),
        "clip_index": jax.random.randint(key_list[12], (MICRO,), 0, NT).astype(jnp.int32),
    }


EPS = 1e-05

@jax.custom_vjp
def low(v):
    return lax.optimization_barrier(v.astype(jnp.bfloat16)).astype(jnp.float32)

@jax.custom_vjp
def low_back(v):
    return v

def low_keep(v):
    return (low(v), None)

def low_pass(kept, grad):
    return (grad,)

def back_keep(v):
    return (v, None)

def back_low(kept, grad):
    return (low(grad),)
low.defvjp(low_keep, low_pass)
low_back.defvjp(back_keep, back_low)

def normalize(values, gain_vec, bias_vec):
    center = lax.optimization_barrier(jnp.mean(values, axis=(0, 1)))
    square = lax.optimization_barrier(jnp.mean(values * values, axis=(0, 1)))
    inverse = lax.rsqrt(square - center * center + EPS)
    return (values - center) * inverse * gain_vec + bias_vec

def pool_pairs(logits, values):
    pair_shape = (values.shape[0], values.shape[1] // 2, 2, values.shape[2])
    weights = jax.nn.softmax(logits.reshape(pair_shape), axis=2)
    return lax.optimization_barrier(jnp.sum(weights * values.reshape(pair_shape), axis=2))

def channel_product(left, right):
    return jnp.einsum('slc,co->slo', left, right, precision=lax.Precision.HIGHEST)

def forward(inputs, norm1_gain, norm1_bias, conv1_weight, conv1_bias, norm2_gain, norm2_bias, conv2_weight, conv2_bias, pool_weight):
    rim_width = KW // 2
    hidden_one = low(jax.nn.gelu(normalize(inputs, norm1_gain, norm1_bias)))
    padded = jnp.pad(hidden_one, ((0, 0), (rim_width, rim_width), (0, 0)))
    kernel = conv1_weight.reshape(KW, CIN, COUT)
    conv_out = conv1_bias
    for offset in range(KW):
        conv_out = conv_out + channel_product(padded[:, offset:offset + LEN], kernel[offset])
    first_out = low_back(conv_out)
    hidden_two = low(jax.nn.gelu(normalize(first_out, norm2_gain, norm2_bias)))
    branch = low_back(channel_product(hidden_two, conv2_weight) + conv2_bias)
    second_out = first_out + branch
    logits = low_back(channel_product(low(second_out), pool_weight))
    return pool_pairs(logits, second_out)

def reference(section_input, norm1_gain, norm1_bias, conv1_weight, conv1_bias, norm2_gain, norm2_bias, conv2_weight, conv2_bias, pool_weight, out_grad, clip_table, clip_index):
    params = tuple((param.astype(jnp.float32) for param in (norm1_gain, norm1_bias, conv1_weight, conv1_bias, norm2_gain, norm2_bias, conv2_weight, conv2_bias, pool_weight)))
    outputs = []
    input_grads = []
    totals = None
    for micro_step in range(MICRO):
        section_out, pull = jax.vjp(forward, section_input[micro_step].astype(jnp.float32), *params)
        limit = clip_table[clip_index[micro_step]]
        clipped = limit * jnp.tanh(out_grad[micro_step].astype(jnp.float32) / limit)
        grads = pull(clipped)
        outputs.append(section_out.astype(jnp.bfloat16))
        input_grads.append(grads[0].astype(jnp.bfloat16))
        if totals is None:
            totals = grads[1:]
        else:
            totals = tuple((total + update for total, update in zip(totals, grads[1:])))
    return (jnp.stack(outputs), jnp.stack(input_grads), totals[0], totals[1], totals[2], totals[3], totals[4], totals[5], totals[6], totals[7], totals[8])
```

```python
import functools

import jax
import jax.numpy as jnp
from jax import lax
from jax.experimental import pallas as pl
from jax.experimental.pallas import tpu as pltpu
from jax.sharding import PartitionSpec as P

KW = 5
RIM = KW // 2
PIECES = KW + 1
EPS = 1e-05
MESH = pl.DeviceIdType.MESH
C0 = 0.7978845608028654
C1 = 0.044715
F32 = jnp.float32
BF16 = jnp.bfloat16
VMEM_LIMIT = 60 * 1024 * 1024

NT = (((1,), (1,)), ((), ()))
TN = (((0,), (0,)), ((), ()))


def params(**kw):
    return pltpu.CompilerParams(vmem_limit_bytes=VMEM_LIMIT, **kw)


def gelu(u):
    return 0.5 * u * (1.0 + jnp.tanh(C0 * (u + C1 * u * u * u)))


def gelu_slope(u):
    square = u * u
    t = jnp.tanh(C0 * (u + C1 * square * u))
    return 0.5 * (1.0 + t) + 0.5 * u * (1.0 - t * t) * (C0 + (3.0 * C0 * C1) * square)


def reduce_kernel(v_ref, o_ref, near, mid, far, near_send, near_recv, far_send, far_recv):
    batch, pos, ch = (lax.axis_index(a) for a in ("batch", "pos", "ch"))
    pos_count = lax.axis_size("pos")
    me = batch * 2 + ch
    barrier = pltpu.get_barrier_semaphore()
    peers = []
    for step in range(1, 4):
        other = lax.rem(me + step, 4)
        peers.append((other // 2, pos, lax.rem(other, 2)))
    for step in range(1, pos_count):
        peers.append((batch, lax.rem(pos + step, pos_count), ch))
    for peer in peers:
        pl.semaphore_signal(barrier, inc=1, device_id=peer, device_id_type=MESH)
    near[pl.ds(me, 1)] = v_ref[...][None]
    pl.semaphore_wait(barrier, len(peers))
    copies = [
        pltpu.make_async_remote_copy(
            v_ref, near.at[me], near_send.at[i], near_recv.at[i], device_id=peer, device_id_type=MESH
        )
        for i, peer in enumerate(peers[:3])
    ]
    for copy in copies:
        copy.start()
    for copy in copies:
        copy.wait()
    mid[...] = (near[0] + near[1]) + (near[2] + near[3])
    far[pl.ds(pos, 1)] = mid[...][None]
    copies = [
        pltpu.make_async_remote_copy(
            mid, far.at[pos], far_send.at[i], far_recv.at[i], device_id=peer, device_id_type=MESH
        )
        for i, peer in enumerate(peers[3:])
    ]
    for copy in copies:
        copy.start()
    for copy in copies:
        copy.wait()
    total = far[0]
    for i in range(1, pos_count):
        total = total + far[i]
    o_ref[...] = total


def reduce_all(values, collective_id):
    rows, width = values.shape
    padded = -(-rows // 8) * 8
    values = jnp.pad(values, ((0, padded - rows), (0, 0)))
    pos_count = lax.axis_size("pos")
    shape = (padded, width)
    total = pl.pallas_call(
        reduce_kernel,
        out_shape=jax.ShapeDtypeStruct(shape, F32),
        in_specs=[pl.BlockSpec(memory_space=pltpu.VMEM)],
        out_specs=pl.BlockSpec(memory_space=pltpu.VMEM),
        scratch_shapes=[
            pltpu.VMEM((4,) + shape, F32),
            pltpu.VMEM(shape, F32),
            pltpu.VMEM((pos_count,) + shape, F32),
            pltpu.SemaphoreType.DMA((3,)),
            pltpu.SemaphoreType.DMA((3,)),
            pltpu.SemaphoreType.DMA((pos_count - 1,)),
            pltpu.SemaphoreType.DMA((pos_count - 1,)),
        ],
        compiler_params=params(collective_id=collective_id, has_side_effects=True),
    )(values)
    return total[:rows]


def hidden_kernel(who, x_ref, vec_ref, h_ref, x_out, scr, raw):
    micro, order = pl.program_id(0), pl.program_id(1)
    half = h_ref.shape[3] * 2
    lanes, ext = scr.shape[:2]
    side = jnp.bitwise_xor(who[0], order)
    begin = pl.multiple_of(side * half, 16)
    first = who[1] + side * half - RIM
    total = who[2]
    center = vec_ref[0, 0:1, :]
    scale = vec_ref[0, 1:2, :]
    bias = vec_ref[0, 2:3, :]

    @pl.loop(0, ext // 16)
    def _(i):
        at = pl.multiple_of(i * 16, 16)
        x = x_ref[0, pl.ds(begin + at, 16), :].astype(F32)
        act = (x - center) * scale + bias
        row = first + at + lax.broadcasted_iota(jnp.int32, x.shape, 0)
        inside = jnp.logical_and(row >= 0, row < total)
        hidden = jnp.where(inside, gelu(act), 0.0)
        for b in range(lanes):
            scr[b, pl.ds(at, 16), :] = hidden[:, b * 128 : (b + 1) * 128]
            raw[b, pl.ds(at, 16), :] = x[:, b * 128 : (b + 1) * 128]

    pairs = half // 2

    @pl.loop(0, pairs // 16)
    def _(i):
        at = pl.multiple_of(i * 16, 16)
        for b in range(lanes):
            lane = slice(b * 128, (b + 1) * 128)
            for d in range(PIECES):
                h_ref[0, d, 0, pl.ds(at, 16), lane] = scr[b, pl.ds(d + 2 * at, 16, stride=2), :].astype(BF16)
            for e in range(2):
                x_out[0, e, 0, pl.ds(at, 16), lane] = raw[
                    b, pl.ds(RIM + e + 2 * at, 16, stride=2), :
                ].astype(BF16)


def make_hidden(who, x_ext, vecs, half):
    micro_count, rows, wide = x_ext.shape
    ext = half + 16
    pairs = half // 2
    return pl.pallas_call(
        hidden_kernel,
        out_shape=(
            jax.ShapeDtypeStruct((2, PIECES, micro_count, pairs, wide), BF16),
            jax.ShapeDtypeStruct((2, 2, micro_count, pairs, wide), BF16),
        ),
        grid_spec=pltpu.PrefetchScalarGridSpec(
            num_scalar_prefetch=1,
            grid=(micro_count, 2),
            in_specs=[
                pl.BlockSpec((1, rows, wide), lambda m, o, w: (m, 0, 0)),
                pl.BlockSpec((1, 8, wide), lambda m, o, w: (m, 0, 0)),
            ],
            out_specs=(
                pl.BlockSpec((1, PIECES, 1, pairs, wide), lambda m, o, w: (o, 0, m, 0, 0)),
                pl.BlockSpec((1, 2, 1, pairs, wide), lambda m, o, w: (o, 0, m, 0, 0)),
            ),
            scratch_shapes=[pltpu.VMEM((wide // 128, ext, 128), F32)] * 2,
        ),
        compiler_params=params(),
        name="hidden",
    )(who, x_ext, vecs)


def conv_kernel(h_ref, w_ref, b_ref, o_ref, s_ref):
    micro_count, pairs = o_ref.shape[1:3]
    rows = micro_count * pairs
    wide = h_ref.shape[2]
    sums = [[0.0, 0.0] for _ in range(micro_count)]
    for e in range(2):
        acc = jnp.dot(h_ref[e], w_ref[0:wide, :], preferred_element_type=F32)
        for k in range(1, KW):
            acc += jnp.dot(
                h_ref[k + e], w_ref[k * wide : (k + 1) * wide, :], preferred_element_type=F32
            )
        acc += b_ref[...]
        for m in range(micro_count):
            part = acc[m * pairs : (m + 1) * pairs]
            o_ref[e, m] = part
            sums[m][0] += jnp.sum(part, axis=0, keepdims=True)
            sums[m][1] += jnp.sum(part * part, axis=0, keepdims=True)
    for m in range(micro_count):
        for i in range(2):
            s_ref[2 * m + i : 2 * m + i + 1, :] = sums[m][i]


def conv_forward(pieces, weight, bias, tile=256):
    _, micro_count, pairs, wide = pieces.shape
    out = weight.shape[1]
    rows = micro_count * pairs
    return pl.pallas_call(
        conv_kernel,
        out_shape=(
            jax.ShapeDtypeStruct((2, micro_count, pairs, out), F32),
            jax.ShapeDtypeStruct((8, out), F32),
        ),
        grid=(out // tile,),
        in_specs=[
            pl.BlockSpec((PIECES, rows, wide), lambda j: (0, 0, 0)),
            pl.BlockSpec((KW * wide, tile), lambda j: (0, j)),
            pl.BlockSpec((1, tile), lambda j: (0, j)),
        ],
        out_specs=(
            pl.BlockSpec((2, micro_count, pairs, tile), lambda j: (0, 0, 0, j)),
            pl.BlockSpec((8, tile), lambda j: (0, j)),
        ),
        compiler_params=params(),
        name="conv_forward",
    )(pieces.reshape(PIECES, rows, wide), weight, bias.reshape(1, out))


def middle_kernel(
    fo_ref,
    fx_ref,
    vec_ref,
    w2_ref,
    wp_ref,
    og_ref,
    lim_ref,
    pooled_ref,
    hid_ref,
    branch_ref,
    diff_ref,
    lg_ref,
    a2g_ref,
    sg_ref,
    sum_ref,
    so,
):
    pairs = og_ref.shape[2]
    rows = 2 * pairs
    wide = w2_ref.shape[0]
    half = wide // 2
    tile = 256
    tiles = wide // tile

    def columns(j):
        return pl.ds(pl.multiple_of(j * tile, tile), tile)

    def load_first(j, e):
        own = j < tiles // 2
        at = pl.ds(pl.multiple_of(lax.rem(j, tiles // 2) * tile, tile), tile)
        return jnp.where(own, fo_ref[e, 0, :, at], fx_ref[e, 0, :, at])

    @pl.loop(0, tiles)
    def _(j):
        c = columns(j)
        for e in range(2):
            f = load_first(j, e)
            act = (f - vec_ref[0, 0:1, c]) * vec_ref[0, 1:2, c] * vec_ref[0, 2:3, c] + vec_ref[0, 3:4, c]
            hid_ref[0, pl.ds(e * pairs, pairs), c] = gelu(act).astype(BF16)

    @pl.loop(0, tiles)
    def _(j):
        c = columns(j)
        branch = jnp.dot(hid_ref[0], w2_ref[:, c], preferred_element_type=F32)
        even = branch[:pairs] + (load_first(j, 0) + vec_ref[0, 4:5, c])
        odd = branch[pairs:] + (load_first(j, 1) + vec_ref[0, 4:5, c])
        so[0, :, c] = even
        so[1, :, c] = odd
        diff_ref[0, :, c] = (even - odd).astype(BF16)

    limit = lim_ref[0, 0:1, 0:1]
    inverse_limit = 1.0 / limit

    @pl.loop(0, tiles)
    def _(j):
        c = columns(j)
        d = jnp.dot(diff_ref[0], wp_ref[:, c], preferred_element_type=F32)
        t = jnp.tanh(0.5 * d)
        weight_even = 0.5 + 0.5 * t
        weight_odd = 0.5 - 0.5 * t
        even, odd = so[0, :, c], so[1, :, c]
        pooled_ref[0, :, c] = (weight_even * even + weight_odd * odd).astype(BF16)
        clipped = limit * jnp.tanh(og_ref[0, 0, :, c].astype(F32) * inverse_limit)
        lg_ref[0, :, c] = (weight_even * weight_odd * (even - odd) * clipped).astype(BF16)
        sg_ref[0, 0, :, c] = weight_even * clipped
        sg_ref[1, 0, :, c] = weight_odd * clipped

    @pl.loop(0, tiles)
    def _(j):
        c = columns(j)
        g = lax.dot_general(lg_ref[0], wp_ref[c, :], NT, preferred_element_type=F32)
        even = sg_ref[0, 0, :, c] + g
        odd = sg_ref[1, 0, :, c] - g
        sg_ref[0, 0, :, c] = even
        sg_ref[1, 0, :, c] = odd
        low_even, low_odd = even.astype(BF16), odd.astype(BF16)
        branch_ref[0, pl.ds(0, pairs), c] = low_even
        branch_ref[0, pl.ds(pairs, pairs), c] = low_odd
        sum_ref[0, 2:3, c] = jnp.sum(low_even.astype(F32) + low_odd.astype(F32), axis=0, keepdims=True)

    @pl.loop(0, tiles)
    def _(j):
        c = columns(j)
        hg = lax.dot_general(branch_ref[0], w2_ref[c, :], NT, preferred_element_type=F32)
        plain, cross = 0.0, 0.0
        for e in range(2):
            f = load_first(j, e)
            normed = (f - vec_ref[0, 0:1, c]) * vec_ref[0, 1:2, c]
            act = normed * vec_ref[0, 2:3, c] + vec_ref[0, 3:4, c]
            grad = hg[e * pairs : (e + 1) * pairs] * gelu_slope(act)
            a2g_ref[e, 0, :, c] = grad
            plain += jnp.sum(grad, axis=0, keepdims=True)
            cross += jnp.sum(grad * normed, axis=0, keepdims=True)
        sum_ref[0, 0:1, c] = plain
        sum_ref[0, 1:2, c] = cross


def middle(first_own, first_other, vecs, w2, wp, out_grad, limits):
    _, micro_count, pairs, half = first_own.shape
    wide = 2 * half
    rows = 2 * pairs
    return pl.pallas_call(
        middle_kernel,
        out_shape=(
            jax.ShapeDtypeStruct((micro_count, pairs, wide), BF16),
            jax.ShapeDtypeStruct((micro_count, rows, wide), BF16),
            jax.ShapeDtypeStruct((micro_count, rows, wide), BF16),
            jax.ShapeDtypeStruct((micro_count, pairs, wide), BF16),
            jax.ShapeDtypeStruct((micro_count, pairs, wide), BF16),
            jax.ShapeDtypeStruct((2, micro_count, pairs, wide), F32),
            jax.ShapeDtypeStruct((2, micro_count, pairs, wide), F32),
            jax.ShapeDtypeStruct((micro_count, 8, wide), F32),
        ),
        grid=(micro_count,),
        in_specs=[
            pl.BlockSpec((2, 1, pairs, half), lambda m: (0, m, 0, 0)),
            pl.BlockSpec((2, 1, pairs, half), lambda m: (0, m, 0, 0)),
            pl.BlockSpec((1, 8, wide), lambda m: (m, 0, 0)),
            pl.BlockSpec((wide, wide), lambda m: (0, 0), pipeline_mode=pl.Buffered(1)),
            pl.BlockSpec((wide, wide), lambda m: (0, 0), pipeline_mode=pl.Buffered(1)),
            pl.BlockSpec((1, 1, pairs, wide), lambda m: (m, 0, 0, 0)),
            pl.BlockSpec((1, 8, 128), lambda m: (m, 0, 0)),
        ],
        out_specs=(
            pl.BlockSpec((1, pairs, wide), lambda m: (m, 0, 0)),
            pl.BlockSpec((1, rows, wide), lambda m: (m, 0, 0)),
            pl.BlockSpec((1, rows, wide), lambda m: (m, 0, 0)),
            pl.BlockSpec((1, pairs, wide), lambda m: (m, 0, 0)),
            pl.BlockSpec((1, pairs, wide), lambda m: (m, 0, 0)),
            pl.BlockSpec((2, 1, pairs, wide), lambda m: (0, m, 0, 0)),
            pl.BlockSpec((2, 1, pairs, wide), lambda m: (0, m, 0, 0)),
            pl.BlockSpec((1, 8, wide), lambda m: (m, 0, 0)),
        ),
        scratch_shapes=[pltpu.VMEM((2, pairs, wide), F32)],
        compiler_params=params(),
        name="middle",
    )(first_own, first_other, vecs, w2, wp, out_grad, limits)


def back_kernel(g_ref, wo_ref, wx_ref, x_ref, vec_ref, o_ref, s_ref):
    micro_count, pairs = o_ref.shape[1:3]
    half = wo_ref.shape[2]
    sums = [[0.0, 0.0] for _ in range(micro_count)]
    for e in range(2):
        acc = 0.0
        for k in range(KW):
            d = e - k + KW - 1
            acc += lax.dot_general(g_ref[d, :, :half], wo_ref[k], NT, preferred_element_type=F32)
            acc += lax.dot_general(g_ref[d, :, half:], wx_ref[k], NT, preferred_element_type=F32)
        for m in range(micro_count):
            x = x_ref[e, m].astype(F32)
            normed = (x - vec_ref[m, 0:1, :]) * vec_ref[m, 3:4, :]
            act = (x - vec_ref[m, 0:1, :]) * vec_ref[m, 1:2, :] + vec_ref[m, 2:3, :]
            grad = acc[m * pairs : (m + 1) * pairs] * gelu_slope(act)
            o_ref[e, m] = grad
            sums[m][0] += jnp.sum(grad, axis=0, keepdims=True)
            sums[m][1] += jnp.sum(grad * normed, axis=0, keepdims=True)
    for m in range(micro_count):
        for i in range(2):
            s_ref[2 * m + i : 2 * m + i + 1, :] = sums[m][i]


def conv_back(pieces, own, other, x, vecs, tile=256):
    _, micro_count, pairs, out = pieces.shape
    wide = own.shape[0] // KW
    half = own.shape[1]
    rows = micro_count * pairs
    return pl.pallas_call(
        back_kernel,
        out_shape=(
            jax.ShapeDtypeStruct((2, micro_count, pairs, wide), F32),
            jax.ShapeDtypeStruct((8, wide), F32),
        ),
        grid=(wide // tile,),
        in_specs=[
            pl.BlockSpec((PIECES, rows, out), lambda j: (0, 0, 0)),
            pl.BlockSpec((KW, tile, half), lambda j: (0, j, 0)),
            pl.BlockSpec((KW, tile, half), lambda j: (0, j, 0)),
            pl.BlockSpec((2, micro_count, pairs, tile), lambda j: (0, 0, 0, j)),
            pl.BlockSpec((micro_count, 8, tile), lambda j: (0, 0, j)),
        ],
        out_specs=(
            pl.BlockSpec((2, micro_count, pairs, tile), lambda j: (0, 0, 0, j)),
            pl.BlockSpec((8, tile), lambda j: (0, j)),
        ),
        compiler_params=params(),
        name="conv_back",
    )(
        pieces.reshape(PIECES, rows, out),
        own.reshape(KW, wide, half),
        other.reshape(KW, wide, half),
        x,
        vecs,
    )


def weight_kernel(he_ref, ho_ref, f_ref, o_ref):
    acc = 0.0
    for s in range(f_ref.shape[0]):
        acc += lax.dot_general(he_ref[s, 0], f_ref[s, 0], TN, preferred_element_type=F32)
        acc += lax.dot_general(ho_ref[s, 0], f_ref[s, 1], TN, preferred_element_type=F32)
    o_ref[...] = acc.astype(BF16)


def conv_weight_grad(pieces, low, tile=256):
    sides, _, micro_count, pairs, wide = pieces.shape
    out = low.shape[-1]
    rows = micro_count * pairs
    pieces = pieces.reshape(sides, PIECES, rows, wide)
    low = low.reshape(sides, 2, rows, out)
    per = wide // tile
    return pl.pallas_call(
        weight_kernel,
        out_shape=jax.ShapeDtypeStruct((KW * wide, out), BF16),
        grid=(KW, per),
        in_specs=[
            pl.BlockSpec((sides, 1, rows, tile), lambda k, j: (0, k, 0, j)),
            pl.BlockSpec((sides, 1, rows, tile), lambda k, j: (0, k + 1, 0, j)),
            pl.BlockSpec((sides, 2, rows, out), lambda k, j: (0, 0, 0, 0)),
        ],
        out_specs=pl.BlockSpec((tile, out), lambda k, j: (k * per + j, 0)),
        compiler_params=params(),
        name="conv_weight_grad",
    )(pieces, pieces, low)


def local(
    section_input,
    norm1_gain,
    norm1_bias,
    conv1_weight,
    conv1_bias,
    norm2_gain,
    norm2_bias,
    conv2_weight,
    conv2_bias,
    pool_weight,
    out_grad,
    clip_table,
    clip_index,
):
    micro_count, seq_count, local_rows, local_in = section_input.shape
    batch_count, pos_count, ch_count = (lax.axis_size(a) for a in ("batch", "pos", "ch"))
    batch, pos, ch = (lax.axis_index(a) for a in ("batch", "pos", "ch"))
    total_rows = seq_count * local_rows * batch_count * pos_count
    wide_in = 2 * local_in
    local_out = conv1_weight.shape[1]
    wide_out = 2 * local_out
    half = local_rows // 2
    pairs = half // 2
    plane = batch_count * pos_count
    spot = batch * pos_count + pos
    swap = [(0, 1), (1, 0)]
    is_low = ch == 0

    def other_ch(v):
        return lax.ppermute(v, "ch", swap)

    def natural(own, other, axis):
        return jnp.where(
            is_low,
            jnp.concatenate([own, other], axis=axis),
            jnp.concatenate([other, own], axis=axis),
        )

    x = section_input.reshape(micro_count, local_rows, local_in)

    def fetch(w):
        rows = w.shape[0] // plane
        piece = lax.dynamic_slice_in_dim(w, spot * rows, rows, axis=0)
        return lax.all_gather(other_ch(piece), ("batch", "pos"), axis=0, tiled=True)

    w1_other = fetch(conv1_weight)
    w2_other = fetch(conv2_weight)
    wp_other = fetch(pool_weight)

    up = [(i, i + 1) for i in range(pos_count - 1)]
    down = [(j, i) for i, j in up]
    before = lax.ppermute(x[:, -RIM:], "pos", up)
    after = lax.ppermute(x[:, :RIM], "pos", down)
    pad = jnp.zeros((micro_count, 16 - 2 * RIM, local_in), BF16)
    x_ext = jnp.concatenate([before, x, after, pad], axis=1)
    x_full = natural(x_ext, other_ch(x_ext), 2)

    x32 = x.astype(F32)
    lead = spot == 0
    stats = jnp.concatenate(
        [
            jnp.sum(x32, axis=1),
            jnp.sum(x32 * x32, axis=1),
            jnp.where(lead, jnp.stack([norm1_gain, norm1_bias]), 0.0),
        ]
    )
    small = jnp.stack([conv1_bias, norm2_gain, norm2_bias, conv2_bias])
    small = jnp.where(lead, small, 0.0)
    stats = natural(stats, jnp.zeros_like(stats), 1)
    small = natural(small, jnp.zeros_like(small), 1)
    stats = jnp.concatenate([stats, jnp.zeros((stats.shape[0], wide_out - wide_in), F32)], axis=1)
    summed = reduce_all(jnp.concatenate([stats, small]), 1)
    moments = summed[: 2 * micro_count, :wide_in] / total_rows
    gain1, bias1 = summed[2 * micro_count, :wide_in], summed[2 * micro_count + 1, :wide_in]
    small = summed[2 * micro_count + 2 :]
    center1 = moments[:micro_count]
    inverse1 = lax.rsqrt(moments[micro_count:] - center1 * center1 + EPS)

    def own_first(v):
        return jnp.where(
            is_low, v, jnp.concatenate([v[..., local_out:], v[..., :local_out]], axis=-1)
        )

    small = own_first(small)
    vec1 = jnp.stack(
        [center1, inverse1 * gain1, jnp.broadcast_to(bias1, center1.shape), inverse1]
        + [jnp.zeros_like(center1)] * 4,
        axis=1,
    )
    who = jnp.stack([ch, pos * local_rows, pos_count * local_rows]).astype(jnp.int32)
    pieces, x_split = make_hidden(who, x_full, vec1, half)

    first_own, stat_own = conv_forward(pieces[0], conv1_weight, small[0, :local_out])
    first_other, stat_other = conv_forward(pieces[0], w1_other, small[0, local_out:])
    stats2 = jnp.concatenate([stat_own[: 2 * micro_count], stat_other[: 2 * micro_count]], axis=1)

    def to_natural(v):
        return own_first(v)

    summed2 = own_first(reduce_all(to_natural(stats2), 2)) / total_rows
    center2 = summed2[0::2]
    inverse2 = lax.rsqrt(summed2[1::2] - center2 * center2 + EPS)
    spread = lambda v: jnp.broadcast_to(v, center2.shape)
    vec2 = jnp.stack(
        [center2, inverse2, spread(small[1]), spread(small[2]), spread(small[3])]
        + [jnp.zeros_like(center2)] * 3,
        axis=1,
    )

    def own_rows(w):
        return jnp.where(is_low, w, jnp.concatenate([w[local_out:], w[:local_out]], axis=0))

    w2 = jnp.concatenate([own_rows(conv2_weight), own_rows(w2_other)], axis=1)
    wp = jnp.concatenate([own_rows(pool_weight), own_rows(wp_other)], axis=1)

    bins = local_rows // 2
    mine = bins // 2
    og = out_grad.reshape(micro_count, bins, local_out)
    og_own = lax.dynamic_slice_in_dim(og, ch * mine, mine, axis=1)
    og_away = lax.dynamic_slice_in_dim(og, (1 - ch) * mine, mine, axis=1)
    og_full = jnp.concatenate([og_own, other_ch(og_away)], axis=2)
    table_pos = jnp.arange(clip_table.shape[0], dtype=jnp.int32)
    limit = jnp.sum(jnp.where(table_pos[None] == clip_index[:, None], clip_table[None], 0.0), axis=1)
    limits = jnp.broadcast_to(limit[:, None, None], (micro_count, 8, 128))

    pooled, hid2, branch, diff, lg, a2g, sg, sums3 = middle(
        first_own, first_other, vec2, w2, wp, og_full.reshape(micro_count, 1, mine, wide_out), limits
    )

    pooled_away = other_ch(pooled[:, :, local_out:])
    section_output = natural(pooled[:, :, :local_out], pooled_away, 1)
    section_output = section_output.reshape(micro_count, seq_count, bins, local_out)

    sums3 = sums3[:, :3].reshape(3 * micro_count, wide_out)
    sums3 = own_first(reduce_all(to_natural(sums3), 3)).reshape(micro_count, 3, wide_out)
    gain2 = small[1]
    mean_grad = (sums3[:, 0] / total_rows)[None, :, None]
    mean_cross = (sums3[:, 1] / total_rows)[None, :, None]
    normed = jnp.concatenate([first_own, first_other], axis=-1) - center2[None, :, None]
    normed = normed * inverse2[None, :, None]
    first_low = sg + (inverse2 * gain2)[None, :, None] * (a2g - mean_grad - normed * mean_cross)
    first_low = first_low.astype(BF16)
    low_sum = jnp.sum(first_low.astype(F32), axis=2)
    low_sum = low_sum[0] + low_sum[1]

    def turned(v):
        return jnp.where(is_low, v, jnp.concatenate([v[..., local_out:], v[..., :local_out]], axis=-1))

    line = pos_count * ch_count
    up = [(i, i + 1) for i in range(line - 1)]
    down = [(j, i) for i, j in up]
    last = lax.ppermute(turned(first_low[:, :, -1:]), ("pos", "ch"), up)
    head = lax.ppermute(turned(first_low[:, :, :1]), ("pos", "ch"), down)
    longer = jnp.concatenate([turned(last), first_low, turned(head)], axis=2)
    grad_pieces = jnp.stack(
        [longer[d % 2, :, d // 2 : d // 2 + pairs] for d in range(PIECES)]
    )
    a1g, sums4 = conv_back(grad_pieces, conv1_weight, w1_other, x_split[0], vec1)

    low_away = other_ch(first_low[..., local_out:])
    low_both = jnp.stack([first_low[..., :local_out], low_away])
    dw1 = conv_weight_grad(pieces, low_both)

    def split_grad(left, right):
        left = own_first(left)
        grad = jnp.einsum("mrc,mro->co", left, right, preferred_element_type=F32)
        away = other_ch(grad[:, local_out:].astype(BF16))
        return (grad[:, :local_out] + away.astype(F32)).astype(BF16)

    dw2 = split_grad(hid2, branch)
    dwp = split_grad(diff, lg)

    def scatter(v):
        return lax.psum_scatter(v, ("batch", "pos"), scatter_dimension=0, tiled=True).astype(F32)

    part = jnp.concatenate(
        [sums4[: 2 * micro_count], jnp.zeros((2 * micro_count, wide_out - wide_in), F32)], axis=1
    )
    part = jnp.concatenate([part, to_natural(low_sum)])
    part = reduce_all(part, 4)
    one = part[: 2 * micro_count, :wide_in]
    grad_sum, cross_sum = one[0::2], one[1::2]
    normed1 = (x_split[0].astype(F32) - center1[None, :, None]) * inverse1[None, :, None]
    dx = (inverse1 * gain1)[None, :, None] * (
        a1g - (grad_sum / total_rows)[None, :, None] - normed1 * (cross_sum / total_rows)[None, :, None]
    )
    dx = jnp.stack([dx[0], dx[1]], axis=2).reshape(micro_count, half, wide_in).astype(BF16)
    dx_own = lax.dynamic_slice_in_dim(dx, ch * local_in, local_in, axis=2)
    dx_away = other_ch(lax.dynamic_slice_in_dim(dx, (1 - ch) * local_in, local_in, axis=2))
    input_grad = natural(dx_own, dx_away, 1).reshape(section_input.shape)

    def mine_of(v, width):
        return lax.dynamic_slice_in_dim(v, ch * width, width, axis=0)

    return (
        section_output,
        input_grad,
        mine_of(jnp.sum(cross_sum, axis=0), local_in),
        mine_of(jnp.sum(grad_sum, axis=0), local_in),
        scatter(dw1),
        mine_of(jnp.sum(part[2 * micro_count :], axis=0), local_out),
        jnp.sum(sums3[:, 1], axis=0)[:local_out],
        jnp.sum(sums3[:, 0], axis=0)[:local_out],
        scatter(dw2),
        jnp.sum(sums3[:, 2], axis=0)[:local_out],
        scatter(dwp),
    )


def solution(mesh):
    placed = (
        P(None, "batch", "pos", "ch"),
        P("ch"),
        P("ch"),
        P(None, "ch"),
        P("ch"),
        P("ch"),
        P("ch"),
        P(None, "ch"),
        P("ch"),
        P(None, "ch"),
        P(None, "batch", "pos", "ch"),
        P(),
        P(),
    )
    return jax.shard_map(
        local,
        mesh=mesh,
        in_specs=placed,
        out_specs=(
            P(None, "batch", "pos", "ch"),
            P(None, "batch", "pos", "ch"),
            P("ch"),
            P("ch"),
            P(("batch", "pos"), "ch"),
            P("ch"),
            P("ch"),
            P("ch"),
            P(("batch", "pos"), "ch"),
            P("ch"),
            P(("batch", "pos"), "ch"),
        ),
        check_vma=False,
    )
```

```python
import functools

import jax
import jax.numpy as jnp
from jax import lax
from jax.experimental import pallas as pl
from jax.experimental.pallas import tpu as pltpu
from jax.sharding import PartitionSpec as P

KW = 5
RIM = KW // 2
PIECES = KW + 1
EPS = 1e-05
MESH = pl.DeviceIdType.MESH
C0 = 0.7978845608028654
C1 = 0.044715
F32 = jnp.float32
BF16 = jnp.bfloat16
VMEM_LIMIT = 60 * 1024 * 1024

NT = (((1,), (1,)), ((), ()))
TN = (((0,), (0,)), ((), ()))


def params(**kw):
    return pltpu.CompilerParams(vmem_limit_bytes=VMEM_LIMIT, **kw)


def gelu(u):
    return 0.5 * u * (1.0 + jnp.tanh(C0 * (u + C1 * u * u * u)))


def gelu_slope(u):
    square = u * u
    t = jnp.tanh(C0 * (u + C1 * square * u))
    return 0.5 * (1.0 + t) + 0.5 * u * (1.0 - t * t) * (C0 + (3.0 * C0 * C1) * square)


class Reduce:
    def __init__(self, value, core_in, near, far, result, sems):
        self.value, self.core_in, self.near, self.far, self.result = value, core_in, near, far, result
        self.send, self.recv = sems
        self.batch, self.pos, self.ch = (lax.axis_index(a) for a in ("batch", "pos", "ch"))
        self.core = lax.rem(self.pos, 2)
        self.z = self.pos // 2
        self.far_count = lax.axis_size("pos") // 2
        half = value.shape[1] // 2
        self.mine = pl.ds(pl.multiple_of(self.core * half, half), half)
        self.away = pl.ds(pl.multiple_of((1 - self.core) * half, half), half)
        self.me = self.batch * 2 + self.ch
        self.core_peer = (self.batch, self.z * 2 + 1 - self.core, self.ch)
        self.near_peers = []
        for step in range(1, 4):
            other = lax.rem(self.me + step, 4)
            self.near_peers.append((other // 2, self.pos, lax.rem(other, 2)))
        self.far_peers = []
        for step in range(1, self.far_count):
            other = lax.rem(self.z + step, self.far_count)
            self.far_peers.append((self.batch, other * 2 + self.core, self.ch))

    @staticmethod
    def scratch(width):
        far = lax.axis_size("pos") // 2
        count = 2 + 3 + far - 1
        return [
            pltpu.VMEM((8, width), F32),
            pltpu.VMEM((8, width // 2), F32),
            pltpu.VMEM((4, 8, width // 2), F32),
            pltpu.VMEM((far, 8, width // 2), F32),
            pltpu.VMEM((8, width), F32),
            pltpu.SemaphoreType.DMA((count,)),
            pltpu.SemaphoreType.DMA((count,)),
        ]

    def peers(self):
        return [self.core_peer] + self.near_peers + self.far_peers

    def copy(self, i, src, dst, peer):
        return pltpu.make_async_remote_copy(
            src, dst, self.send.at[i], self.recv.at[i], device_id=peer, device_id_type=MESH
        )

    def copies(self, stage):
        if stage == 0:
            return [self.copy(0, self.value.at[:, self.away], self.core_in, self.core_peer)]
        if stage == 1:
            slot = self.near.at[self.me]
            return [self.copy(1 + i, slot, slot, p) for i, p in enumerate(self.near_peers)]
        if stage == 2:
            slot = self.far.at[self.z]
            return [self.copy(4 + i, slot, slot, p) for i, p in enumerate(self.far_peers)]
        part = self.result.at[:, self.mine]
        return [self.copy(3 + self.far_count, part, part, self.core_peer)]

    def wait(self, stage):
        for copy in self.copies(stage):
            copy.wait()

    def start(self, stage):
        if stage == 1:
            self.wait(0)
            self.near[pl.ds(self.me, 1)] = (self.value[:, self.mine] + self.core_in[...])[None]
        if stage == 2:
            self.wait(1)
            total = (self.near[0] + self.near[1]) + (self.near[2] + self.near[3])
            self.far[pl.ds(self.z, 1)] = total[None]
        if stage == 3:
            self.wait(2)
            total = self.far[0]
            for i in range(1, self.far_count):
                total = total + self.far[i]
            self.result[:, self.mine] = total
        for copy in self.copies(stage):
            copy.start()


def meet(peers):
    barrier = pltpu.get_barrier_semaphore()
    for peer in peers:
        pl.semaphore_signal(barrier, inc=1, device_id=peer, device_id_type=MESH)
    pl.semaphore_wait(barrier, len(peers))


def reduce_kernel(v_ref, o_ref, *scratch):
    value, core_in, near, far, result, send, recv = scratch
    reduce = Reduce(value, core_in, near, far, result, (send, recv))
    value[...] = v_ref[...]
    meet(reduce.peers())
    for stage in range(4):
        reduce.start(stage)
    reduce.wait(3)
    o_ref[...] = result[...]


def reduce_all(values, collective_id):
    rows, width = values.shape
    total = pl.pallas_call(
        reduce_kernel,
        out_shape=jax.ShapeDtypeStruct((8, width), F32),
        in_specs=[pl.BlockSpec(memory_space=pltpu.VMEM)],
        out_specs=pl.BlockSpec(memory_space=pltpu.VMEM),
        scratch_shapes=Reduce.scratch(width),
        compiler_params=params(collective_id=collective_id, has_side_effects=True),
        name="reduce",
    )(jnp.pad(values, ((0, 8 - rows), (0, 0))))
    return total[:rows]


def hidden_kernel(who, x_ref, vec_ref, h_ref, x_out, scr, raw):
    micro, order = pl.program_id(0), pl.program_id(1)
    half = h_ref.shape[3] * 2
    lanes, ext = scr.shape[:2]
    side = jnp.bitwise_xor(who[0], order)
    begin = pl.multiple_of(side * half, 16)
    first = who[1] + side * half - RIM
    total = who[2]
    center = vec_ref[0, 0:1, :]
    scale = vec_ref[0, 1:2, :]
    bias = vec_ref[0, 2:3, :]

    @pl.loop(0, ext // 16)
    def _(i):
        at = pl.multiple_of(i * 16, 16)
        x = x_ref[0, pl.ds(begin + at, 16), :].astype(F32)
        act = (x - center) * scale + bias
        row = first + at + lax.broadcasted_iota(jnp.int32, x.shape, 0)
        inside = jnp.logical_and(row >= 0, row < total)
        hidden = jnp.where(inside, gelu(act), 0.0)
        for b in range(lanes):
            scr[b, pl.ds(at, 16), :] = hidden[:, b * 128 : (b + 1) * 128]
            raw[b, pl.ds(at, 16), :] = x[:, b * 128 : (b + 1) * 128]

    pairs = half // 2

    @pl.loop(0, pairs // 16)
    def _(i):
        at = pl.multiple_of(i * 16, 16)
        for b in range(lanes):
            lane = slice(b * 128, (b + 1) * 128)
            for d in range(PIECES):
                h_ref[0, d, 0, pl.ds(at, 16), lane] = scr[b, pl.ds(d + 2 * at, 16, stride=2), :].astype(BF16)
            for e in range(2):
                x_out[0, e, 0, pl.ds(at, 16), lane] = raw[
                    b, pl.ds(RIM + e + 2 * at, 16, stride=2), :
                ].astype(BF16)


def make_hidden(who, x_ext, vecs, half):
    micro_count, rows, wide = x_ext.shape
    ext = half + 16
    pairs = half // 2
    return pl.pallas_call(
        hidden_kernel,
        out_shape=(
            jax.ShapeDtypeStruct((2, PIECES, micro_count, pairs, wide), BF16),
            jax.ShapeDtypeStruct((2, 2, micro_count, pairs, wide), BF16),
        ),
        grid_spec=pltpu.PrefetchScalarGridSpec(
            num_scalar_prefetch=1,
            grid=(micro_count, 2),
            in_specs=[
                pl.BlockSpec((1, rows, wide), lambda m, o, w: (m, 0, 0)),
                pl.BlockSpec((1, 8, wide), lambda m, o, w: (m, 0, 0)),
            ],
            out_specs=(
                pl.BlockSpec((1, PIECES, 1, pairs, wide), lambda m, o, w: (o, 0, m, 0, 0)),
                pl.BlockSpec((1, 2, 1, pairs, wide), lambda m, o, w: (o, 0, m, 0, 0)),
            ),
            scratch_shapes=[pltpu.VMEM((wide // 128, ext, 128), F32)] * 2,
        ),
        compiler_params=params(),
        name="hidden",
    )(who, x_ext, vecs)


def conv_kernel(h_ref, w_ref, b_ref, o_ref, s_ref):
    micro_count, pairs = o_ref.shape[1:3]
    rows = micro_count * pairs
    wide = h_ref.shape[2]
    sums = [[0.0, 0.0] for _ in range(micro_count)]
    for e in range(2):
        acc = jnp.dot(h_ref[e], w_ref[0:wide, :], preferred_element_type=F32)
        for k in range(1, KW):
            acc += jnp.dot(
                h_ref[k + e], w_ref[k * wide : (k + 1) * wide, :], preferred_element_type=F32
            )
        acc += b_ref[...]
        for m in range(micro_count):
            part = acc[m * pairs : (m + 1) * pairs]
            o_ref[e, m] = part
            sums[m][0] += jnp.sum(part, axis=0, keepdims=True)
            sums[m][1] += jnp.sum(part * part, axis=0, keepdims=True)
    for m in range(micro_count):
        for i in range(2):
            s_ref[2 * m + i : 2 * m + i + 1, :] = sums[m][i]


def conv_forward(pieces, weight, bias, tile=256):
    _, micro_count, pairs, wide = pieces.shape
    out = weight.shape[1]
    rows = micro_count * pairs
    return pl.pallas_call(
        conv_kernel,
        out_shape=(
            jax.ShapeDtypeStruct((2, micro_count, pairs, out), F32),
            jax.ShapeDtypeStruct((8, out), F32),
        ),
        grid=(out // tile,),
        in_specs=[
            pl.BlockSpec((PIECES, rows, wide), lambda j: (0, 0, 0)),
            pl.BlockSpec((KW * wide, tile), lambda j: (0, j)),
            pl.BlockSpec((1, tile), lambda j: (0, j)),
        ],
        out_specs=(
            pl.BlockSpec((2, micro_count, pairs, tile), lambda j: (0, 0, 0, j)),
            pl.BlockSpec((8, tile), lambda j: (0, j)),
        ),
        compiler_params=params(),
        name="conv_forward",
    )(pieces.reshape(PIECES, rows, wide), weight, bias.reshape(1, out))


def middle_kernel(
    fo_ref,
    fx_ref,
    vec_ref,
    w2_ref,
    wp_ref,
    og_ref,
    lim_ref,
    pooled_ref,
    hid_ref,
    branch_ref,
    diff_ref,
    lg_ref,
    a2g_ref,
    sg_ref,
    sum_ref,
    so,
):
    pairs = og_ref.shape[2]
    rows = 2 * pairs
    wide = w2_ref.shape[0]
    half = wide // 2
    tile = 256
    tiles = wide // tile

    def columns(j):
        return pl.ds(pl.multiple_of(j * tile, tile), tile)

    def load_first(j, e):
        own = j < tiles // 2
        at = pl.ds(pl.multiple_of(lax.rem(j, tiles // 2) * tile, tile), tile)
        return jnp.where(own, fo_ref[e, 0, :, at], fx_ref[e, 0, :, at])

    @pl.loop(0, tiles)
    def _(j):
        c = columns(j)
        for e in range(2):
            f = load_first(j, e)
            act = (f - vec_ref[0, 0:1, c]) * vec_ref[0, 1:2, c] * vec_ref[0, 2:3, c] + vec_ref[0, 3:4, c]
            hid_ref[0, pl.ds(e * pairs, pairs), c] = gelu(act).astype(BF16)

    @pl.loop(0, tiles)
    def _(j):
        c = columns(j)
        branch = jnp.dot(hid_ref[0], w2_ref[:, c], preferred_element_type=F32)
        even = branch[:pairs] + (load_first(j, 0) + vec_ref[0, 4:5, c])
        odd = branch[pairs:] + (load_first(j, 1) + vec_ref[0, 4:5, c])
        so[0, :, c] = even
        so[1, :, c] = odd
        diff_ref[0, :, c] = (even - odd).astype(BF16)

    limit = lim_ref[0, 0:1, 0:1]
    inverse_limit = 1.0 / limit

    @pl.loop(0, tiles)
    def _(j):
        c = columns(j)
        d = jnp.dot(diff_ref[0], wp_ref[:, c], preferred_element_type=F32)
        t = jnp.tanh(0.5 * d)
        weight_even = 0.5 + 0.5 * t
        weight_odd = 0.5 - 0.5 * t
        even, odd = so[0, :, c], so[1, :, c]
        pooled_ref[0, :, c] = (weight_even * even + weight_odd * odd).astype(BF16)
        clipped = limit * jnp.tanh(og_ref[0, 0, :, c].astype(F32) * inverse_limit)
        lg_ref[0, :, c] = (weight_even * weight_odd * (even - odd) * clipped).astype(BF16)
        sg_ref[0, 0, :, c] = weight_even * clipped
        sg_ref[1, 0, :, c] = weight_odd * clipped

    @pl.loop(0, tiles)
    def _(j):
        c = columns(j)
        g = lax.dot_general(lg_ref[0], wp_ref[c, :], NT, preferred_element_type=F32)
        even = sg_ref[0, 0, :, c] + g
        odd = sg_ref[1, 0, :, c] - g
        sg_ref[0, 0, :, c] = even
        sg_ref[1, 0, :, c] = odd
        low_even, low_odd = even.astype(BF16), odd.astype(BF16)
        branch_ref[0, pl.ds(0, pairs), c] = low_even
        branch_ref[0, pl.ds(pairs, pairs), c] = low_odd
        sum_ref[0, 2:3, c] = jnp.sum(low_even.astype(F32) + low_odd.astype(F32), axis=0, keepdims=True)

    @pl.loop(0, tiles)
    def _(j):
        c = columns(j)
        hg = lax.dot_general(branch_ref[0], w2_ref[c, :], NT, preferred_element_type=F32)
        plain, cross = 0.0, 0.0
        for e in range(2):
            f = load_first(j, e)
            normed = (f - vec_ref[0, 0:1, c]) * vec_ref[0, 1:2, c]
            act = normed * vec_ref[0, 2:3, c] + vec_ref[0, 3:4, c]
            grad = hg[e * pairs : (e + 1) * pairs] * gelu_slope(act)
            a2g_ref[e, 0, :, c] = grad
            plain += jnp.sum(grad, axis=0, keepdims=True)
            cross += jnp.sum(grad * normed, axis=0, keepdims=True)
        sum_ref[0, 0:1, c] = plain
        sum_ref[0, 1:2, c] = cross


def middle(first_own, first_other, vecs, w2, wp, out_grad, limits):
    _, micro_count, pairs, half = first_own.shape
    wide = 2 * half
    rows = 2 * pairs
    return pl.pallas_call(
        middle_kernel,
        out_shape=(
            jax.ShapeDtypeStruct((micro_count, pairs, wide), BF16),
            jax.ShapeDtypeStruct((micro_count, rows, wide), BF16),
            jax.ShapeDtypeStruct((micro_count, rows, wide), BF16),
            jax.ShapeDtypeStruct((micro_count, pairs, wide), BF16),
            jax.ShapeDtypeStruct((micro_count, pairs, wide), BF16),
            jax.ShapeDtypeStruct((2, micro_count, pairs, wide), F32),
            jax.ShapeDtypeStruct((2, micro_count, pairs, wide), F32),
            jax.ShapeDtypeStruct((micro_count, 8, wide), F32),
        ),
        grid=(micro_count,),
        in_specs=[
            pl.BlockSpec((2, 1, pairs, half), lambda m: (0, m, 0, 0)),
            pl.BlockSpec((2, 1, pairs, half), lambda m: (0, m, 0, 0)),
            pl.BlockSpec((1, 8, wide), lambda m: (m, 0, 0)),
            pl.BlockSpec((wide, wide), lambda m: (0, 0), pipeline_mode=pl.Buffered(1)),
            pl.BlockSpec((wide, wide), lambda m: (0, 0), pipeline_mode=pl.Buffered(1)),
            pl.BlockSpec((1, 1, pairs, wide), lambda m: (m, 0, 0, 0)),
            pl.BlockSpec((1, 8, 128), lambda m: (m, 0, 0)),
        ],
        out_specs=(
            pl.BlockSpec((1, pairs, wide), lambda m: (m, 0, 0)),
            pl.BlockSpec((1, rows, wide), lambda m: (m, 0, 0)),
            pl.BlockSpec((1, rows, wide), lambda m: (m, 0, 0)),
            pl.BlockSpec((1, pairs, wide), lambda m: (m, 0, 0)),
            pl.BlockSpec((1, pairs, wide), lambda m: (m, 0, 0)),
            pl.BlockSpec((2, 1, pairs, wide), lambda m: (0, m, 0, 0)),
            pl.BlockSpec((2, 1, pairs, wide), lambda m: (0, m, 0, 0)),
            pl.BlockSpec((1, 8, wide), lambda m: (m, 0, 0)),
        ),
        scratch_shapes=[pltpu.VMEM((2, pairs, wide), F32)],
        compiler_params=params(),
        name="middle",
    )(first_own, first_other, vecs, w2, wp, out_grad, limits)


def tail_kernel(
    scatter,
    total_rows,
    low,
    hp,
    gp,
    wo,
    wx,
    xs_in,
    vec_ref,
    extra_ref,
    ig,
    dw_out,
    sum_out,
    g_buf,
    w_buf,
    a1g,
    xs,
    h_buf,
    f_buf,
    dw,
    core_in,
    x_in,
    z_in,
    dxs,
    weave,
    load_sem,
    w_sem,
    h_sem,
    low_send,
    low_recv,
    core_send,
    core_recv,
    x_send,
    x_recv,
    z_send,
    z_recv,
    ig_send,
    ig_recv,
    ig_sem,
    value,
    r_core,
    r_near,
    r_far,
    r_result,
    r_send,
    r_recv,
):
    reduce = Reduce(value, r_core, r_near, r_far, r_result, (r_send, r_recv))
    batch, pos, ch, core, z = reduce.batch, reduce.pos, reduce.ch, reduce.core, reduce.z
    far_count = reduce.far_count
    chunks, rows_all, chunk = dw.shape
    micro_count, half_rows, wide = dxs.shape
    pairs = half_rows // 2
    rows = micro_count * pairs
    out = gp.shape[2]
    local_out = out // 2
    local_in = wide // 2
    tile = w_buf.shape[2]
    cut = h_buf.shape[3]
    per_half = rows_all // 2 // cut
    y_peer = (batch, pos, 1 - ch)
    x_peer = (1 - batch, pos, ch)
    core_peer = reduce.core_peer

    def loads():
        copies = [
            pltpu.make_async_copy(gp, g_buf, load_sem.at[0]),
            pltpu.make_async_copy(xs_in, xs, load_sem.at[1]),
            pltpu.make_async_copy(low.at[:, :, 0:local_out], f_buf.at[0:2], load_sem.at[2]),
        ]
        return copies

    def w_copies(j):
        s = j % 2
        at = slice(j * tile, (j + 1) * tile)
        return [
            pltpu.make_async_copy(wo.at[:, at, :], w_buf.at[s, :, :, 0:local_out], w_sem.at[s, 0]),
            pltpu.make_async_copy(wx.at[:, at, :], w_buf.at[s, :, :, local_out:out], w_sem.at[s, 1]),
        ]

    def h_copies(side_half, t):
        number = side_half * per_half + t
        k = number // 2
        at = pl.ds(pl.multiple_of(lax.rem(number, 2) * cut, cut), cut)
        slot = lax.rem(t, 2)
        return [
            pltpu.make_async_copy(hp.at[s, k + e, :, at], h_buf.at[slot, 2 * s + e], h_sem.at[slot, 2 * s + e])
            for s in range(2)
            for e in range(2)
        ]

    def low_copy(c):
        return pltpu.make_async_remote_copy(
            low.at[:, :, local_out + c * chunk : local_out + (c + 1) * chunk],
            f_buf.at[2:4, :, c * chunk : (c + 1) * chunk],
            low_send.at[c],
            low_recv.at[c],
            device_id=y_peer,
            device_id_type=MESH,
        )

    for copy in loads():
        copy.start()
    for copy in w_copies(0):
        copy.start()
    meet(reduce.peers())
    low_copy(0).start()
    for copy in h_copies(1 - batch, 0):
        copy.start()
    for copy in loads()[:2]:
        copy.wait()
    value[...] = extra_ref[...]

    tiles = wide // tile

    def back(j):
        s = j % 2
        if j + 1 < tiles:
            for copy in w_copies(j + 1):
                copy.start()
        for copy in w_copies(j):
            copy.wait()
        at = slice(j * tile, (j + 1) * tile)
        sums = [[0.0, 0.0] for _ in range(micro_count)]
        for e in range(2):
            acc = 0.0
            for k in range(KW):
                acc += lax.dot_general(
                    g_buf[e - k + KW - 1], w_buf[s, k], NT, preferred_element_type=F32
                )
            for m in range(micro_count):
                x = xs[e, m * pairs : (m + 1) * pairs, at].astype(F32)
                moved = x - vec_ref[m, 0:1, at]
                normed = moved * vec_ref[m, 3:4, at]
                act = moved * vec_ref[m, 1:2, at] + vec_ref[m, 2:3, at]
                grad = acc[m * pairs : (m + 1) * pairs] * gelu_slope(act)
                a1g[e, m * pairs : (m + 1) * pairs, at] = grad
                sums[m][0] += jnp.sum(grad, axis=0, keepdims=True)
                sums[m][1] += jnp.sum(grad * normed, axis=0, keepdims=True)
        for m in range(micro_count):
            for i in range(2):
                value[2 * m + i : 2 * m + i + 1, at] = sums[m][i]

    block = rows_all // (2 * 2 * far_count)

    def block_rows(side_half, zz, cc):
        return pl.ds(pl.multiple_of(((side_half * far_count + zz) * 2 + cc) * block, 16), block)

    def core_copy(c, kind, side_half, zz):
        return pltpu.make_async_remote_copy(
            dw.at[c, block_rows(side_half, zz, 1 - core)],
            core_in.at[c, kind, zz],
            core_send.at[c, kind, zz],
            core_recv.at[c, kind, zz],
            device_id=core_peer,
            device_id_type=MESH,
        )

    def x_copy(c, zz):
        return pltpu.make_async_remote_copy(
            dw.at[c, block_rows(1 - batch, zz, core)],
            x_in.at[c, zz],
            x_send.at[c, zz],
            x_recv.at[c, zz],
            device_id=x_peer,
            device_id_type=MESH,
        )

    def z_copy(c, r, zz):
        return pltpu.make_async_remote_copy(
            dw.at[c, block_rows(batch, zz, core)],
            z_in.at[c, r],
            z_send.at[c, r],
            z_recv.at[c, r],
            device_id=(batch, zz * 2 + core, ch),
            device_id_type=MESH,
        )

    steps = list(range(far_count // 2, far_count)) + list(range(1, far_count // 2)) + [0]
    if far_count == 4:
        steps = [2, 1, 3, 0]

    def away(r):
        return lax.rem(z + steps[r], far_count)

    def weigh(c, kind, side_half, following):
        lanes = slice(c * chunk, (c + 1) * chunk)

        @pl.loop(0, per_half)
        def _(t):
            @pl.when(t + 1 < per_half)
            def _():
                for copy in h_copies(side_half, t + 1):
                    copy.start()

            for copy in h_copies(side_half, t):
                copy.wait()
            slot = lax.rem(t, 2)
            grad = lax.dot_general(
                h_buf[slot].reshape(4 * rows, cut),
                f_buf[:, :, lanes].reshape(4 * rows, chunk),
                TN,
                preferred_element_type=F32,
            )
            at = pl.multiple_of((side_half * per_half + t) * cut, 16)
            dw[c, pl.ds(at, cut), :] = grad.astype(BF16)

        if following is not None:
            for copy in h_copies(following, 0):
                copy.start()
        if scatter:
            for r in range(far_count):
                core_copy(c, kind, side_half, away(r)).start()

    def add_to(c, at, ref, *index):
        dw[c, at, :] = (dw[c, at, :].astype(F32) + ref[index].astype(F32)).astype(BF16)

    def send_x(c):
        if scatter:
            for r in range(far_count):
                zz = away(r)
                core_copy(c, 0, 1 - batch, zz).wait_recv()
                add_to(c, block_rows(1 - batch, zz, core), core_in, c, 0, zz)
                x_copy(c, zz).start()

    def send_z(c):
        if scatter:
            for r in range(far_count):
                zz = away(r)
                core_copy(c, 1, batch, zz).wait_recv()
                x_copy(c, zz).wait_recv()
                at = block_rows(batch, zz, core)
                total = dw[c, at, :].astype(F32) + core_in[c, 1, zz].astype(F32) + x_in[c, zz].astype(F32)
                lanes = slice(c * chunk, (c + 1) * chunk)
                if r < far_count - 1:
                    dw[c, at, :] = total.astype(BF16)
                    z_copy(c, r, zz).start()
                else:
                    dw_out[:, lanes] = total

    def finish(c):
        lanes = slice(c * chunk, (c + 1) * chunk)
        if scatter:
            for r in range(far_count - 1):
                z_copy(c, r, away(r)).wait_recv()
                dw_out[:, lanes] = dw_out[:, lanes] + z_in[c, r].astype(F32)
        else:
            copy = pltpu.make_async_copy(dw.at[c], dw_out.at[:, lanes], load_sem.at[3])
            copy.start()
            copy.wait()

    def ig_remote(m):
        at = pl.ds(pl.multiple_of(ch * half_rows, half_rows), half_rows)
        lanes = pl.ds(pl.multiple_of((1 - ch) * local_in, 128), local_in)
        return pltpu.make_async_remote_copy(
            dxs.at[m, :, lanes], ig.at[m, at], ig_send.at[m], ig_recv.at[m], device_id=y_peer, device_id_type=MESH
        )

    def ig_local(m):
        at = pl.ds(pl.multiple_of(ch * half_rows, half_rows), half_rows)
        lanes = pl.ds(pl.multiple_of(ch * local_in, 128), local_in)
        return pltpu.make_async_copy(dxs.at[m, :, lanes], ig.at[m, at], ig_sem.at[m])

    def input_grad(m):
        scale = 1.0 / total_rows

        @pl.loop(0, wide // 128)
        def _(b):
            at = pl.ds(pl.multiple_of(b * 128, 128), 128)
            plain = r_result[2 * m : 2 * m + 1, at] * scale
            cross = r_result[2 * m + 1 : 2 * m + 2, at] * scale
            inverse = vec_ref[m, 3:4, at]
            for e in range(2):
                x = xs[e, m * pairs : (m + 1) * pairs, at].astype(F32)
                normed = (x - vec_ref[m, 0:1, at]) * inverse
                grad = a1g[e, m * pairs : (m + 1) * pairs, at]
                weave[pl.ds(e, pairs, stride=2), :] = vec_ref[m, 1:2, at] * (grad - plain - normed * cross)
            dxs[m, :, at] = weave[...].astype(BF16)

        ig_local(m).start()
        ig_remote(m).start()

    for j in range(2):
        back(j)
    loads()[2].wait()
    low_copy(0).wait_recv()
    for c in range(1, chunks):
        low_copy(c).start()
    weigh(0, 0, 1 - batch, batch)
    send_x(0)
    for j in range(2, tiles):
        back(j)
    reduce.start(0)
    weigh(0, 1, batch, 1 - batch)
    reduce.start(1)
    low_copy(1).wait_recv()
    weigh(1, 0, 1 - batch, batch)
    send_x(1)
    reduce.start(2)
    send_z(0)
    weigh(1, 1, batch, 1 - batch)
    reduce.start(3)
    low_copy(2).wait_recv()
    weigh(2, 0, 1 - batch, batch)
    send_x(2)
    reduce.wait(3)
    sum_out[...] = r_result[...]
    for m in range(micro_count):
        input_grad(m)
    weigh(2, 1, batch, None)
    send_z(1)
    finish(0)
    send_z(2)
    finish(1)
    finish(2)
    for m in range(micro_count):
        ig_local(m).wait()
        ig_remote(m).wait()
    for c in range(chunks):
        low_copy(c).wait_send()
        if scatter:
            for r in range(far_count):
                zz = away(r)
                core_copy(c, 0, 1 - batch, zz).wait_send()
                core_copy(c, 1, batch, zz).wait_send()
                x_copy(c, zz).wait_send()
                if r < far_count - 1:
                    z_copy(c, r, zz).wait_send()


def tail(low, pieces, grad_pieces, own, other, x_split, vecs, extra, total_rows):
    sides, _, micro_count, pairs, wide = pieces.shape
    rows = micro_count * pairs
    out = grad_pieces.shape[-1]
    local_out = out // 2
    chunks = 3
    chunk = local_out // chunks
    far = lax.axis_size("pos") // 2
    rows_all = KW * wide
    block = rows_all // (4 * far)
    scatter = block % 16 == 0
    tile = 256
    land = block if scatter else 16
    any_space = pl.BlockSpec(memory_space=pl.ANY)
    in_vmem = pl.BlockSpec(memory_space=pltpu.VMEM)
    dma = pltpu.SemaphoreType.DMA
    return pl.pallas_call(
        functools.partial(tail_kernel, scatter, total_rows),
        out_shape=(
            jax.ShapeDtypeStruct((micro_count, 4 * pairs, wide // 2), BF16),
            jax.ShapeDtypeStruct((block, local_out) if scatter else (rows_all, local_out), F32 if scatter else BF16),
            jax.ShapeDtypeStruct((8, out), F32),
        ),
        in_specs=[any_space] * 6 + [in_vmem] * 2,
        out_specs=(any_space, in_vmem if scatter else any_space, in_vmem),
        scratch_shapes=[
            pltpu.VMEM((PIECES, rows, out), BF16),
            pltpu.VMEM((2, KW, tile, out), BF16),
            pltpu.VMEM((2, rows, wide), F32),
            pltpu.VMEM((2, rows, wide), BF16),
            pltpu.VMEM((2, 4, rows, wide // 2), BF16),
            pltpu.VMEM((4, rows, local_out), BF16),
            pltpu.VMEM((chunks, rows_all, chunk), BF16),
            pltpu.VMEM((chunks, 2, far, land, chunk), BF16),
            pltpu.VMEM((chunks, far, land, chunk), BF16),
            pltpu.VMEM((chunks, far - 1, land, chunk), BF16),
            pltpu.VMEM((micro_count, 2 * pairs, wide), BF16),
            pltpu.VMEM((2 * pairs, 128), F32),
            dma((4,)),
            dma((2, 2)),
            dma((2, 4)),
            dma((chunks,)),
            dma((chunks,)),
            dma((chunks, 2, far)),
            dma((chunks, 2, far)),
            dma((chunks, far)),
            dma((chunks, far)),
            dma((chunks, far - 1)),
            dma((chunks, far - 1)),
            dma((micro_count,)),
            dma((micro_count,)),
            dma((micro_count,)),
        ]
        + Reduce.scratch(out),
        compiler_params=params(collective_id=5, has_side_effects=True),
        name="tail",
    )(
        low.reshape(2, rows, out),
        pieces.reshape(sides, PIECES, rows, wide),
        grad_pieces.reshape(PIECES, rows, out),
        own.reshape(KW, wide, local_out),
        other.reshape(KW, wide, local_out),
        x_split.reshape(2, rows, wide),
        vecs,
        extra,
    )


def local(
    section_input,
    norm1_gain,
    norm1_bias,
    conv1_weight,
    conv1_bias,
    norm2_gain,
    norm2_bias,
    conv2_weight,
    conv2_bias,
    pool_weight,
    out_grad,
    clip_table,
    clip_index,
):
    micro_count, seq_count, local_rows, local_in = section_input.shape
    batch_count, pos_count, ch_count = (lax.axis_size(a) for a in ("batch", "pos", "ch"))
    batch, pos, ch = (lax.axis_index(a) for a in ("batch", "pos", "ch"))
    total_rows = seq_count * local_rows * batch_count * pos_count
    wide_in = 2 * local_in
    local_out = conv1_weight.shape[1]
    wide_out = 2 * local_out
    half = local_rows // 2
    pairs = half // 2
    plane = batch_count * pos_count
    spot = batch * pos_count + pos
    swap = [(0, 1), (1, 0)]
    is_low = ch == 0

    def other_ch(v):
        return lax.ppermute(v, "ch", swap)

    def natural(own, other, axis):
        return jnp.where(
            is_low,
            jnp.concatenate([own, other], axis=axis),
            jnp.concatenate([other, own], axis=axis),
        )

    x = section_input.reshape(micro_count, local_rows, local_in)

    def fetch(w):
        rows = w.shape[0] // plane
        piece = lax.dynamic_slice_in_dim(w, spot * rows, rows, axis=0)
        return lax.all_gather(other_ch(piece), ("batch", "pos"), axis=0, tiled=True)

    w1_other = fetch(conv1_weight)
    w2_other = fetch(conv2_weight)
    wp_other = fetch(pool_weight)

    up = [(i, i + 1) for i in range(pos_count - 1)]
    down = [(j, i) for i, j in up]
    before = lax.ppermute(x[:, -RIM:], "pos", up)
    after = lax.ppermute(x[:, :RIM], "pos", down)
    pad = jnp.zeros((micro_count, 16 - 2 * RIM, local_in), BF16)
    x_ext = jnp.concatenate([before, x, after, pad], axis=1)
    x_full = natural(x_ext, other_ch(x_ext), 2)

    x32 = x.astype(F32)
    stats = jnp.concatenate([jnp.sum(x32, axis=1), jnp.sum(x32 * x32, axis=1)])
    stats = natural(stats, jnp.zeros_like(stats), 1)
    moments = reduce_all(stats, 1) / total_rows
    small = jnp.stack([conv1_bias, norm2_gain, norm2_bias, conv2_bias])
    small = jnp.concatenate([small, jnp.pad(jnp.stack([norm1_gain, norm1_bias]), ((0, 0), (0, local_out - local_in)))])
    small_other = other_ch(small)
    gains1 = natural(small[4:, :local_in], small_other[4:, :local_in], 1)
    gain1, bias1 = gains1[0], gains1[1]
    small = jnp.concatenate([small[:4], small_other[:4]], axis=1)
    center1 = moments[:micro_count]
    inverse1 = lax.rsqrt(moments[micro_count:] - center1 * center1 + EPS)

    def own_first(v):
        return jnp.where(
            is_low, v, jnp.concatenate([v[..., local_out:], v[..., :local_out]], axis=-1)
        )

    vec1 = jnp.stack(
        [center1, inverse1 * gain1, jnp.broadcast_to(bias1, center1.shape), inverse1]
        + [jnp.zeros_like(center1)] * 4,
        axis=1,
    )
    who = jnp.stack([ch, pos * local_rows, pos_count * local_rows]).astype(jnp.int32)
    pieces, x_split = make_hidden(who, x_full, vec1, half)

    first_own, stat_own = conv_forward(pieces[0], conv1_weight, small[0, :local_out])
    first_other, stat_other = conv_forward(pieces[0], w1_other, small[0, local_out:])
    stats2 = jnp.concatenate([stat_own[: 2 * micro_count], stat_other[: 2 * micro_count]], axis=1)

    def to_natural(v):
        return own_first(v)

    summed2 = own_first(reduce_all(to_natural(stats2), 2)) / total_rows
    center2 = summed2[0::2]
    inverse2 = lax.rsqrt(summed2[1::2] - center2 * center2 + EPS)
    spread = lambda v: jnp.broadcast_to(v, center2.shape)
    vec2 = jnp.stack(
        [center2, inverse2, spread(small[1]), spread(small[2]), spread(small[3])]
        + [jnp.zeros_like(center2)] * 3,
        axis=1,
    )

    def own_rows(w):
        return jnp.where(is_low, w, jnp.concatenate([w[local_out:], w[:local_out]], axis=0))

    w2 = jnp.concatenate([own_rows(conv2_weight), own_rows(w2_other)], axis=1)
    wp = jnp.concatenate([own_rows(pool_weight), own_rows(wp_other)], axis=1)

    bins = local_rows // 2
    mine = bins // 2
    og = out_grad.reshape(micro_count, bins, local_out)
    og_own = lax.dynamic_slice_in_dim(og, ch * mine, mine, axis=1)
    og_away = lax.dynamic_slice_in_dim(og, (1 - ch) * mine, mine, axis=1)
    og_full = jnp.concatenate([og_own, other_ch(og_away)], axis=2)
    table_pos = jnp.arange(clip_table.shape[0], dtype=jnp.int32)
    limit = jnp.sum(jnp.where(table_pos[None] == clip_index[:, None], clip_table[None], 0.0), axis=1)
    limits = jnp.broadcast_to(limit[:, None, None], (micro_count, 8, 128))

    pooled, hid2, branch, diff, lg, a2g, sg, sums3 = middle(
        first_own, first_other, vec2, w2, wp, og_full.reshape(micro_count, 1, mine, wide_out), limits
    )

    pooled_away = other_ch(pooled[:, :, local_out:])
    section_output = natural(pooled[:, :, :local_out], pooled_away, 1)
    section_output = section_output.reshape(micro_count, seq_count, bins, local_out)

    sums3 = sums3[:, :3].reshape(3 * micro_count, wide_out)
    sums3 = own_first(reduce_all(to_natural(sums3), 3)).reshape(micro_count, 3, wide_out)
    gain2 = small[1]
    mean_grad = (sums3[:, 0] / total_rows)[None, :, None]
    mean_cross = (sums3[:, 1] / total_rows)[None, :, None]
    normed = jnp.concatenate([first_own, first_other], axis=-1) - center2[None, :, None]
    normed = normed * inverse2[None, :, None]
    first_low = sg + (inverse2 * gain2)[None, :, None] * (a2g - mean_grad - normed * mean_cross)
    first_low = first_low.astype(BF16)
    low_sum = jnp.sum(first_low.astype(F32), axis=2)
    low_sum = low_sum[0] + low_sum[1]

    def turned(v):
        return jnp.where(is_low, v, jnp.concatenate([v[..., local_out:], v[..., :local_out]], axis=-1))

    line = pos_count * ch_count
    up = [(i, i + 1) for i in range(line - 1)]
    down = [(j, i) for i, j in up]
    last = lax.ppermute(turned(first_low[:, :, -1:]), ("pos", "ch"), up)
    head = lax.ppermute(turned(first_low[:, :, :1]), ("pos", "ch"), down)
    longer = jnp.concatenate([turned(last), first_low, turned(head)], axis=2)
    grad_pieces = jnp.stack(
        [longer[d % 2, :, d // 2 : d // 2 + pairs] for d in range(PIECES)]
    )
    extra = jnp.pad(to_natural(low_sum), ((2 * micro_count, 8 - 3 * micro_count), (0, 0)))
    input_grad, dw1, part = tail(
        first_low, pieces, grad_pieces, conv1_weight, w1_other, x_split[0], vec1, extra, total_rows
    )
    input_grad = input_grad.reshape(section_input.shape)

    def split_grad(left, right):
        left = own_first(left)
        grad = jnp.einsum("mrc,mro->co", left, right, preferred_element_type=F32)
        away = other_ch(grad[:, local_out:].astype(BF16))
        return (grad[:, :local_out] + away.astype(F32)).astype(BF16)

    dw2 = split_grad(hid2, branch)
    dwp = split_grad(diff, lg)

    def scatter(v):
        return lax.psum_scatter(v, ("batch", "pos"), scatter_dimension=0, tiled=True).astype(F32)

    one = part[: 2 * micro_count, :wide_in]
    grad_sum, cross_sum = one[0::2], one[1::2]
    low_sum = part[2 * micro_count : 3 * micro_count]
    if dw1.shape[0] != KW * wide_in // plane:
        dw1 = scatter(dw1)

    def mine_of(v, width):
        return lax.dynamic_slice_in_dim(v, ch * width, width, axis=0)

    return (
        section_output,
        input_grad,
        mine_of(jnp.sum(cross_sum, axis=0), local_in),
        mine_of(jnp.sum(grad_sum, axis=0), local_in),
        dw1,
        mine_of(jnp.sum(low_sum, axis=0), local_out),
        jnp.sum(sums3[:, 1], axis=0)[:local_out],
        jnp.sum(sums3[:, 0], axis=0)[:local_out],
        scatter(dw2),
        jnp.sum(sums3[:, 2], axis=0)[:local_out],
        scatter(dwp),
    )


def solution(mesh):
    placed = (
        P(None, "batch", "pos", "ch"),
        P("ch"),
        P("ch"),
        P(None, "ch"),
        P("ch"),
        P("ch"),
        P("ch"),
        P(None, "ch"),
        P("ch"),
        P(None, "ch"),
        P(None, "batch", "pos", "ch"),
        P(),
        P(),
    )
    return jax.shard_map(
        local,
        mesh=mesh,
        in_specs=placed,
        out_specs=(
            P(None, "batch", "pos", "ch"),
            P(None, "batch", "pos", "ch"),
            P("ch"),
            P("ch"),
            P(("batch", "pos"), "ch"),
            P("ch"),
            P("ch"),
            P("ch"),
            P(("batch", "pos"), "ch"),
            P("ch"),
            P(("batch", "pos"), "ch"),
        ),
        check_vma=False,
    )
```

```python
import functools

import jax
import jax.numpy as jnp
from jax import lax
from jax.experimental import pallas as pl
from jax.experimental.pallas import tpu as pltpu
from jax.sharding import PartitionSpec as P

KW = 5
RIM = KW // 2
PIECES = KW + 1
EPS = 1e-05
MESH = pl.DeviceIdType.MESH
C0 = 0.7978845608028654
C1 = 0.044715
F32 = jnp.float32
BF16 = jnp.bfloat16
VMEM_LIMIT = 60 * 1024 * 1024

NT = (((1,), (1,)), ((), ()))
TN = (((0,), (0,)), ((), ()))


def params(**kw):
    return pltpu.CompilerParams(vmem_limit_bytes=VMEM_LIMIT, **kw)


def gelu(u):
    return 0.5 * u * (1.0 + jnp.tanh(C0 * (u + C1 * u * u * u)))


def gelu_slope(u):
    square = u * u
    t = jnp.tanh(C0 * (u + C1 * square * u))
    return 0.5 * (1.0 + t) + 0.5 * u * (1.0 - t * t) * (C0 + (3.0 * C0 * C1) * square)


class Reduce:
    def __init__(self, value, core_in, near, far, result, sems):
        self.value, self.core_in, self.near, self.far, self.result = value, core_in, near, far, result
        self.send, self.recv = sems
        self.batch, self.pos, self.ch = (lax.axis_index(a) for a in ("batch", "pos", "ch"))
        self.core = lax.rem(self.pos, 2)
        self.z = self.pos // 2
        self.far_count = lax.axis_size("pos") // 2
        half = value.shape[1] // 2
        self.mine = pl.ds(pl.multiple_of(self.core * half, half), half)
        self.away = pl.ds(pl.multiple_of((1 - self.core) * half, half), half)
        self.me = self.batch * 2 + self.ch
        self.core_peer = (self.batch, self.z * 2 + 1 - self.core, self.ch)
        self.near_peers = []
        for step in range(1, 4):
            other = lax.rem(self.me + step, 4)
            self.near_peers.append((other // 2, self.pos, lax.rem(other, 2)))
        self.far_peers = []
        for step in range(1, self.far_count):
            other = lax.rem(self.z + step, self.far_count)
            self.far_peers.append((self.batch, other * 2 + self.core, self.ch))

    @staticmethod
    def scratch(width):
        far = lax.axis_size("pos") // 2
        count = 2 + 3 + far - 1
        return [
            pltpu.VMEM((8, width), F32),
            pltpu.VMEM((8, width // 2), F32),
            pltpu.VMEM((4, 8, width // 2), F32),
            pltpu.VMEM((far, 8, width // 2), F32),
            pltpu.VMEM((8, width), F32),
            pltpu.SemaphoreType.DMA((count,)),
            pltpu.SemaphoreType.DMA((count,)),
        ]

    def peers(self):
        return [self.core_peer] + self.near_peers + self.far_peers

    def copy(self, i, src, dst, peer):
        return pltpu.make_async_remote_copy(
            src, dst, self.send.at[i], self.recv.at[i], device_id=peer, device_id_type=MESH
        )

    def copies(self, stage):
        if stage == 0:
            return [self.copy(0, self.value.at[:, self.away], self.core_in, self.core_peer)]
        if stage == 1:
            slot = self.near.at[self.me]
            return [self.copy(1 + i, slot, slot, p) for i, p in enumerate(self.near_peers)]
        if stage == 2:
            slot = self.far.at[self.z]
            return [self.copy(4 + i, slot, slot, p) for i, p in enumerate(self.far_peers)]
        part = self.result.at[:, self.mine]
        return [self.copy(3 + self.far_count, part, part, self.core_peer)]

    def wait(self, stage):
        for copy in self.copies(stage):
            copy.wait()

    def start(self, stage):
        if stage == 1:
            self.wait(0)
            self.near[pl.ds(self.me, 1)] = (self.value[:, self.mine] + self.core_in[...])[None]
        if stage == 2:
            self.wait(1)
            total = (self.near[0] + self.near[1]) + (self.near[2] + self.near[3])
            self.far[pl.ds(self.z, 1)] = total[None]
        if stage == 3:
            self.wait(2)
            total = self.far[0]
            for i in range(1, self.far_count):
                total = total + self.far[i]
            self.result[:, self.mine] = total
        for copy in self.copies(stage):
            copy.start()


def meet(peers):
    barrier = pltpu.get_barrier_semaphore()
    for peer in peers:
        pl.semaphore_signal(barrier, inc=1, device_id=peer, device_id_type=MESH)
    pl.semaphore_wait(barrier, len(peers))


def reduce_kernel(v_ref, o_ref, *scratch):
    value, core_in, near, far, result, send, recv = scratch
    reduce = Reduce(value, core_in, near, far, result, (send, recv))
    value[...] = v_ref[...]
    meet(reduce.peers())
    for stage in range(4):
        reduce.start(stage)
    reduce.wait(3)
    o_ref[...] = result[...]


def reduce_all(values, collective_id):
    rows, width = values.shape
    total = pl.pallas_call(
        reduce_kernel,
        out_shape=jax.ShapeDtypeStruct((8, width), F32),
        in_specs=[pl.BlockSpec(memory_space=pltpu.VMEM)],
        out_specs=pl.BlockSpec(memory_space=pltpu.VMEM),
        scratch_shapes=Reduce.scratch(width),
        compiler_params=params(collective_id=collective_id, has_side_effects=True),
        name="reduce",
    )(jnp.pad(values, ((0, 8 - rows), (0, 0))))
    return total[:rows]


def hidden_kernel(who, x_ref, vec_ref, h_ref, scr):
    lanes, ext = scr.shape[:2]
    first, total = who[0], who[1]
    center = vec_ref[0, 0:1, :]
    scale = vec_ref[0, 1:2, :]
    bias = vec_ref[0, 2:3, :]

    @pl.loop(0, ext // 16)
    def _(i):
        at = pl.multiple_of(i * 16, 16)
        x = x_ref[0, pl.ds(at, 16), :].astype(F32)
        act = (x - center) * scale + bias
        row = first + at + lax.broadcasted_iota(jnp.int32, x.shape, 0)
        inside = jnp.logical_and(row >= 0, row < total)
        hidden = jnp.where(inside, gelu(act), 0.0)
        for b in range(lanes):
            scr[b, pl.ds(at, 16), :] = hidden[:, b * 128 : (b + 1) * 128]

    @pl.loop(0, h_ref.shape[2] // 16)
    def _(i):
        at = pl.multiple_of(i * 16, 16)
        for b in range(lanes):
            lane = slice(b * 128, (b + 1) * 128)
            for d in range(PIECES):
                h_ref[d, 0, pl.ds(at, 16), lane] = scr[
                    b, pl.ds(16 - RIM + d + 2 * at, 16, stride=2), :
                ].astype(BF16)


def make_hidden(who, x_ext, vecs, half):
    micro_count, ext, wide = x_ext.shape
    pairs = half // 2
    return pl.pallas_call(
        hidden_kernel,
        out_shape=jax.ShapeDtypeStruct((PIECES, micro_count, pairs, wide), BF16),
        grid_spec=pltpu.PrefetchScalarGridSpec(
            num_scalar_prefetch=1,
            grid=(micro_count,),
            in_specs=[
                pl.BlockSpec((1, ext, wide), lambda m, w: (m, 0, 0)),
                pl.BlockSpec((1, 8, wide), lambda m, w: (m, 0, 0)),
            ],
            out_specs=pl.BlockSpec((PIECES, 1, pairs, wide), lambda m, w: (0, m, 0, 0)),
            scratch_shapes=[pltpu.VMEM((wide // 128, ext, 128), F32)],
        ),
        compiler_params=params(),
        cost_estimate=pl.CostEstimate(flops=10**10, bytes_accessed=2 * 10**7, transcendentals=0),
        name="hidden",
    )(who, x_ext, vecs)


def head_kernel(
    total_rows,
    x,
    w1,
    w2,
    wp,
    og,
    small_ref,
    hp,
    xs_out,
    f_own,
    f_other,
    w1x,
    w2x,
    wpx,
    ogx,
    vec1,
    vec2,
    small_x,
    x_loc,
    x_ext,
    scr,
    raw,
    h_cat,
    xs,
    w_buf,
    f_buf,
    load_sem,
    w_sem,
    f_sem,
    out_sem,
    in_send,
    in_recv,
    halo_send,
    halo_recv,
    y1_send,
    y1_recv,
    z1_send,
    z1_recv,
    x1_send,
    x1_recv,
    c1_send,
    c1_recv,
    y2_send,
    y2_recv,
    c2_send,
    c2_recv,
    og_send,
    og_recv,
    small_send,
    small_recv,
    value,
    r_core,
    r_near,
    r_far,
    r_result,
    r_send,
    r_recv,
    value2,
    s_core,
    s_near,
    s_far,
    s_result,
    s_send,
    s_recv,
):
    first = Reduce(value, r_core, r_near, r_far, r_result, (r_send, r_recv))
    second = Reduce(value2, s_core, s_near, s_far, s_result, (s_send, s_recv))
    batch, pos, ch, core, z = first.batch, first.pos, first.ch, first.core, first.z
    far_count = first.far_count
    pos_count = 2 * far_count
    plane = 2 * pos_count
    micro_count, local_rows, local_in = x.shape
    wide = 2 * local_in
    half = local_rows // 2
    pairs = half // 2
    rows = micro_count * pairs
    ext = half + 32
    main = half + 16
    local_out = w1.shape[1]
    parts, chunk = w_buf.shape[0], w_buf.shape[2]
    lanes_count = wide // 128
    y_peer = (batch, pos, 1 - ch)
    x_peer = (1 - batch, pos, ch)
    up_pos = lax.rem(pos + 1, pos_count)
    down_pos = lax.rem(pos + pos_count - 1, pos_count)

    def remote(src, dst, send, recv, peer):
        return pltpu.make_async_remote_copy(src, dst, send, recv, device_id=peer, device_id_type=MESH)

    my_lanes = pl.ds(pl.multiple_of(ch * local_in, 128), local_in)

    def own_input():
        begin = pl.multiple_of(ch * (half - 16), 16)
        return pltpu.make_async_copy(
            x.at[:, pl.ds(begin, main), :],
            x_ext.at[:, pl.ds(pl.multiple_of(16 - 16 * ch, 16), main), my_lanes],
            load_sem.at[0],
        )

    def main_input():
        begin = pl.multiple_of((1 - ch) * (half - 16), 16)
        return remote(
            x.at[:, pl.ds(begin, main), :],
            x_ext.at[:, pl.ds(pl.multiple_of(16 * ch, 16), main), my_lanes],
            in_send,
            in_recv,
            y_peer,
        )

    def halo_up(s):
        return remote(
            x.at[:, local_rows - 16 : local_rows, :],
            x_ext.at[:, 0:16, my_lanes],
            halo_send.at[0],
            halo_recv.at[s],
            (batch, up_pos, 0),
        )

    def halo_down(s):
        return remote(
            x.at[:, 0:16, :],
            x_ext.at[:, ext - 16 : ext, my_lanes],
            halo_send.at[1],
            halo_recv.at[s],
            (batch, down_pos, 1),
        )

    def piece_rows(count):
        return -(-(count // plane) // 16) * 16

    def piece_at(count, bb, zz, cc):
        size = piece_rows(count)
        start = ((bb * far_count + zz) * 2 + cc) * size
        if size * plane != count:
            start = jnp.minimum(start, count - size)
        return pl.ds(pl.multiple_of(start, 16), size)

    class Fetch:
        def __init__(self, number, src, dst, lanes):
            self.number, self.src, self.dst, self.lanes = number, src, dst, lanes
            self.count = src.shape[0]

        def at(self, ref, bb, zz, cc):
            return ref.at[piece_at(self.count, bb, zz, cc), self.lanes]

        def over_y(self):
            return remote(
                self.at(self.src, batch, z, core),
                self.at(self.dst, batch, z, core),
                y1_send.at[self.number],
                y1_recv.at[self.number],
                y_peer,
            )

        def over_z(self, r):
            there = lax.rem(z + order[r], far_count)
            part = self.at(self.dst, batch, z, core)
            return remote(
                part, part, z1_send.at[self.number, r], z1_recv.at[self.number, r], (batch, there * 2 + core, ch)
            )

        def source(self, r):
            if r == 0:
                return z
            return lax.rem(z + far_count - order[r - 1], far_count)

        def over_x(self, r):
            part = self.at(self.dst, batch, self.source(r), core)
            return remote(part, part, x1_send.at[self.number, r], x1_recv.at[self.number, r], x_peer)

        def over_core(self, r, bb):
            part = self.at(self.dst, batch if bb == 0 else 1 - batch, self.source(r), core)
            return remote(
                part, part, c1_send.at[self.number, bb, r], c1_recv.at[self.number, bb, r], first.core_peer
            )

        def begin(self):
            self.over_x(0).start()
            self.over_z(0).start()
            self.over_core(0, 0).start()

        def step(self, r):
            self.over_z(r).wait_recv()
            if r + 1 < far_count - 1:
                self.over_z(r + 1).start()
            self.over_x(r + 1).start()
            self.over_core(r + 1, 0).start()

        def end(self):
            for r in range(far_count):
                self.over_x(r).wait_recv()
                self.over_core(r, 1).start()

        def done(self):
            for r in range(far_count):
                for bb in range(2):
                    self.over_core(r, bb).wait_recv()

        def drain(self):
            self.over_y().wait_send()
            for r in range(far_count - 1):
                self.over_z(r).wait_send()
            for r in range(far_count):
                self.over_x(r).wait_send()
                for bb in range(2):
                    self.over_core(r, bb).wait_send()

    order = [1, 3, 2] if far_count == 4 else list(range(1, far_count))
    fetch1 = [
        Fetch(c, w1, w1x, slice(c * chunk, (c + 1) * chunk)) for c in range(local_out // chunk)
    ]
    fetch_p = Fetch(len(fetch1), wp, wpx, slice(0, local_out))

    half2 = w2.shape[0] // 2
    part2 = pl.ds(pl.multiple_of(core * half2, 16), half2)

    def second_y():
        return remote(w2.at[part2], w2x.at[part2], y2_send, y2_recv, y_peer)

    def second_core():
        return remote(w2x.at[part2], w2x.at[part2], c2_send, c2_recv, first.core_peer)

    bins = og.shape[1] // 2

    def og_local():
        at = pl.ds(pl.multiple_of(ch * bins, 16), bins)
        return pltpu.make_async_copy(og.at[:, at, :], ogx.at[:, :, 0:local_out], load_sem.at[1])

    def og_remote():
        at = pl.ds(pl.multiple_of((1 - ch) * bins, 16), bins)
        return remote(og.at[:, at, :], ogx.at[:, :, local_out : 2 * local_out], og_send, og_recv, y_peer)

    def small_copy():
        return remote(small_ref, small_x, small_send, small_recv, y_peer)

    def x_load():
        return pltpu.make_async_copy(x, x_loc, load_sem.at[2])

    tiles = local_out // chunk

    def w_load(i):
        src = w1 if i < tiles else w1x
        c = i % tiles
        return pltpu.make_async_copy(
            src.at[:, c * chunk : (c + 1) * chunk], w_buf.at[i % parts], w_sem.at[i % parts]
        )

    x_load().start()
    own_input().start()
    og_local().start()
    w_load(0).start()
    w_load(1).start()
    meet_peers = first.peers() + [
        (batch, lax.rem(pos + pos_count + 2 * ch - 1, pos_count), 0),
        (batch, lax.rem(pos + pos_count + 2 * ch - 1, pos_count), 1),
    ]
    meet(meet_peers)
    small_copy().start()
    fetch1[0].over_y().start()
    halo_up(ch).start()
    halo_down(ch).start()

    value[...] = jnp.zeros_like(value)
    x_load().wait()
    for m in range(micro_count):

        def add(i, sums):
            part = x_loc[m, pl.ds(pl.multiple_of(i * 64, 64), 64), :].astype(F32).reshape(8, 8, local_in)
            return sums[0] + jnp.sum(part, axis=0), sums[1] + jnp.sum(part * part, axis=0)

        zero = jnp.zeros((8, local_in), F32)
        plain, square = lax.fori_loop(0, local_rows // 64, add, (zero, zero))
        value[2 * m : 2 * m + 1, my_lanes] = jnp.sum(plain, axis=0, keepdims=True)
        value[2 * m + 1 : 2 * m + 2, my_lanes] = jnp.sum(square, axis=0, keepdims=True)
    first.start(0)
    first.start(1)
    fetch1[0].over_y().wait_recv()
    fetch1[0].begin()
    fetch1[1].over_y().start()
    first.start(2)
    first.start(3)
    fetch1[1].over_y().wait_recv()
    main_input().start()
    small_copy().wait_recv()
    first.wait(3)
    gain = jnp.zeros((1, wide), F32)
    scale = 1.0 / total_rows
    for m in range(micro_count):
        center = r_result[2 * m : 2 * m + 1, :] * scale
        square = r_result[2 * m + 1 : 2 * m + 2, :] * scale
        inverse = lax.rsqrt(square - center * center + EPS)
        vec1[m, 0:1, :] = center
        vec1[m, 3:4, :] = inverse
        for source, lanes in ((small_ref, ch), (small_x, 1 - ch)):
            at = pl.ds(pl.multiple_of(lanes * local_in, 128), local_in)
            vec1[m, 1:2, at] = vec1[m, 3:4, at] * source[4:5, 0:local_in]
            vec1[m, 2:3, at] = source[5:6, 0:local_in]
        vec1[m, 4:8, :] = jnp.zeros((4, wide), F32)

    for r in range(far_count - 1):
        fetch1[0].step(r)
    fetch1[1].begin()
    for r in range(far_count - 3):
        fetch1[1].step(r)
    main_input().wait_recv()
    own_input().wait()
    for s in range(2):
        halo_up(s).wait_recv()
    fetch_p.over_y().start()
    second_y().start()

    begin = pos * local_rows + ch * half - 16
    for m in range(micro_count):

        @pl.loop(0, ext // 16)
        def _(i):
            at = pl.multiple_of(i * 16, 16)
            v = x_ext[m, pl.ds(at, 16), :].astype(F32)
            act = (v - vec1[m, 0:1, :]) * vec1[m, 1:2, :] + vec1[m, 2:3, :]
            row = begin + at + lax.broadcasted_iota(jnp.int32, v.shape, 0)
            inside = jnp.logical_and(row >= 0, row < pos_count * local_rows)
            hidden = jnp.where(inside, gelu(act), 0.0)
            for b in range(lanes_count):
                scr[b, pl.ds(at, 16), :] = hidden[:, b * 128 : (b + 1) * 128]
                raw[b, pl.ds(at, 16), :] = v[:, b * 128 : (b + 1) * 128]

        @pl.loop(0, pairs // 16)
        def _(i):
            at = pl.multiple_of(i * 16, 16)
            to = pl.ds(pl.multiple_of(m * pairs + at, 16), 16)
            for b in range(lanes_count):
                for d in range(PIECES):
                    h_cat[to, d * wide + b * 128 : d * wide + (b + 1) * 128] = scr[
                        b, pl.ds(16 - RIM + d + 2 * at, 16, stride=2), :
                    ].astype(BF16)
                for e in range(2):
                    xs[e, to, b * 128 : (b + 1) * 128] = raw[
                        b, pl.ds(16 + e + 2 * at, 16, stride=2), :
                    ].astype(BF16)

    def pieces_out():
        copies = [
            pltpu.make_async_copy(h_cat.at[:, d * wide : (d + 1) * wide], hp.at[d], out_sem.at[d])
            for d in range(PIECES)
        ]
        return copies + [pltpu.make_async_copy(xs, xs_out, out_sem.at[PIECES])]

    for copy in pieces_out():
        copy.start()

    def f_copy(i):
        dst = f_own if i < tiles else f_other
        c = i % tiles
        return pltpu.make_async_copy(
            f_buf.at[i % 2], dst.at[:, :, c * chunk : (c + 1) * chunk], f_sem.at[i % 2]
        )

    value2[...] = jnp.zeros_like(value2)

    def conv(i):
        w_load(i).wait()
        if i >= 2:
            f_copy(i - 2).wait()
        c = i % tiles
        source, side = (small_ref, ch) if i < tiles else (small_x, 1 - ch)
        bias = source[0:1, c * chunk : (c + 1) * chunk]
        at = pl.ds(pl.multiple_of(side * local_out + c * chunk, 128), chunk)
        sums = [[0.0, 0.0] for _ in range(micro_count)]
        for e in range(2):
            acc = jnp.dot(
                h_cat[:, e * wide : (e + KW) * wide], w_buf[i % parts], preferred_element_type=F32
            )
            acc += bias
            f_buf[i % 2, e] = acc
            for m in range(micro_count):
                part = acc[m * pairs : (m + 1) * pairs]
                sums[m][0] += jnp.sum(part, axis=0, keepdims=True)
                sums[m][1] += jnp.sum(part * part, axis=0, keepdims=True)
        for m in range(micro_count):
            for k in range(2):
                value2[2 * m + k : 2 * m + k + 1, at] = sums[m][k]
        f_copy(i).start()

    fetch1[0].end()
    fetch1[1].step(far_count - 3)
    conv(0)
    fetch1[0].done()
    w_load(2).start()
    conv(1)
    og_remote().start()
    fetch1[1].step(far_count - 2)
    fetch_p.over_y().wait_recv()
    fetch_p.begin()
    conv(2)
    for r in range(far_count - 1):
        fetch_p.step(r)
    fetch1[1].end()
    fetch1[1].done()
    w_load(3).start()
    second_y().wait_recv()
    second_core().start()
    fetch_p.end()
    conv(3)
    second.start(0)
    for copy in pieces_out():
        copy.wait()
    second.start(1)
    fetch_p.done()
    second.start(2)
    second_core().wait()
    second.start(3)
    og_local().wait()
    og_remote().wait()
    for f in fetch1 + [fetch_p]:
        f.drain()
    second_y().wait_send()
    main_input().wait_send()
    halo_up(0).wait_send()
    halo_down(0).wait_send()
    small_copy().wait_send()
    f_copy(2).wait()
    f_copy(3).wait()
    second.wait(3)
    for m in range(micro_count):
        for q, (source, side) in enumerate(((small_ref, ch), (small_x, 1 - ch))):
            at = pl.ds(pl.multiple_of(side * local_out, 128), local_out)
            to = slice(q * local_out, (q + 1) * local_out)
            center = s_result[2 * m : 2 * m + 1, at] * scale
            square = s_result[2 * m + 1 : 2 * m + 2, at] * scale
            vec2[m, 0:1, to] = center
            vec2[m, 1:2, to] = lax.rsqrt(square - center * center + EPS)
            vec2[m, 2:5, to] = source[1:4, :]
            vec2[m, 5:8, to] = jnp.zeros((3, local_out), F32)


def head(x, w1, w2, wp, og, small, total_rows):
    micro_count, local_rows, local_in = x.shape
    wide = 2 * local_in
    half = local_rows // 2
    pairs = half // 2
    rows = micro_count * pairs
    ext = half + 32
    local_out = w1.shape[1]
    out = 2 * local_out
    chunk = local_out // 2
    far = lax.axis_size("pos") // 2
    any_space = pl.BlockSpec(memory_space=pl.ANY)
    in_vmem = pl.BlockSpec(memory_space=pltpu.VMEM)
    dma = pltpu.SemaphoreType.DMA
    fetches = local_out // chunk + 1
    return pl.pallas_call(
        functools.partial(head_kernel, total_rows),
        out_shape=(
            jax.ShapeDtypeStruct((PIECES, rows, wide), BF16),
            jax.ShapeDtypeStruct((2, rows, wide), BF16),
            jax.ShapeDtypeStruct((2, rows, local_out), F32),
            jax.ShapeDtypeStruct((2, rows, local_out), F32),
            jax.ShapeDtypeStruct(w1.shape, BF16),
            jax.ShapeDtypeStruct(w2.shape, BF16),
            jax.ShapeDtypeStruct(wp.shape, BF16),
            jax.ShapeDtypeStruct((micro_count, og.shape[1] // 2, out), BF16),
            jax.ShapeDtypeStruct((micro_count, 8, wide), F32),
            jax.ShapeDtypeStruct((micro_count, 8, out), F32),
        ),
        in_specs=[any_space] * 5 + [in_vmem],
        out_specs=(any_space,) * 8 + (in_vmem,) * 2,
        scratch_shapes=[
            pltpu.VMEM((8, local_out), F32),
            pltpu.VMEM((micro_count, local_rows, local_in), BF16),
            pltpu.VMEM((micro_count, ext, wide), BF16),
            pltpu.VMEM((wide // 128, ext, 128), F32),
            pltpu.VMEM((wide // 128, ext, 128), F32),
            pltpu.VMEM((rows, PIECES * wide), BF16),
            pltpu.VMEM((2, rows, wide), BF16),
            pltpu.VMEM((2, KW * wide, chunk), BF16),
            pltpu.VMEM((2, 2, rows, chunk), F32),
            dma((3,)),
            dma((2,)),
            dma((2,)),
            dma((PIECES + 1,)),
            dma,
            dma,
            dma((2,)),
            dma((2,)),
            dma((fetches,)),
            dma((fetches,)),
            dma((fetches, far - 1)),
            dma((fetches, far - 1)),
            dma((fetches, far)),
            dma((fetches, far)),
            dma((fetches, 2, far)),
            dma((fetches, 2, far)),
            dma,
            dma,
            dma,
            dma,
            dma,
            dma,
            dma,
            dma,
        ]
        + Reduce.scratch(wide)
        + Reduce.scratch(out),
        compiler_params=params(collective_id=6, has_side_effects=True),
        name="head",
    )(x, w1, w2, wp, og, small)


class Scatter:
    def __init__(self, reduce, kept, sent, x_in, z_in, y_out, y_in, sems, steps):
        self.reduce, self.kept, self.sent = reduce, kept, sent
        self.x_in, self.z_in, self.y_out, self.y_in = x_in, z_in, y_out, y_in
        self.x_send, self.x_recv, self.z_send, self.z_recv, self.y_send, self.y_recv = sems
        self.steps = steps
        self.count = reduce.far_count
        self.half = y_in.shape[1]

    @staticmethod
    def scratch(block, width):
        far = lax.axis_size("pos") // 2
        dma = pltpu.SemaphoreType.DMA
        return [
            pltpu.VMEM((far, block, width), BF16),
            pltpu.VMEM((far - 1, block, width), BF16),
            pltpu.VMEM((block, width // 2), BF16),
            pltpu.VMEM((block, width // 2), BF16),
            dma((far,)),
            dma((far,)),
            dma((far - 1,)),
            dma((far - 1,)),
            dma,
            dma,
        ]

    def away(self, r):
        return lax.rem(self.reduce.z + self.steps[r], self.count)

    def copy(self, src, dst, send, recv, peer):
        return pltpu.make_async_remote_copy(src, dst, send, recv, device_id=peer, device_id_type=MESH)

    def over_x(self, r):
        zz, me = self.away(r), self.reduce
        peer = (1 - me.batch, me.pos, me.ch)
        return self.copy(self.sent(zz), self.x_in.at[zz], self.x_send.at[zz], self.x_recv.at[zz], peer)

    def over_z(self, r):
        zz, me = self.away(r), self.reduce
        peer = (me.batch, zz * 2 + me.core, me.ch)
        return self.copy(self.x_in.at[zz], self.z_in.at[r], self.z_send.at[r], self.z_recv.at[r], peer)

    def over_y(self):
        me = self.reduce
        return self.copy(self.y_out, self.y_in, self.y_send, self.y_recv, (me.batch, me.pos, 1 - me.ch))

    def send_x(self, r):
        self.over_x(r).start()

    def send_z(self, r):
        zz = self.away(r)
        self.over_x(r).wait_recv()
        self.x_in[zz] = (self.x_in[zz].astype(F32) + self.kept(zz)[...].astype(F32)).astype(BF16)
        if r < self.count - 1:
            self.over_z(r).start()

    def send_y(self):
        zz = self.away(self.count - 1)
        total = self.x_in[zz].astype(F32)
        for r in range(self.count - 1):
            self.over_z(r).wait_recv()
            total = total + self.z_in[r].astype(F32)
        self.y_out[...] = total[:, self.half :].astype(BF16)
        self.over_y().start()
        return total[:, : self.half]

    def finish(self):
        self.over_y().wait_recv()
        return self.y_in[...].astype(F32)

    def drain(self):
        for r in range(self.count):
            self.over_x(r).wait_send()
            if r < self.count - 1:
                self.over_z(r).wait_send()
        self.over_y().wait_send()


def round_steps(far_count):
    if far_count == 4:
        return [2, 1, 3, 0]
    return list(range(far_count // 2, far_count)) + list(range(1, far_count // 2)) + [0]


def middle_kernel(
    scatter,
    total_rows,
    f_own,
    f_other,
    w2_own,
    w2_other,
    wp_own,
    wp_other,
    ogx,
    x,
    vec_ref,
    lim_ref,
    pooled_out,
    gp,
    xa,
    dw2_out,
    dwp_out,
    sum_out,
    extra,
    w2_ref,
    wp_ref,
    first,
    so,
    a2g,
    hid,
    branch,
    diff,
    lg,
    og,
    pooled,
    dwp,
    dw2,
    p_core,
    q_core,
    low32,
    edge_out,
    edge_in,
    w_sem,
    f_sem,
    misc_sem,
    gp_sem,
    pooled_sem,
    pooled_send,
    pooled_recv,
    xa_send,
    xa_recv,
    rim_send,
    rim_recv,
    edge_send,
    edge_recv,
    pc_send,
    pc_recv,
    qc_send,
    qc_recv,
    value,
    r_core,
    r_near,
    r_far,
    r_result,
    r_send,
    r_recv,
    x_in,
    z_in,
    y_out,
    y_in,
    *s_sems,
):
    reduce = Reduce(value, r_core, r_near, r_far, r_result, (r_send, r_recv))
    batch, pos, ch, core, z = reduce.batch, reduce.pos, reduce.ch, reduce.core, reduce.z
    far_count = reduce.far_count
    pos_count = 2 * far_count
    _, micro_count, pairs, wide = first.shape
    rows = 2 * pairs
    half = wide // 2
    tile = 256
    tiles = wide // tile
    y_peer = (batch, pos, 1 - ch)
    local_rows, local_in = x.shape[1:]
    half_rows = local_rows // 2
    ext = xa.shape[1]
    main = half_rows + 16

    def columns(j):
        return pl.ds(pl.multiple_of(j * tile, tile), tile)

    def natural(j):
        at = lax.rem(j * tile + ch * half, wide)
        return pl.ds(pl.multiple_of(at, tile), tile)

    def remote(src, dst, send, recv, peer):
        return pltpu.make_async_remote_copy(src, dst, send, recv, device_id=peer, device_id_type=MESH)

    def w_copies(kind):
        copies = []
        dst = (w2_ref, wp_ref)[kind]
        for q, src in enumerate(((w2_own, w2_other), (wp_own, wp_other))[kind]):
            for r in range(2):
                at = pl.ds(pl.multiple_of(lax.rem(ch + r, 2) * half, 16), half)
                copies.append(
                    pltpu.make_async_copy(
                        src.at[at, :],
                        dst.at[r * half : (r + 1) * half, q * half : (q + 1) * half],
                        w_sem.at[kind, q, r],
                    )
                )
        return copies

    def f_copies():
        return [
            pltpu.make_async_copy(src, first.at[:, :, :, q * half : (q + 1) * half], f_sem.at[q])
            for q, src in enumerate((f_own, f_other))
        ]

    def og_copy():
        return pltpu.make_async_copy(ogx, og, misc_sem.at[0])

    lanes_in = pl.ds(pl.multiple_of(ch * local_in, 128), local_in)

    def xa_local():
        begin = pl.multiple_of((1 - ch) * (half_rows - 16), 16)
        return pltpu.make_async_copy(
            x.at[:, pl.ds(begin, main), :],
            xa.at[:, pl.ds(pl.multiple_of(16 * ch, 16), main), lanes_in],
            misc_sem.at[1],
        )

    def xa_remote():
        begin = pl.multiple_of(ch * (half_rows - 16), 16)
        return remote(
            x.at[:, pl.ds(begin, main), :],
            xa.at[:, pl.ds(pl.multiple_of(16 * (1 - ch), 16), main), lanes_in],
            xa_send,
            xa_recv,
            y_peer,
        )

    def rim_up(s):
        return remote(
            x.at[:, local_rows - 16 : local_rows, :],
            xa.at[:, 0:16, lanes_in],
            rim_send.at[0],
            rim_recv.at[s],
            (batch, lax.rem(pos + 1, pos_count), 1),
        )

    def rim_down(s):
        return remote(
            x.at[:, 0:16, :],
            xa.at[:, ext - 16 : ext, lanes_in],
            rim_send.at[1],
            rim_recv.at[s],
            (batch, lax.rem(pos + pos_count - 1, pos_count), 0),
        )

    right = (batch, lax.rem(pos + ch, pos_count), 1 - ch)
    left = (batch, lax.rem(pos + pos_count - 1 + ch, pos_count), 1 - ch)
    rim_from = lax.rem(pos + pos_count + 1 - 2 * ch, pos_count)

    for copy in f_copies():
        copy.start()
    for kind in range(2):
        for copy in w_copies(kind):
            copy.start()
    og_copy().start()
    xa_local().start()
    meet(reduce.peers() + [right, left, (batch, rim_from, 0), (batch, rim_from, 1)])
    xa_remote().start()
    rim_up(ch).start()
    rim_down(ch).start()
    value[...] = jnp.zeros_like(value)
    for copy in f_copies():
        copy.wait()

    def normal(m, e, c):
        return (first[e, m, :, c] - vec_ref[m, 0:1, c]) * vec_ref[m, 1:2, c]

    def forward(m):
        @pl.loop(0, tiles)
        def _(j):
            c = columns(j)
            for e in range(2):
                act = normal(m, e, c) * vec_ref[m, 2:3, c] + vec_ref[m, 3:4, c]
                hid[m, e * pairs : (e + 1) * pairs, c] = gelu(act).astype(BF16)

        if m == 0:
            for copy in w_copies(0):
                copy.wait()

        @pl.loop(0, tiles)
        def _(j):
            c = columns(j)
            step = jnp.dot(hid[m], w2_ref[:, c], preferred_element_type=F32)
            even = step[:pairs] + (first[0, m, :, c] + vec_ref[m, 4:5, c])
            odd = step[pairs:] + (first[1, m, :, c] + vec_ref[m, 4:5, c])
            so[m, 0, :, c] = even
            so[m, 1, :, c] = odd
            diff[m, :, c] = (even - odd).astype(BF16)

        if m == 0:
            for copy in w_copies(1):
                copy.wait()
            og_copy().wait()
        limit = lim_ref[m, 0:1, 0:1]
        inverse_limit = 1.0 / limit

        @pl.loop(0, tiles)
        def _(j):
            c = columns(j)
            d = jnp.dot(diff[m], wp_ref[:, c], preferred_element_type=F32)
            t = jnp.tanh(0.5 * d)
            weight_even = 0.5 + 0.5 * t
            weight_odd = 0.5 - 0.5 * t
            even, odd = so[m, 0, :, c], so[m, 1, :, c]
            pooled[m, :, c] = (weight_even * even + weight_odd * odd).astype(BF16)
            clipped = limit * jnp.tanh(og[m, :, c].astype(F32) * inverse_limit)
            lg[m, :, c] = (weight_even * weight_odd * (even - odd) * clipped).astype(BF16)
            so[m, 0, :, c] = weight_even * clipped
            so[m, 1, :, c] = weight_odd * clipped

        pooled_local(m).start()
        pooled_remote(m).start()

    bins_at = pl.ds(pl.multiple_of(ch * pairs, 16), pairs)

    def pooled_local(m):
        return pltpu.make_async_copy(pooled.at[m, :, 0:half], pooled_out.at[m, bins_at], pooled_sem.at[m])

    def pooled_remote(m):
        return remote(
            pooled.at[m, :, half:wide], pooled_out.at[m, bins_at], pooled_send.at[m], pooled_recv.at[m], y_peer
        )

    def pool_back(m):
        @pl.loop(0, tiles)
        def _(j):
            c = columns(j)
            g = lax.dot_general(lg[m], wp_ref[c, :], NT, preferred_element_type=F32)
            even = so[m, 0, :, c] + g
            odd = so[m, 1, :, c] - g
            so[m, 0, :, c] = even
            so[m, 1, :, c] = odd
            low_even, low_odd = even.astype(BF16), odd.astype(BF16)
            branch[m, 0:pairs, c] = low_even
            branch[m, pairs:rows, c] = low_odd
            both = low_even.astype(F32) + low_odd.astype(F32)
            value[3 * m + 2 : 3 * m + 3, natural(j)] = jnp.sum(both, axis=0, keepdims=True)

    def act_back(m):
        @pl.loop(0, tiles)
        def _(j):
            c = columns(j)
            hg = lax.dot_general(branch[m], w2_ref[c, :], NT, preferred_element_type=F32)
            plain, cross = 0.0, 0.0
            for e in range(2):
                normed = normal(m, e, c)
                act = normed * vec_ref[m, 2:3, c] + vec_ref[m, 3:4, c]
                grad = hg[e * pairs : (e + 1) * pairs] * gelu_slope(act)
                a2g[m, e, :, c] = grad
                plain += jnp.sum(grad, axis=0, keepdims=True)
                cross += jnp.sum(grad * normed, axis=0, keepdims=True)
            value[3 * m : 3 * m + 1, natural(j)] = plain
            value[3 * m + 1 : 3 * m + 2, natural(j)] = cross

    blocks = 4 * far_count
    block = wide // blocks

    def product(dst, left, right_side):
        depth = left.shape[0] * left.shape[1]

        @pl.loop(0, tiles)
        def _(j):
            c = columns(j)
            dst[c, :] = lax.dot_general(
                left[:, :, c].reshape(depth, tile),
                right_side[...].reshape(depth, wide),
                TN,
                preferred_element_type=F32,
            ).astype(BF16)

    def block_rows(bb, zz, cc):
        number = lax.rem((bb * far_count + zz) * 2 + cc + ch * (blocks // 2), blocks)
        return pl.ds(pl.multiple_of(number * block, 16), block)

    def core_copies(src, dst, send, recv):
        return [
            remote(
                src.at[block_rows(bb, zz, 1 - core)], dst.at[bb, zz], send.at[bb, zz], recv.at[bb, zz], reduce.core_peer
            )
            for bb in range(2)
            for zz in range(far_count)
        ]

    def add_core(src, dst, sends):
        i = 0
        for bb in range(2):
            for zz in range(far_count):
                sends[i].wait_recv()
                i += 1
                mine = src[block_rows(bb, zz, core), :].astype(F32)
                dst[bb, zz] = (dst[bb, zz].astype(F32) + mine).astype(BF16)

    p_sends = core_copies(dwp, p_core, pc_send, pc_recv) if scatter else []
    q_sends = core_copies(dw2, q_core, qc_send, qc_recv) if scatter else []
    steps = round_steps(far_count)
    pool = Scatter(
        reduce,
        lambda zz: p_core.at[batch, zz],
        lambda zz: p_core.at[1 - batch, zz],
        x_in,
        z_in,
        y_out,
        y_in,
        s_sems,
        steps,
    )

    def dw2_copy():
        return pltpu.make_async_copy(q_core if scatter else dw2, dw2_out, misc_sem.at[2])

    for m in range(micro_count):
        forward(m)
    product(dwp, diff, lg)
    for copy in p_sends:
        copy.start()
    for m in range(micro_count):
        pool_back(m)
    if scatter:
        add_core(dwp, p_core, p_sends)
        for r in range(far_count):
            pool.send_x(r)
    product(dw2, hid, branch)
    for copy in q_sends:
        copy.start()
    if not scatter:
        dw2_copy().start()
    for m in range(micro_count):
        act_back(m)
    reduce.start(0)
    if scatter:
        pool.send_z(0)
    reduce.start(1)
    if scatter:
        add_core(dw2, q_core, q_sends)
        dw2_copy().start()
    reduce.start(2)
    if scatter:
        pool.send_z(1)
    reduce.start(3)
    reduce.wait(3)
    sum_out[...] = r_result[...]

    scale = 1.0 / total_rows

    def first_low(m, e, c, n, at):
        plain = r_result[3 * m : 3 * m + 1, n] * scale
        cross = r_result[3 * m + 1 : 3 * m + 2, n] * scale
        normed = (first[e, m, at, c] - vec_ref[m, 0:1, c]) * vec_ref[m, 1:2, c]
        grad = so[m, e, at, c] + vec_ref[m, 1:2, c] * vec_ref[m, 2:3, c] * (
            a2g[m, e, at, c] - plain - normed * cross
        )
        return grad.astype(BF16).astype(F32)

    edge_out[...] = jnp.zeros_like(edge_out)
    for q in range(2):
        c = slice(q * half, (q + 1) * half)
        n = pl.ds(pl.multiple_of(lax.rem(q + ch, 2) * half, 128), half)
        for m in range(micro_count):
            for e in range(2):
                row = 2 * m + e
                top = first_low(m, e, c, n, slice(0, 8))
                bottom = first_low(m, e, c, n, slice(pairs - 8, pairs))
                edge_out[0, row : row + 1, n] = top[0:1]
                edge_out[1, row : row + 1, n] = bottom[7:8]

    def edge_copy(side):
        return remote(
            edge_out.at[side], edge_in.at[1 - side], edge_send.at[side], edge_recv.at[1 - side], (left, right)[side]
        )

    for side in range(2):
        edge_copy(side).start()
    line = pos * 2 + ch
    edge_copy(1).wait_send()
    edge_copy(0).wait_send()
    for side in range(2):
        edge_copy(side).wait_recv()
    keep_before = jnp.where(line > 0, 1.0, 0.0)
    keep_after = jnp.where(line < 2 * pos_count - 1, 1.0, 0.0)
    slots = 2

    def gp_copies(slot, c):
        return [
            pltpu.make_async_copy(
                w2_ref.at[slot * micro_count * pairs : (slot + 1) * micro_count * pairs, d * tile : (d + 1) * tile],
                gp.at[d, :, c],
                gp_sem.at[slot, d],
            )
            for d in range(PIECES)
        ]

    extra[...] = jnp.zeros_like(extra)
    for j in range(tiles):
        c = columns(j)
        n = natural(j)
        slot = j % slots
        if j >= slots:
            for copy in gp_copies(slot, columns(j - slots)):
                copy.wait()
        for m in range(micro_count):
            total = 0.0
            for e in range(2):
                row = 2 * m + e
                low = first_low(m, e, c, n, slice(0, pairs))
                low32[e, 8 : 8 + pairs, :] = low
                low32[e, 7:8, :] = edge_in[0, row : row + 1, n] * keep_before
                low32[e, 8 + pairs : 9 + pairs, :] = edge_in[1, row : row + 1, n] * keep_after
                total += jnp.sum(low, axis=0, keepdims=True)
            extra[2 * micro_count + m : 2 * micro_count + m + 1, n] = total
            begin = slot * micro_count * pairs + m * pairs
            for d in range(PIECES):
                shift = 7 + d // 2
                w2_ref[begin : begin + pairs, d * tile : (d + 1) * tile] = low32[
                    d % 2, shift : shift + pairs, :
                ].astype(BF16)
        for copy in gp_copies(slot, c):
            copy.start()
        if scatter and j == 1:
            for r in range(2, far_count):
                pool.send_z(r)
    for j in range(tiles - slots, tiles):
        for copy in gp_copies(j % slots, columns(j)):
            copy.wait()
    if scatter:
        dwp_out[...] = pool.send_y()
    else:
        copy = pltpu.make_async_copy(dwp, dwp_out, misc_sem.at[3])
        copy.start()
        copy.wait()
    xa_local().wait()
    xa_remote().wait()
    for s in range(2):
        rim_up(s).wait_recv()
    rim_up(0).wait_send()
    rim_down(0).wait_send()
    for m in range(micro_count):
        pooled_local(m).wait()
        pooled_remote(m).wait()
    dw2_copy().wait()
    if scatter:
        dwp_out[...] += pool.finish()
        pool.drain()
        for copy in p_sends + q_sends:
            copy.wait_send()


def middle(first_own, first_other, weights, og, x, vecs, limits, total_rows):
    _, micro_count, pairs, half = first_own.shape
    wide = 2 * half
    rows = 2 * pairs
    depth = micro_count * pairs
    local_rows, local_in = x.shape[1:]
    far = lax.axis_size("pos") // 2
    block = wide // (4 * far)
    scatter = block % 16 == 0
    land = block if scatter else 16
    tile = 256
    any_space = pl.BlockSpec(memory_space=pl.ANY)
    in_vmem = pl.BlockSpec(memory_space=pltpu.VMEM)
    dma = pltpu.SemaphoreType.DMA
    return pl.pallas_call(
        functools.partial(middle_kernel, scatter, total_rows),
        out_shape=(
            jax.ShapeDtypeStruct((micro_count, rows, half), BF16),
            jax.ShapeDtypeStruct((PIECES, depth, wide), BF16),
            jax.ShapeDtypeStruct((micro_count, local_rows // 2 + 32, 2 * local_in), BF16),
            jax.ShapeDtypeStruct((2, far, block, wide) if scatter else (wide, wide), BF16),
            jax.ShapeDtypeStruct((block, half) if scatter else (wide, wide), F32 if scatter else BF16),
            jax.ShapeDtypeStruct((8, wide), F32),
            jax.ShapeDtypeStruct((8, wide), F32),
        ),
        in_specs=[any_space] * 8 + [in_vmem] * 2,
        out_specs=(any_space,) * 4 + (in_vmem if scatter else any_space, in_vmem, in_vmem),
        scratch_shapes=[
            pltpu.VMEM((wide, wide), BF16),
            pltpu.VMEM((wide, wide), BF16),
            pltpu.VMEM((2, micro_count, pairs, wide), F32),
            pltpu.VMEM((micro_count, 2, pairs, wide), F32),
            pltpu.VMEM((micro_count, 2, pairs, wide), F32),
            pltpu.VMEM((micro_count, rows, wide), BF16),
            pltpu.VMEM((micro_count, rows, wide), BF16),
            pltpu.VMEM((micro_count, pairs, wide), BF16),
            pltpu.VMEM((micro_count, pairs, wide), BF16),
            pltpu.VMEM((micro_count, pairs, wide), BF16),
            pltpu.VMEM((micro_count, pairs, wide), BF16),
            pltpu.VMEM((wide, wide), BF16),
            pltpu.VMEM((wide, wide), BF16),
            pltpu.VMEM((2, far, land, wide), BF16),
            pltpu.VMEM((2, far, land, wide), BF16),
            pltpu.VMEM((2, pairs + 16, tile), F32),
            pltpu.VMEM((2, 8, wide), F32),
            pltpu.VMEM((2, 8, wide), F32),
            dma((2, 2, 2)),
            dma((2,)),
            dma((4,)),
            dma((2, PIECES)),
            dma((micro_count,)),
            dma((micro_count,)),
            dma((micro_count,)),
            dma,
            dma,
            dma((2,)),
            dma((2,)),
            dma((2,)),
            dma((2,)),
            dma((2, far)),
            dma((2, far)),
            dma((2, far)),
            dma((2, far)),
        ]
        + Reduce.scratch(wide)
        + Scatter.scratch(land, wide),
        compiler_params=params(collective_id=7, has_side_effects=True),
        name="middle",
    )(first_own, first_other, *weights, og, x, vecs, limits)


def tail_kernel(
    scatter,
    total_rows,
    hp_own,
    hp_other,
    gp,
    wo,
    wx,
    xs_in,
    dw2,
    vec_ref,
    extra_ref,
    ig,
    dw_out,
    dw2_out,
    sum_out,
    g_buf,
    w_buf,
    a1g,
    xs,
    h_buf,
    f_buf,
    dw,
    core_in,
    x_in,
    z_in,
    dxs,
    weave,
    load_sem,
    w_sem,
    h_sem,
    low_send,
    low_recv,
    core_send,
    core_recv,
    x_send,
    x_recv,
    z_send,
    z_recv,
    ig_send,
    ig_recv,
    ig_sem,
    value,
    r_core,
    r_near,
    r_far,
    r_result,
    r_send,
    r_recv,
    k2_buf,
    x2_in,
    z2_in,
    y2_out,
    y2_in,
    *s_sems,
):
    reduce = Reduce(value, r_core, r_near, r_far, r_result, (r_send, r_recv))
    batch, pos, ch, core, z = reduce.batch, reduce.pos, reduce.ch, reduce.core, reduce.z
    far_count = reduce.far_count
    chunks, rows_all, chunk = dw.shape
    micro_count, half_rows, wide = dxs.shape
    pairs = half_rows // 2
    rows = micro_count * pairs
    out = gp.shape[2]
    local_out = out // 2
    local_in = wide // 2
    tile = w_buf.shape[2]
    cut = h_buf.shape[3]
    per_half = rows_all // 2 // cut
    y_peer = (batch, pos, 1 - ch)
    x_peer = (1 - batch, pos, ch)
    core_peer = reduce.core_peer

    def loads():
        copies = [
            pltpu.make_async_copy(gp, g_buf, load_sem.at[0]),
            pltpu.make_async_copy(xs_in, xs, load_sem.at[1]),
            pltpu.make_async_copy(gp.at[2:4, :, 0:local_out], f_buf.at[0:2], load_sem.at[2]),
        ]
        return copies

    def w_copies(j):
        s = j % 2
        at = slice(j * tile, (j + 1) * tile)
        return [
            pltpu.make_async_copy(wo.at[:, at, :], w_buf.at[s, :, :, 0:local_out], w_sem.at[s, 0]),
            pltpu.make_async_copy(wx.at[:, at, :], w_buf.at[s, :, :, local_out:out], w_sem.at[s, 1]),
        ]

    def h_copies(side_half, t):
        number = side_half * per_half + t
        k = number // 2
        at = pl.ds(pl.multiple_of(lax.rem(number, 2) * cut, cut), cut)
        slot = lax.rem(t, 2)
        return [
            pltpu.make_async_copy((hp_own, hp_other)[s].at[k + e, :, at], h_buf.at[slot, 2 * s + e], h_sem.at[slot, 2 * s + e])
            for s in range(2)
            for e in range(2)
        ]

    def low_copy(c):
        return pltpu.make_async_remote_copy(
            gp.at[2:4, :, local_out + c * chunk : local_out + (c + 1) * chunk],
            f_buf.at[2:4, :, c * chunk : (c + 1) * chunk],
            low_send.at[c],
            low_recv.at[c],
            device_id=y_peer,
            device_id_type=MESH,
        )

    second = Scatter(
        reduce,
        lambda zz: k2_buf.at[zz],
        lambda zz: dw2.at[1 - batch, zz],
        x2_in,
        z2_in,
        y2_out,
        y2_in,
        s_sems,
        round_steps(far_count),
    )

    def k2_copy():
        return pltpu.make_async_copy(dw2.at[batch], k2_buf, load_sem.at[4])

    for copy in loads():
        copy.start()
    for copy in w_copies(0):
        copy.start()
    if scatter:
        k2_copy().start()
    meet(reduce.peers())
    low_copy(0).start()
    if scatter:
        for r in range(far_count):
            second.send_x(r)
    for copy in h_copies(1 - batch, 0):
        copy.start()
    for copy in loads()[:2]:
        copy.wait()
    value[...] = extra_ref[...]

    tiles = wide // tile

    def back(j):
        s = j % 2
        if j + 1 < tiles:
            for copy in w_copies(j + 1):
                copy.start()
        for copy in w_copies(j):
            copy.wait()
        at = slice(j * tile, (j + 1) * tile)
        sums = [[0.0, 0.0] for _ in range(micro_count)]
        for e in range(2):
            acc = 0.0
            for k in range(KW):
                acc += lax.dot_general(
                    g_buf[e - k + KW - 1], w_buf[s, k], NT, preferred_element_type=F32
                )
            for m in range(micro_count):
                x = xs[e, m * pairs : (m + 1) * pairs, at].astype(F32)
                moved = x - vec_ref[m, 0:1, at]
                normed = moved * vec_ref[m, 3:4, at]
                act = moved * vec_ref[m, 1:2, at] + vec_ref[m, 2:3, at]
                grad = acc[m * pairs : (m + 1) * pairs] * gelu_slope(act)
                a1g[e, m * pairs : (m + 1) * pairs, at] = grad
                sums[m][0] += jnp.sum(grad, axis=0, keepdims=True)
                sums[m][1] += jnp.sum(grad * normed, axis=0, keepdims=True)
        for m in range(micro_count):
            for i in range(2):
                value[2 * m + i : 2 * m + i + 1, at] = sums[m][i]

    block = rows_all // (2 * 2 * far_count)

    def block_rows(side_half, zz, cc):
        return pl.ds(pl.multiple_of(((side_half * far_count + zz) * 2 + cc) * block, 16), block)

    def core_copy(c, kind, side_half, zz):
        return pltpu.make_async_remote_copy(
            dw.at[c, block_rows(side_half, zz, 1 - core)],
            core_in.at[c, kind, zz],
            core_send.at[c, kind, zz],
            core_recv.at[c, kind, zz],
            device_id=core_peer,
            device_id_type=MESH,
        )

    def x_copy(c, zz):
        return pltpu.make_async_remote_copy(
            dw.at[c, block_rows(1 - batch, zz, core)],
            x_in.at[c, zz],
            x_send.at[c, zz],
            x_recv.at[c, zz],
            device_id=x_peer,
            device_id_type=MESH,
        )

    def z_copy(c, r, zz):
        return pltpu.make_async_remote_copy(
            dw.at[c, block_rows(batch, zz, core)],
            z_in.at[c, r],
            z_send.at[c, r],
            z_recv.at[c, r],
            device_id=(batch, zz * 2 + core, ch),
            device_id_type=MESH,
        )

    steps = round_steps(far_count)

    def away(r):
        return lax.rem(z + steps[r], far_count)

    def weigh(c, kind, side_half, following):
        lanes = slice(c * chunk, (c + 1) * chunk)

        @pl.loop(0, per_half)
        def _(t):
            @pl.when(t + 1 < per_half)
            def _():
                for copy in h_copies(side_half, t + 1):
                    copy.start()

            for copy in h_copies(side_half, t):
                copy.wait()
            slot = lax.rem(t, 2)
            grad = lax.dot_general(
                h_buf[slot].reshape(4 * rows, cut),
                f_buf[:, :, lanes].reshape(4 * rows, chunk),
                TN,
                preferred_element_type=F32,
            )
            at = pl.multiple_of((side_half * per_half + t) * cut, 16)
            dw[c, pl.ds(at, cut), :] = grad.astype(BF16)

        if following is not None:
            for copy in h_copies(following, 0):
                copy.start()
        if scatter:
            for r in range(far_count):
                core_copy(c, kind, side_half, away(r)).start()

    def add_to(c, at, ref, *index):
        dw[c, at, :] = (dw[c, at, :].astype(F32) + ref[index].astype(F32)).astype(BF16)

    def send_x(c):
        if scatter:
            for r in range(far_count):
                zz = away(r)
                core_copy(c, 0, 1 - batch, zz).wait_recv()
                add_to(c, block_rows(1 - batch, zz, core), core_in, c, 0, zz)
                x_copy(c, zz).start()

    def send_z(c):
        if scatter:
            for r in range(far_count):
                zz = away(r)
                core_copy(c, 1, batch, zz).wait_recv()
                x_copy(c, zz).wait_recv()
                at = block_rows(batch, zz, core)
                total = dw[c, at, :].astype(F32) + core_in[c, 1, zz].astype(F32) + x_in[c, zz].astype(F32)
                lanes = slice(c * chunk, (c + 1) * chunk)
                if r < far_count - 1:
                    dw[c, at, :] = total.astype(BF16)
                    z_copy(c, r, zz).start()
                else:
                    dw_out[:, lanes] = total

    def finish(c):
        lanes = slice(c * chunk, (c + 1) * chunk)
        if scatter:
            for r in range(far_count - 1):
                z_copy(c, r, away(r)).wait_recv()
                dw_out[:, lanes] = dw_out[:, lanes] + z_in[c, r].astype(F32)
        else:
            copy = pltpu.make_async_copy(dw.at[c], dw_out.at[:, lanes], load_sem.at[3])
            copy.start()
            copy.wait()

    def ig_remote(m):
        at = pl.ds(pl.multiple_of(ch * half_rows, half_rows), half_rows)
        lanes = pl.ds(pl.multiple_of((1 - ch) * local_in, 128), local_in)
        return pltpu.make_async_remote_copy(
            dxs.at[m, :, lanes], ig.at[m, at], ig_send.at[m], ig_recv.at[m], device_id=y_peer, device_id_type=MESH
        )

    def ig_local(m):
        at = pl.ds(pl.multiple_of(ch * half_rows, half_rows), half_rows)
        lanes = pl.ds(pl.multiple_of(ch * local_in, 128), local_in)
        return pltpu.make_async_copy(dxs.at[m, :, lanes], ig.at[m, at], ig_sem.at[m])

    def input_grad(m):
        scale = 1.0 / total_rows

        @pl.loop(0, wide // 128)
        def _(b):
            at = pl.ds(pl.multiple_of(b * 128, 128), 128)
            plain = r_result[2 * m : 2 * m + 1, at] * scale
            cross = r_result[2 * m + 1 : 2 * m + 2, at] * scale
            inverse = vec_ref[m, 3:4, at]
            for e in range(2):
                x = xs[e, m * pairs : (m + 1) * pairs, at].astype(F32)
                normed = (x - vec_ref[m, 0:1, at]) * inverse
                grad = a1g[e, m * pairs : (m + 1) * pairs, at]
                weave[pl.ds(e, pairs, stride=2), :] = vec_ref[m, 1:2, at] * (grad - plain - normed * cross)
            dxs[m, :, at] = weave[...].astype(BF16)

        ig_local(m).start()
        ig_remote(m).start()

    for j in range(2):
        back(j)
    if scatter:
        k2_copy().wait()
        second.send_z(0)
    loads()[2].wait()
    low_copy(0).wait_recv()
    for c in range(1, chunks):
        low_copy(c).start()
    weigh(0, 0, 1 - batch, batch)
    send_x(0)
    if scatter:
        for r in range(1, far_count):
            second.send_z(r)
    for j in range(2, tiles):
        back(j)
    reduce.start(0)
    weigh(0, 1, batch, 1 - batch)
    reduce.start(1)
    low_copy(1).wait_recv()
    weigh(1, 0, 1 - batch, batch)
    send_x(1)
    reduce.start(2)
    if scatter:
        dw2_out[...] = second.send_y()
    send_z(0)
    weigh(1, 1, batch, 1 - batch)
    reduce.start(3)
    low_copy(2).wait_recv()
    weigh(2, 0, 1 - batch, batch)
    send_x(2)
    reduce.wait(3)
    sum_out[...] = r_result[...]
    for m in range(micro_count):
        input_grad(m)
    weigh(2, 1, batch, None)
    send_z(1)
    finish(0)
    send_z(2)
    finish(1)
    finish(2)
    for m in range(micro_count):
        ig_local(m).wait()
        ig_remote(m).wait()
    if scatter:
        dw2_out[...] += second.finish()
        second.drain()
    else:
        dw2_out[...] = jnp.zeros_like(dw2_out)
    for c in range(chunks):
        low_copy(c).wait_send()
        if scatter:
            for r in range(far_count):
                zz = away(r)
                core_copy(c, 0, 1 - batch, zz).wait_send()
                core_copy(c, 1, batch, zz).wait_send()
                x_copy(c, zz).wait_send()
                if r < far_count - 1:
                    z_copy(c, r, zz).wait_send()


def tail(pieces, other_pieces, grad_pieces, own, other, x_split, dw2, vecs, extra, total_rows):
    _, micro_count, pairs, wide = other_pieces.shape
    rows = micro_count * pairs
    out = grad_pieces.shape[-1]
    local_out = out // 2
    chunks = 3
    chunk = local_out // chunks
    far = lax.axis_size("pos") // 2
    rows_all = KW * wide
    block = rows_all // (4 * far)
    scatter = block % 16 == 0
    tile = 256
    land = block if scatter else 16
    block2 = dw2.shape[2] if scatter else 16
    any_space = pl.BlockSpec(memory_space=pl.ANY)
    in_vmem = pl.BlockSpec(memory_space=pltpu.VMEM)
    dma = pltpu.SemaphoreType.DMA
    return pl.pallas_call(
        functools.partial(tail_kernel, scatter, total_rows),
        out_shape=(
            jax.ShapeDtypeStruct((micro_count, 4 * pairs, wide // 2), BF16),
            jax.ShapeDtypeStruct((block, local_out) if scatter else (rows_all, local_out), F32 if scatter else BF16),
            jax.ShapeDtypeStruct((block2, local_out), F32),
            jax.ShapeDtypeStruct((8, out), F32),
        ),
        in_specs=[any_space] * 7 + [in_vmem] * 2,
        out_specs=(any_space, in_vmem if scatter else any_space, in_vmem, in_vmem),
        scratch_shapes=[
            pltpu.VMEM((PIECES, rows, out), BF16),
            pltpu.VMEM((2, KW, tile, out), BF16),
            pltpu.VMEM((2, rows, wide), F32),
            pltpu.VMEM((2, rows, wide), BF16),
            pltpu.VMEM((2, 4, rows, wide // 2), BF16),
            pltpu.VMEM((4, rows, local_out), BF16),
            pltpu.VMEM((chunks, rows_all, chunk), BF16),
            pltpu.VMEM((chunks, 2, far, land, chunk), BF16),
            pltpu.VMEM((chunks, far, land, chunk), BF16),
            pltpu.VMEM((chunks, far - 1, land, chunk), BF16),
            pltpu.VMEM((micro_count, 2 * pairs, wide), BF16),
            pltpu.VMEM((2 * pairs, 128), F32),
            dma((5,)),
            dma((2, 2)),
            dma((2, 4)),
            dma((chunks,)),
            dma((chunks,)),
            dma((chunks, 2, far)),
            dma((chunks, 2, far)),
            dma((chunks, far)),
            dma((chunks, far)),
            dma((chunks, far - 1)),
            dma((chunks, far - 1)),
            dma((micro_count,)),
            dma((micro_count,)),
            dma((micro_count,)),
        ]
        + Reduce.scratch(out)
        + [pltpu.VMEM((far, block2, out), BF16)]
        + Scatter.scratch(block2, out),
        compiler_params=params(collective_id=5, has_side_effects=True),
        name="tail",
    )(
        pieces,
        other_pieces.reshape(PIECES, rows, wide),
        grad_pieces,
        own.reshape(KW, wide, local_out),
        other.reshape(KW, wide, local_out),
        x_split,
        dw2,
        vecs,
        extra,
    )


def local(
    section_input,
    norm1_gain,
    norm1_bias,
    conv1_weight,
    conv1_bias,
    norm2_gain,
    norm2_bias,
    conv2_weight,
    conv2_bias,
    pool_weight,
    out_grad,
    clip_table,
    clip_index,
):
    micro_count, seq_count, local_rows, local_in = section_input.shape
    batch_count, pos_count, ch_count = (lax.axis_size(a) for a in ("batch", "pos", "ch"))
    batch, pos, ch = (lax.axis_index(a) for a in ("batch", "pos", "ch"))
    total_rows = seq_count * local_rows * batch_count * pos_count
    wide_in = 2 * local_in
    local_out = conv1_weight.shape[1]
    wide_out = 2 * local_out
    half = local_rows // 2
    pairs = half // 2
    plane = batch_count * pos_count
    spot = batch * pos_count + pos
    swap = [(0, 1), (1, 0)]
    is_low = ch == 0

    def other_ch(v):
        return lax.ppermute(v, "ch", swap)

    def natural(own, other, axis):
        return jnp.where(
            is_low,
            jnp.concatenate([own, other], axis=axis),
            jnp.concatenate([other, own], axis=axis),
        )

    x = section_input.reshape(micro_count, local_rows, local_in)

    def own_first(v):
        return jnp.where(
            is_low, v, jnp.concatenate([v[..., local_out:], v[..., :local_out]], axis=-1)
        )

    to_natural = own_first
    bins = local_rows // 2
    mine = bins // 2
    small = jnp.stack([conv1_bias, norm2_gain, norm2_bias, conv2_bias])
    small = jnp.concatenate(
        [small, jnp.pad(jnp.stack([norm1_gain, norm1_bias]), ((0, 2), (0, local_out - local_in)))]
    )
    (
        pieces,
        x_split,
        first_own,
        first_other,
        w1_other,
        w2_other,
        wp_other,
        og_full,
        vec1,
        vec2,
    ) = head(
        x,
        conv1_weight,
        conv2_weight,
        pool_weight,
        out_grad.reshape(micro_count, bins, local_out),
        small,
        total_rows,
    )
    first_own = first_own.reshape(2, micro_count, pairs, local_out)
    first_other = first_other.reshape(2, micro_count, pairs, local_out)
    table_pos = jnp.arange(clip_table.shape[0], dtype=jnp.int32)
    limit = jnp.sum(jnp.where(table_pos[None] == clip_index[:, None], clip_table[None], 0.0), axis=1)
    limits = jnp.broadcast_to(limit[:, None, None], (micro_count, 8, 128))

    section_output, grad_pieces, x_away, dw2, dwp, sums3, extra = middle(
        first_own,
        first_other,
        (conv2_weight, w2_other, pool_weight, wp_other),
        og_full,
        x,
        vec2,
        limits,
        total_rows,
    )
    section_output = section_output.reshape(micro_count, seq_count, bins, local_out)
    sums3 = sums3[: 3 * micro_count].reshape(micro_count, 3, wide_out)
    who = jnp.stack([pos * local_rows + (1 - ch) * half - 16, pos_count * local_rows]).astype(jnp.int32)
    other_pieces = make_hidden(who, x_away, vec1, half)
    whole_two = dw2
    input_grad, dw1, dw2, part = tail(
        pieces, other_pieces, grad_pieces, conv1_weight, w1_other, x_split, dw2, vec1, extra, total_rows
    )
    input_grad = input_grad.reshape(section_input.shape)

    def scatter(v):
        return lax.psum_scatter(v, ("batch", "pos"), scatter_dimension=0, tiled=True).astype(F32)

    def fold(v):
        v = jnp.where(is_low, v, jnp.concatenate([v[local_out:], v[:local_out]], axis=0))
        away = other_ch(v[:, local_out:])
        return scatter((v[:, :local_out].astype(F32) + away.astype(F32)).astype(BF16))

    if dwp.shape[0] == wide_out:
        dw2, dwp = fold(whole_two), fold(dwp)
    one = part[: 2 * micro_count, :wide_in]
    grad_sum, cross_sum = one[0::2], one[1::2]
    low_sum = part[2 * micro_count : 3 * micro_count]
    if dw1.shape[0] != KW * wide_in // plane:
        dw1 = scatter(dw1)

    def mine_of(v, width):
        return lax.dynamic_slice_in_dim(v, ch * width, width, axis=0)

    return (
        section_output,
        input_grad,
        mine_of(jnp.sum(cross_sum, axis=0), local_in),
        mine_of(jnp.sum(grad_sum, axis=0), local_in),
        dw1,
        mine_of(jnp.sum(low_sum, axis=0), local_out),
        mine_of(jnp.sum(sums3[:, 1], axis=0), local_out),
        mine_of(jnp.sum(sums3[:, 0], axis=0), local_out),
        dw2,
        mine_of(jnp.sum(sums3[:, 2], axis=0), local_out),
        dwp,
    )


def solution(mesh):
    placed = (
        P(None, "batch", "pos", "ch"),
        P("ch"),
        P("ch"),
        P(None, "ch"),
        P("ch"),
        P("ch"),
        P("ch"),
        P(None, "ch"),
        P("ch"),
        P(None, "ch"),
        P(None, "batch", "pos", "ch"),
        P(),
        P(),
    )
    return jax.shard_map(
        local,
        mesh=mesh,
        in_specs=placed,
        out_specs=(
            P(None, "batch", "pos", "ch"),
            P(None, "batch", "pos", "ch"),
            P("ch"),
            P("ch"),
            P(("batch", "pos"), "ch"),
            P("ch"),
            P("ch"),
            P("ch"),
            P(("batch", "pos"), "ch"),
            P("ch"),
            P(("batch", "pos"), "ch"),
        ),
        check_vma=False,
    )
```

```python
import functools

import jax
import jax.numpy as jnp
from jax import lax
from jax.experimental import pallas as pl
from jax.experimental.pallas import tpu as pltpu
from jax.sharding import PartitionSpec as P

KW = 5
RIM = KW // 2
PIECES = KW + 1
EPS = 1e-05
MESH = pl.DeviceIdType.MESH
C0 = 0.7978845608028654
C1 = 0.044715
F32 = jnp.float32
BF16 = jnp.bfloat16
VMEM_LIMIT = 60 * 1024 * 1024

NT = (((1,), (1,)), ((), ()))
TN = (((0,), (0,)), ((), ()))


def params(**kw):
    return pltpu.CompilerParams(vmem_limit_bytes=VMEM_LIMIT, **kw)


def gelu(u):
    return 0.5 * u * (1.0 + jnp.tanh(C0 * (u + C1 * u * u * u)))


def gelu_slope(u):
    square = u * u
    t = jnp.tanh(C0 * (u + C1 * square * u))
    return 0.5 * (1.0 + t) + 0.5 * u * (1.0 - t * t) * (C0 + (3.0 * C0 * C1) * square)


class Reduce:
    def __init__(self, value, core_in, near, far, result, sems):
        self.value, self.core_in, self.near, self.far, self.result = value, core_in, near, far, result
        self.send, self.recv = sems
        self.batch, self.pos, self.ch = (lax.axis_index(a) for a in ("batch", "pos", "ch"))
        self.core = lax.rem(self.pos, 2)
        self.z = self.pos // 2
        self.far_count = lax.axis_size("pos") // 2
        half = value.shape[1] // 2
        self.mine = pl.ds(pl.multiple_of(self.core * half, half), half)
        self.away = pl.ds(pl.multiple_of((1 - self.core) * half, half), half)
        self.me = self.batch * 2 + self.ch
        self.core_peer = (self.batch, self.z * 2 + 1 - self.core, self.ch)
        self.near_peers = []
        for step in range(1, 4):
            other = lax.rem(self.me + step, 4)
            self.near_peers.append((other // 2, self.pos, lax.rem(other, 2)))
        self.far_peers = []
        for step in range(1, self.far_count):
            other = lax.rem(self.z + step, self.far_count)
            self.far_peers.append((self.batch, other * 2 + self.core, self.ch))

    @staticmethod
    def scratch(width):
        far = lax.axis_size("pos") // 2
        count = 2 + 3 + far - 1
        return [
            pltpu.VMEM((8, width), F32),
            pltpu.VMEM((8, width // 2), F32),
            pltpu.VMEM((4, 8, width // 2), F32),
            pltpu.VMEM((far, 8, width // 2), F32),
            pltpu.VMEM((8, width), F32),
            pltpu.SemaphoreType.DMA((count,)),
            pltpu.SemaphoreType.DMA((count,)),
        ]

    def peers(self):
        return [self.core_peer] + self.near_peers + self.far_peers

    def copy(self, i, src, dst, peer):
        return pltpu.make_async_remote_copy(
            src, dst, self.send.at[i], self.recv.at[i], device_id=peer, device_id_type=MESH
        )

    def copies(self, stage):
        if stage == 0:
            return [self.copy(0, self.value.at[:, self.away], self.core_in, self.core_peer)]
        if stage == 1:
            slot = self.near.at[self.me]
            return [self.copy(1 + i, slot, slot, p) for i, p in enumerate(self.near_peers)]
        if stage == 2:
            slot = self.far.at[self.z]
            return [self.copy(4 + i, slot, slot, p) for i, p in enumerate(self.far_peers)]
        part = self.result.at[:, self.mine]
        return [self.copy(3 + self.far_count, part, part, self.core_peer)]

    def wait(self, stage):
        for copy in self.copies(stage):
            copy.wait()

    def start(self, stage):
        if stage == 1:
            self.wait(0)
            self.near[pl.ds(self.me, 1)] = (self.value[:, self.mine] + self.core_in[...])[None]
        if stage == 2:
            self.wait(1)
            total = (self.near[0] + self.near[1]) + (self.near[2] + self.near[3])
            self.far[pl.ds(self.z, 1)] = total[None]
        if stage == 3:
            self.wait(2)
            total = self.far[0]
            for i in range(1, self.far_count):
                total = total + self.far[i]
            self.result[:, self.mine] = total
        for copy in self.copies(stage):
            copy.start()


def meet(peers):
    barrier = pltpu.get_barrier_semaphore()
    for peer in peers:
        pl.semaphore_signal(barrier, inc=1, device_id=peer, device_id_type=MESH)
    pl.semaphore_wait(barrier, len(peers))


def reduce_kernel(v_ref, o_ref, *scratch):
    value, core_in, near, far, result, send, recv = scratch
    reduce = Reduce(value, core_in, near, far, result, (send, recv))
    value[...] = v_ref[...]
    meet(reduce.peers())
    for stage in range(4):
        reduce.start(stage)
    reduce.wait(3)
    o_ref[...] = result[...]


def reduce_all(values, collective_id):
    rows, width = values.shape
    total = pl.pallas_call(
        reduce_kernel,
        out_shape=jax.ShapeDtypeStruct((8, width), F32),
        in_specs=[pl.BlockSpec(memory_space=pltpu.VMEM)],
        out_specs=pl.BlockSpec(memory_space=pltpu.VMEM),
        scratch_shapes=Reduce.scratch(width),
        compiler_params=params(collective_id=collective_id, has_side_effects=True),
        name="reduce",
    )(jnp.pad(values, ((0, 8 - rows), (0, 0))))
    return total[:rows]


def head_kernel(
    total_rows,
    x,
    w1,
    w2,
    wp,
    og,
    small_ref,
    hp,
    xs_out,
    f_own,
    f_other,
    w1x,
    w2x,
    wpx,
    ogx,
    vec1,
    vec2,
    small_x,
    x_loc,
    x_ext,
    scr,
    raw,
    h_cat,
    xs,
    w_buf,
    f_buf,
    load_sem,
    w_sem,
    f_sem,
    out_sem,
    in_send,
    in_recv,
    halo_send,
    halo_recv,
    y1_send,
    y1_recv,
    z1_send,
    z1_recv,
    x1_send,
    x1_recv,
    c1_send,
    c1_recv,
    y2_send,
    y2_recv,
    c2_send,
    c2_recv,
    og_send,
    og_recv,
    small_send,
    small_recv,
    value,
    r_core,
    r_near,
    r_far,
    r_result,
    r_send,
    r_recv,
    value2,
    s_core,
    s_near,
    s_far,
    s_result,
    s_send,
    s_recv,
):
    first = Reduce(value, r_core, r_near, r_far, r_result, (r_send, r_recv))
    second = Reduce(value2, s_core, s_near, s_far, s_result, (s_send, s_recv))
    batch, pos, ch, core, z = first.batch, first.pos, first.ch, first.core, first.z
    far_count = first.far_count
    pos_count = 2 * far_count
    plane = 2 * pos_count
    micro_count, local_rows, local_in = x.shape
    wide = 2 * local_in
    half = local_rows // 2
    pairs = half // 2
    rows = micro_count * pairs
    ext = half + 32
    main = half + 16
    local_out = w1.shape[1]
    parts, chunk = w_buf.shape[0], w_buf.shape[2]
    lanes_count = wide // 128
    y_peer = (batch, pos, 1 - ch)
    x_peer = (1 - batch, pos, ch)
    up_pos = lax.rem(pos + 1, pos_count)
    down_pos = lax.rem(pos + pos_count - 1, pos_count)

    def remote(src, dst, send, recv, peer):
        return pltpu.make_async_remote_copy(src, dst, send, recv, device_id=peer, device_id_type=MESH)

    my_lanes = pl.ds(pl.multiple_of(ch * local_in, 128), local_in)

    def own_input():
        begin = pl.multiple_of(ch * (half - 16), 16)
        return pltpu.make_async_copy(
            x.at[:, pl.ds(begin, main), :],
            x_ext.at[:, pl.ds(pl.multiple_of(16 - 16 * ch, 16), main), my_lanes],
            load_sem.at[0],
        )

    def main_input():
        begin = pl.multiple_of((1 - ch) * (half - 16), 16)
        return remote(
            x.at[:, pl.ds(begin, main), :],
            x_ext.at[:, pl.ds(pl.multiple_of(16 * ch, 16), main), my_lanes],
            in_send,
            in_recv,
            y_peer,
        )

    def halo_up(s):
        return remote(
            x.at[:, local_rows - 16 : local_rows, :],
            x_ext.at[:, 0:16, my_lanes],
            halo_send.at[0],
            halo_recv.at[s],
            (batch, up_pos, 0),
        )

    def halo_down(s):
        return remote(
            x.at[:, 0:16, :],
            x_ext.at[:, ext - 16 : ext, my_lanes],
            halo_send.at[1],
            halo_recv.at[s],
            (batch, down_pos, 1),
        )

    def piece_rows(count):
        return -(-(count // plane) // 16) * 16

    def piece_at(count, bb, zz, cc):
        size = piece_rows(count)
        start = ((bb * far_count + zz) * 2 + cc) * size
        if size * plane != count:
            start = jnp.minimum(start, count - size)
        return pl.ds(pl.multiple_of(start, 16), size)

    class Fetch:
        def __init__(self, number, src, dst, lanes):
            self.number, self.src, self.dst, self.lanes = number, src, dst, lanes
            self.count = src.shape[0]

        def at(self, ref, bb, zz, cc):
            return ref.at[piece_at(self.count, bb, zz, cc), self.lanes]

        def over_y(self):
            return remote(
                self.at(self.src, batch, z, core),
                self.at(self.dst, batch, z, core),
                y1_send.at[self.number],
                y1_recv.at[self.number],
                y_peer,
            )

        def over_z(self, r):
            there = lax.rem(z + order[r], far_count)
            part = self.at(self.dst, batch, z, core)
            return remote(
                part, part, z1_send.at[self.number, r], z1_recv.at[self.number, r], (batch, there * 2 + core, ch)
            )

        def source(self, r):
            if r == 0:
                return z
            return lax.rem(z + far_count - order[r - 1], far_count)

        def over_x(self, r):
            part = self.at(self.dst, batch, self.source(r), core)
            return remote(part, part, x1_send.at[self.number, r], x1_recv.at[self.number, r], x_peer)

        def over_core(self, r, bb):
            part = self.at(self.dst, batch if bb == 0 else 1 - batch, self.source(r), core)
            return remote(
                part, part, c1_send.at[self.number, bb, r], c1_recv.at[self.number, bb, r], first.core_peer
            )

        def begin(self):
            self.over_x(0).start()
            for r in range(min(2, far_count - 1)):
                self.over_z(r).start()
            self.over_core(0, 0).start()

        def step(self, r):
            self.over_z(r).wait_recv()
            if r + 2 < far_count - 1:
                self.over_z(r + 2).start()
            self.over_x(r + 1).start()
            self.over_core(r + 1, 0).start()

        def end(self):
            for r in range(far_count):
                self.over_x(r).wait_recv()
                self.over_core(r, 1).start()

        def done(self):
            for r in range(far_count):
                for bb in range(2):
                    self.over_core(r, bb).wait_recv()

        def drain(self):
            self.over_y().wait_send()
            for r in range(far_count - 1):
                self.over_z(r).wait_send()
            for r in range(far_count):
                self.over_x(r).wait_send()
                for bb in range(2):
                    self.over_core(r, bb).wait_send()

    order = [1, 3, 2] if far_count == 4 else list(range(1, far_count))
    fetch1 = [
        Fetch(c, w1, w1x, slice(c * chunk, (c + 1) * chunk)) for c in range(local_out // chunk)
    ]
    fetch_p = Fetch(len(fetch1), wp, wpx, slice(0, local_out))

    half2 = w2.shape[0] // 2
    part2 = pl.ds(pl.multiple_of(core * half2, 16), half2)

    def second_y():
        return remote(w2.at[part2], w2x.at[part2], y2_send, y2_recv, y_peer)

    def second_core():
        return remote(w2x.at[part2], w2x.at[part2], c2_send, c2_recv, first.core_peer)

    bins = og.shape[1] // 2

    def og_local():
        at = pl.ds(pl.multiple_of(ch * bins, 16), bins)
        return pltpu.make_async_copy(og.at[:, at, :], ogx.at[:, :, 0:local_out], load_sem.at[1])

    def og_remote():
        at = pl.ds(pl.multiple_of((1 - ch) * bins, 16), bins)
        return remote(og.at[:, at, :], ogx.at[:, :, local_out : 2 * local_out], og_send, og_recv, y_peer)

    def small_copy():
        return remote(small_ref, small_x, small_send, small_recv, y_peer)

    def x_load():
        return pltpu.make_async_copy(x, x_loc, load_sem.at[2])

    tiles = local_out // chunk

    def w_load(i):
        src = w1 if i < tiles else w1x
        c = i % tiles
        return pltpu.make_async_copy(
            src.at[:, c * chunk : (c + 1) * chunk], w_buf.at[i % parts], w_sem.at[i % parts]
        )

    x_load().start()
    own_input().start()
    og_local().start()
    w_load(0).start()
    w_load(1).start()
    meet_peers = first.peers() + [
        (batch, lax.rem(pos + pos_count + 2 * ch - 1, pos_count), 0),
        (batch, lax.rem(pos + pos_count + 2 * ch - 1, pos_count), 1),
    ]
    meet(meet_peers)
    small_copy().start()
    fetch1[0].over_y().start()
    halo_up(ch).start()
    halo_down(ch).start()

    value[...] = jnp.zeros_like(value)
    x_load().wait()
    for m in range(micro_count):

        def add(i, sums):
            part = x_loc[m, pl.ds(pl.multiple_of(i * 64, 64), 64), :].astype(F32).reshape(8, 8, local_in)
            return sums[0] + jnp.sum(part, axis=0), sums[1] + jnp.sum(part * part, axis=0)

        zero = jnp.zeros((8, local_in), F32)
        plain, square = lax.fori_loop(0, local_rows // 64, add, (zero, zero))
        value[2 * m : 2 * m + 1, my_lanes] = jnp.sum(plain, axis=0, keepdims=True)
        value[2 * m + 1 : 2 * m + 2, my_lanes] = jnp.sum(square, axis=0, keepdims=True)
    first.start(0)
    first.start(1)
    fetch1[0].over_y().wait_recv()
    fetch1[0].begin()
    fetch1[1].over_y().start()
    first.start(2)
    fetch1[0].step(0)
    fetch1[1].over_y().wait_recv()
    main_input().start()
    first.start(3)
    for r in range(1, far_count - 2):
        fetch1[0].step(r)
    fetch1[1].begin()
    small_copy().wait_recv()
    first.wait(3)
    scale = 1.0 / total_rows
    for m in range(micro_count):
        center = r_result[2 * m : 2 * m + 1, :] * scale
        square = r_result[2 * m + 1 : 2 * m + 2, :] * scale
        inverse = lax.rsqrt(square - center * center + EPS)
        vec1[m, 0:1, :] = center
        vec1[m, 3:4, :] = inverse
        for source, lanes in ((small_ref, ch), (small_x, 1 - ch)):
            at = pl.ds(pl.multiple_of(lanes * local_in, 128), local_in)
            vec1[m, 1:2, at] = vec1[m, 3:4, at] * source[4:5, 0:local_in]
            vec1[m, 2:3, at] = source[5:6, 0:local_in]
        vec1[m, 4:8, :] = jnp.zeros((4, wide), F32)

    fetch1[0].step(far_count - 2)
    main_input().wait_recv()
    own_input().wait()
    for s in range(2):
        halo_up(s).wait_recv()
    fetch_p.over_y().start()
    second_y().start()
    for r in range(far_count - 3):
        fetch1[1].step(r)

    begin = pos * local_rows + ch * half - 16
    for m in range(micro_count):
        if m == 1:
            fetch1[1].step(far_count - 3)

        @pl.loop(0, ext // 16)
        def _(i):
            at = pl.multiple_of(i * 16, 16)
            v = x_ext[m, pl.ds(at, 16), :].astype(F32)
            act = (v - vec1[m, 0:1, :]) * vec1[m, 1:2, :] + vec1[m, 2:3, :]
            row = begin + at + lax.broadcasted_iota(jnp.int32, v.shape, 0)
            inside = jnp.logical_and(row >= 0, row < pos_count * local_rows)
            hidden = jnp.where(inside, gelu(act), 0.0)
            for b in range(lanes_count):
                scr[b, pl.ds(at, 16), :] = hidden[:, b * 128 : (b + 1) * 128]
                raw[b, pl.ds(at, 16), :] = v[:, b * 128 : (b + 1) * 128]

        @pl.loop(0, pairs // 16)
        def _(i):
            at = pl.multiple_of(i * 16, 16)
            to = pl.ds(pl.multiple_of(m * pairs + at, 16), 16)
            for b in range(lanes_count):
                for d in range(PIECES):
                    h_cat[to, d * wide + b * 128 : d * wide + (b + 1) * 128] = scr[
                        b, pl.ds(16 - RIM + d + 2 * at, 16, stride=2), :
                    ].astype(BF16)
                for e in range(2):
                    xs[e, to, b * 128 : (b + 1) * 128] = raw[
                        b, pl.ds(16 + e + 2 * at, 16, stride=2), :
                    ].astype(BF16)

    def pieces_out():
        copies = [
            pltpu.make_async_copy(h_cat.at[:, d * wide : (d + 1) * wide], hp.at[d], out_sem.at[d])
            for d in range(PIECES)
        ]
        return copies + [pltpu.make_async_copy(xs, xs_out, out_sem.at[PIECES])]

    for copy in pieces_out():
        copy.start()

    def f_copy(i):
        dst = f_own if i < tiles else f_other
        c = i % tiles
        return pltpu.make_async_copy(
            f_buf.at[i % 2], dst.at[:, :, c * chunk : (c + 1) * chunk], f_sem.at[i % 2]
        )

    value2[...] = jnp.zeros_like(value2)

    def conv(i):
        w_load(i).wait()
        if i >= 2:
            f_copy(i - 2).wait()
        c = i % tiles
        source, side = (small_ref, ch) if i < tiles else (small_x, 1 - ch)
        bias = source[0:1, c * chunk : (c + 1) * chunk]
        at = pl.ds(pl.multiple_of(side * local_out + c * chunk, 128), chunk)
        sums = [[0.0, 0.0] for _ in range(micro_count)]
        for e in range(2):
            acc = jnp.dot(
                h_cat[:, e * wide : (e + KW) * wide], w_buf[i % parts], preferred_element_type=F32
            )
            acc += bias
            f_buf[i % 2, e] = acc
            for m in range(micro_count):
                part = acc[m * pairs : (m + 1) * pairs]
                sums[m][0] += jnp.sum(part, axis=0, keepdims=True)
                sums[m][1] += jnp.sum(part * part, axis=0, keepdims=True)
        for m in range(micro_count):
            for k in range(2):
                value2[2 * m + k : 2 * m + k + 1, at] = sums[m][k]
        f_copy(i).start()

    fetch1[0].end()
    conv(0)
    fetch1[0].done()
    w_load(2).start()
    conv(1)
    og_remote().start()
    fetch1[1].step(far_count - 2)
    fetch_p.over_y().wait_recv()
    fetch_p.begin()
    conv(2)
    fetch1[1].end()
    fetch1[1].done()
    w_load(3).start()
    for r in range(far_count - 3):
        fetch_p.step(r)
    conv(3)
    second.start(0)
    fetch_p.step(far_count - 3)
    second.start(1)
    fetch_p.step(far_count - 2)
    second.start(2)
    second_y().wait_recv()
    second_core().start()
    fetch_p.end()
    second.start(3)
    for copy in pieces_out():
        copy.wait()
    fetch_p.done()
    second_core().wait()
    og_local().wait()
    og_remote().wait()
    for f in fetch1 + [fetch_p]:
        f.drain()
    second_y().wait_send()
    main_input().wait_send()
    halo_up(0).wait_send()
    halo_down(0).wait_send()
    small_copy().wait_send()
    f_copy(2).wait()
    f_copy(3).wait()
    second.wait(3)
    for m in range(micro_count):
        for q, (source, side) in enumerate(((small_ref, ch), (small_x, 1 - ch))):
            at = pl.ds(pl.multiple_of(side * local_out, 128), local_out)
            to = slice(q * local_out, (q + 1) * local_out)
            center = s_result[2 * m : 2 * m + 1, at] * scale
            square = s_result[2 * m + 1 : 2 * m + 2, at] * scale
            vec2[m, 0:1, to] = center
            vec2[m, 1:2, to] = lax.rsqrt(square - center * center + EPS)
            vec2[m, 2:5, to] = source[1:4, :]
            vec2[m, 5:8, to] = jnp.zeros((3, local_out), F32)


def head(x, w1, w2, wp, og, small, total_rows):
    micro_count, local_rows, local_in = x.shape
    wide = 2 * local_in
    half = local_rows // 2
    pairs = half // 2
    rows = micro_count * pairs
    ext = half + 32
    local_out = w1.shape[1]
    out = 2 * local_out
    chunk = local_out // 2
    far = lax.axis_size("pos") // 2
    any_space = pl.BlockSpec(memory_space=pl.ANY)
    in_vmem = pl.BlockSpec(memory_space=pltpu.VMEM)
    dma = pltpu.SemaphoreType.DMA
    fetches = local_out // chunk + 1
    return pl.pallas_call(
        functools.partial(head_kernel, total_rows),
        out_shape=(
            jax.ShapeDtypeStruct((PIECES, rows, wide), BF16),
            jax.ShapeDtypeStruct((2, rows, wide), BF16),
            jax.ShapeDtypeStruct((2, rows, local_out), F32),
            jax.ShapeDtypeStruct((2, rows, local_out), F32),
            jax.ShapeDtypeStruct(w1.shape, BF16),
            jax.ShapeDtypeStruct(w2.shape, BF16),
            jax.ShapeDtypeStruct(wp.shape, BF16),
            jax.ShapeDtypeStruct((micro_count, og.shape[1] // 2, out), BF16),
            jax.ShapeDtypeStruct((micro_count, 8, wide), F32),
            jax.ShapeDtypeStruct((micro_count, 8, out), F32),
        ),
        in_specs=[any_space] * 5 + [in_vmem],
        out_specs=(any_space,) * 8 + (in_vmem,) * 2,
        scratch_shapes=[
            pltpu.VMEM((8, local_out), F32),
            pltpu.VMEM((micro_count, local_rows, local_in), BF16),
            pltpu.VMEM((micro_count, ext, wide), BF16),
            pltpu.VMEM((wide // 128, ext, 128), F32),
            pltpu.VMEM((wide // 128, ext, 128), F32),
            pltpu.VMEM((rows, PIECES * wide), BF16),
            pltpu.VMEM((2, rows, wide), BF16),
            pltpu.VMEM((2, KW * wide, chunk), BF16),
            pltpu.VMEM((2, 2, rows, chunk), F32),
            dma((3,)),
            dma((2,)),
            dma((2,)),
            dma((PIECES + 1,)),
            dma,
            dma,
            dma((2,)),
            dma((2,)),
            dma((fetches,)),
            dma((fetches,)),
            dma((fetches, far - 1)),
            dma((fetches, far - 1)),
            dma((fetches, far)),
            dma((fetches, far)),
            dma((fetches, 2, far)),
            dma((fetches, 2, far)),
            dma,
            dma,
            dma,
            dma,
            dma,
            dma,
            dma,
            dma,
        ]
        + Reduce.scratch(wide)
        + Reduce.scratch(out),
        compiler_params=params(collective_id=6, has_side_effects=True),
        name="head",
    )(x, w1, w2, wp, og, small)


class Scatter:
    def __init__(self, reduce, kept, sent, x_in, z_in, y_out, y_in, sems, steps):
        self.reduce, self.kept, self.sent = reduce, kept, sent
        self.x_in, self.z_in, self.y_out, self.y_in = x_in, z_in, y_out, y_in
        self.z_send, self.z_recv, self.y_send, self.y_recv, *self.x_sems = sems
        self.steps = steps
        self.count = reduce.far_count
        self.half = y_in.shape[1]

    @staticmethod
    def scratch(block, width):
        far = lax.axis_size("pos") // 2
        dma = pltpu.SemaphoreType.DMA
        return [
            pltpu.VMEM((far, block, width), BF16),
            pltpu.VMEM((far - 1, block, width), BF16),
            pltpu.VMEM((block, width // 2), BF16),
            pltpu.VMEM((block, width // 2), BF16),
            dma((far - 1,)),
            dma((far - 1,)),
            dma,
            dma,
        ]

    def away(self, r):
        return lax.rem(self.reduce.z + self.steps[r], self.count)

    def copy(self, src, dst, send, recv, peer):
        return pltpu.make_async_remote_copy(src, dst, send, recv, device_id=peer, device_id_type=MESH)

    def over_x(self, r):
        zz, me = self.away(r), self.reduce
        peer = (1 - me.batch, me.pos, me.ch)
        return self.copy(self.sent(zz), self.x_in.at[zz], self.x_sems[0].at[zz], self.x_sems[1].at[zz], peer)

    def over_z(self, r):
        zz, me = self.away(r), self.reduce
        peer = (me.batch, zz * 2 + me.core, me.ch)
        return self.copy(self.x_in.at[zz], self.z_in.at[r], self.z_send.at[r], self.z_recv.at[r], peer)

    def over_y(self):
        me = self.reduce
        return self.copy(self.y_out, self.y_in, self.y_send, self.y_recv, (me.batch, me.pos, 1 - me.ch))

    def send_x(self, r):
        self.over_x(r).start()

    def send_z(self, r):
        zz = self.away(r)
        if self.x_sems:
            self.over_x(r).wait_recv()
            self.x_in[zz] = (self.x_in[zz].astype(F32) + self.kept(zz)[...].astype(F32)).astype(BF16)
        if r < self.count - 1:
            self.over_z(r).start()

    def send_y(self):
        zz = self.away(self.count - 1)
        total = self.x_in[zz].astype(F32)
        for r in range(self.count - 1):
            self.over_z(r).wait_recv()
            total = total + self.z_in[r].astype(F32)
        self.y_out[...] = total[:, self.half :].astype(BF16)
        self.over_y().start()
        return total[:, : self.half]

    def finish(self):
        self.over_y().wait_recv()
        return self.y_in[...].astype(F32)

    def drain(self):
        for r in range(self.count):
            if self.x_sems:
                self.over_x(r).wait_send()
            if r < self.count - 1:
                self.over_z(r).wait_send()
        self.over_y().wait_send()


def round_steps(far_count):
    if far_count == 4:
        return [2, 1, 3, 0]
    return list(range(far_count // 2, far_count)) + list(range(1, far_count // 2)) + [0]


def middle_kernel(
    scatter,
    total_rows,
    f_own,
    f_other,
    w2_own,
    w2_other,
    wp_own,
    wp_other,
    ogx,
    x,
    vec_ref,
    vec1_ref,
    lim_ref,
    pooled_out,
    gp,
    xa,
    h_other,
    dw2_out,
    dwp_out,
    sum_out,
    extra,
    w2_ref,
    wp_ref,
    first,
    so,
    a2g,
    hid,
    branch,
    diff,
    lg,
    og,
    pooled,
    dwp,
    dw2,
    p_core,
    q_core,
    low32,
    edge_out,
    edge_in,
    h_in,
    h_wide,
    h_stage,
    h_in_sem,
    h_out_sem,
    w_sem,
    f_sem,
    misc_sem,
    gp_sem,
    pooled_sem,
    pooled_send,
    pooled_recv,
    xa_send,
    xa_recv,
    rim_send,
    rim_recv,
    edge_send,
    edge_recv,
    pc_send,
    pc_recv,
    qc_send,
    qc_recv,
    value,
    r_core,
    r_near,
    r_far,
    r_result,
    r_send,
    r_recv,
    x_in,
    x_send,
    x_recv,
):
    reduce = Reduce(value, r_core, r_near, r_far, r_result, (r_send, r_recv))
    batch, pos, ch, core, z = reduce.batch, reduce.pos, reduce.ch, reduce.core, reduce.z
    far_count = reduce.far_count
    pos_count = 2 * far_count
    _, micro_count, pairs, wide = first.shape
    rows = 2 * pairs
    half = wide // 2
    tile = 256
    tiles = wide // tile
    y_peer = (batch, pos, 1 - ch)
    local_rows, local_in = x.shape[1:]
    half_rows = local_rows // 2
    ext = xa.shape[1]
    main = half_rows + 16

    def columns(j):
        return pl.ds(pl.multiple_of(j * tile, tile), tile)

    def natural(j):
        at = lax.rem(j * tile + ch * half, wide)
        return pl.ds(pl.multiple_of(at, tile), tile)

    def remote(src, dst, send, recv, peer):
        return pltpu.make_async_remote_copy(src, dst, send, recv, device_id=peer, device_id_type=MESH)

    def w_copies(kind):
        copies = []
        dst = (w2_ref, wp_ref)[kind]
        for q, src in enumerate(((w2_own, w2_other), (wp_own, wp_other))[kind]):
            for r in range(2):
                at = pl.ds(pl.multiple_of(lax.rem(ch + r, 2) * half, 16), half)
                copies.append(
                    pltpu.make_async_copy(
                        src.at[at, :],
                        dst.at[r * half : (r + 1) * half, q * half : (q + 1) * half],
                        w_sem.at[kind, q, r],
                    )
                )
        return copies

    def f_copies():
        return [
            pltpu.make_async_copy(src, first.at[:, :, :, q * half : (q + 1) * half], f_sem.at[q])
            for q, src in enumerate((f_own, f_other))
        ]

    def og_copy():
        return pltpu.make_async_copy(ogx, og, misc_sem.at[0])

    lanes_in = pl.ds(pl.multiple_of(ch * local_in, 128), local_in)

    def xa_local():
        begin = pl.multiple_of((1 - ch) * (half_rows - 16), 16)
        return pltpu.make_async_copy(
            x.at[:, pl.ds(begin, main), :],
            xa.at[:, pl.ds(pl.multiple_of(16 * ch, 16), main), lanes_in],
            misc_sem.at[1],
        )

    def xa_remote():
        begin = pl.multiple_of(ch * (half_rows - 16), 16)
        return remote(
            x.at[:, pl.ds(begin, main), :],
            xa.at[:, pl.ds(pl.multiple_of(16 * (1 - ch), 16), main), lanes_in],
            xa_send,
            xa_recv,
            y_peer,
        )

    def rim_up(s):
        return remote(
            x.at[:, local_rows - 16 : local_rows, :],
            xa.at[:, 0:16, lanes_in],
            rim_send.at[0],
            rim_recv.at[s],
            (batch, lax.rem(pos + 1, pos_count), 1),
        )

    def rim_down(s):
        return remote(
            x.at[:, 0:16, :],
            xa.at[:, ext - 16 : ext, lanes_in],
            rim_send.at[1],
            rim_recv.at[s],
            (batch, lax.rem(pos + pos_count - 1, pos_count), 0),
        )

    right = (batch, lax.rem(pos + ch, pos_count), 1 - ch)
    left = (batch, lax.rem(pos + pos_count - 1 + ch, pos_count), 1 - ch)
    rim_from = lax.rem(pos + pos_count + 1 - 2 * ch, pos_count)

    for copy in f_copies():
        copy.start()
    for kind in range(2):
        for copy in w_copies(kind):
            copy.start()
    og_copy().start()
    xa_local().start()
    meet(reduce.peers() + [right, left, (batch, rim_from, 0), (batch, rim_from, 1)])
    xa_remote().start()
    rim_up(ch).start()
    rim_down(ch).start()
    value[...] = jnp.zeros_like(value)
    for copy in f_copies():
        copy.wait()

    def normal(m, e, c):
        return (first[e, m, :, c] - vec_ref[m, 0:1, c]) * vec_ref[m, 1:2, c]

    def forward(m):
        @pl.loop(0, tiles)
        def _(j):
            c = columns(j)
            for e in range(2):
                act = normal(m, e, c) * vec_ref[m, 2:3, c] + vec_ref[m, 3:4, c]
                hid[m, e * pairs : (e + 1) * pairs, c] = gelu(act).astype(BF16)

        if m == 0:
            for copy in w_copies(0):
                copy.wait()

        @pl.loop(0, tiles)
        def _(j):
            c = columns(j)
            step = jnp.dot(hid[m], w2_ref[:, c], preferred_element_type=F32)
            even = step[:pairs] + (first[0, m, :, c] + vec_ref[m, 4:5, c])
            odd = step[pairs:] + (first[1, m, :, c] + vec_ref[m, 4:5, c])
            so[m, 0, :, c] = even
            so[m, 1, :, c] = odd
            diff[m, :, c] = (even - odd).astype(BF16)

        if m == 0:
            for copy in w_copies(1):
                copy.wait()
            og_copy().wait()
        limit = lim_ref[m, 0:1, 0:1]
        inverse_limit = 1.0 / limit

        @pl.loop(0, tiles)
        def _(j):
            c = columns(j)
            d = jnp.dot(diff[m], wp_ref[:, c], preferred_element_type=F32)
            t = jnp.tanh(0.5 * d)
            weight_even = 0.5 + 0.5 * t
            weight_odd = 0.5 - 0.5 * t
            even, odd = so[m, 0, :, c], so[m, 1, :, c]
            pooled[m, :, c] = (weight_even * even + weight_odd * odd).astype(BF16)
            clipped = limit * jnp.tanh(og[m, :, c].astype(F32) * inverse_limit)
            lg[m, :, c] = (weight_even * weight_odd * (even - odd) * clipped).astype(BF16)
            so[m, 0, :, c] = weight_even * clipped
            so[m, 1, :, c] = weight_odd * clipped

        pooled_local(m).start()
        pooled_remote(m).start()

    bins_at = pl.ds(pl.multiple_of(ch * pairs, 16), pairs)

    def pooled_local(m):
        return pltpu.make_async_copy(pooled.at[m, :, 0:half], pooled_out.at[m, bins_at], pooled_sem.at[m])

    def pooled_remote(m):
        return remote(
            pooled.at[m, :, half:wide], pooled_out.at[m, bins_at], pooled_send.at[m], pooled_recv.at[m], y_peer
        )

    def pool_back(m):
        @pl.loop(0, tiles)
        def _(j):
            c = columns(j)
            g = lax.dot_general(lg[m], wp_ref[c, :], NT, preferred_element_type=F32)
            even = so[m, 0, :, c] + g
            odd = so[m, 1, :, c] - g
            so[m, 0, :, c] = even
            so[m, 1, :, c] = odd
            low_even, low_odd = even.astype(BF16), odd.astype(BF16)
            branch[m, 0:pairs, c] = low_even
            branch[m, pairs:rows, c] = low_odd
            both = low_even.astype(F32) + low_odd.astype(F32)
            value[3 * m + 2 : 3 * m + 3, natural(j)] = jnp.sum(both, axis=0, keepdims=True)

    def act_back(m):
        @pl.loop(0, tiles)
        def _(j):
            c = columns(j)
            hg = lax.dot_general(branch[m], w2_ref[c, :], NT, preferred_element_type=F32)
            plain, cross = 0.0, 0.0
            for e in range(2):
                normed = normal(m, e, c)
                act = normed * vec_ref[m, 2:3, c] + vec_ref[m, 3:4, c]
                grad = hg[e * pairs : (e + 1) * pairs] * gelu_slope(act)
                a2g[m, e, :, c] = grad
                plain += jnp.sum(grad, axis=0, keepdims=True)
                cross += jnp.sum(grad * normed, axis=0, keepdims=True)
            value[3 * m : 3 * m + 1, natural(j)] = plain
            value[3 * m + 1 : 3 * m + 2, natural(j)] = cross

    blocks = 4 * far_count
    block = wide // blocks

    def product(dst, left, right_side):
        depth = left.shape[0] * left.shape[1]

        @pl.loop(0, tiles)
        def _(j):
            c = columns(j)
            dst[c, :] = lax.dot_general(
                left[:, :, c].reshape(depth, tile),
                right_side[...].reshape(depth, wide),
                TN,
                preferred_element_type=F32,
            ).astype(BF16)

    def block_rows(bb, zz, cc):
        number = lax.rem((bb * far_count + zz) * 2 + cc + ch * (blocks // 2), blocks)
        return pl.ds(pl.multiple_of(number * block, 16), block)

    def core_copies(src, dst, send, recv):
        return [
            remote(
                src.at[block_rows(bb, zz, 1 - core)], dst.at[bb, zz], send.at[bb, zz], recv.at[bb, zz], reduce.core_peer
            )
            for bb in range(2)
            for zz in range(far_count)
        ]

    def add_core(src, dst, sends):
        i = 0
        for bb in range(2):
            for zz in range(far_count):
                sends[i].wait_recv()
                i += 1
                mine = src[block_rows(bb, zz, core), :].astype(F32)
                dst[bb, zz] = (dst[bb, zz].astype(F32) + mine).astype(BF16)

    p_sends = core_copies(dwp, p_core, pc_send, pc_recv) if scatter else []
    q_sends = core_copies(dw2, q_core, qc_send, qc_recv) if scatter else []
    def pool_x(zz):
        return remote(
            p_core.at[1 - batch, zz], x_in.at[zz], x_send.at[zz], x_recv.at[zz], (1 - batch, pos, ch)
        )

    def pool_sum(zz):
        pool_x(zz).wait_recv()
        x_in[zz] = (x_in[zz].astype(F32) + p_core[batch, zz].astype(F32)).astype(BF16)

    def dwp_copy():
        return pltpu.make_async_copy(x_in if scatter else dwp, dwp_out, misc_sem.at[3])

    lanes_count = h_other.shape[2] // 128
    h_count = micro_count * lanes_count
    ext_half = ext // 2
    h_begin = pos * local_rows + (1 - ch) * half_rows - 16

    def h_load(i):
        at = pl.ds(pl.multiple_of(lax.rem(i, lanes_count) * 128, 128), 128)
        slot = lax.rem(i, 2)
        return pltpu.make_async_copy(xa.at[i // lanes_count, :, at], h_in.at[slot], h_in_sem.at[slot])

    def h_store(i):
        at = pl.ds(pl.multiple_of(lax.rem(i, lanes_count) * 128, 128), 128)
        to = pl.ds(pl.multiple_of((i // lanes_count) * pairs, 16), pairs)
        slot = lax.rem(i, 2)
        return pltpu.make_async_copy(h_stage.at[slot], h_other.at[:, to, at], h_out_sem.at[slot])

    def hidden_blocks(low, high):
        @pl.loop(low, high)
        def _(i):
            slot = lax.rem(i, 2)
            m = i // lanes_count
            at = pl.ds(pl.multiple_of(lax.rem(i, lanes_count) * 128, 128), 128)

            @pl.when(i + 1 < h_count)
            def _():
                h_load(i + 1).start()

            h_load(i).wait()

            @pl.when(i >= 2)
            def _():
                h_store(i - 2).wait()

            for part in range(2):
                v = h_in[slot, part * ext_half : (part + 1) * ext_half, :].astype(F32)
                act = (v - vec1_ref[m, 0:1, at]) * vec1_ref[m, 1:2, at] + vec1_ref[m, 2:3, at]
                row = h_begin + part * ext_half + lax.broadcasted_iota(jnp.int32, v.shape, 0)
                inside = jnp.logical_and(row >= 0, row < pos_count * local_rows)
                h_wide[part * ext_half : (part + 1) * ext_half, :] = jnp.where(inside, gelu(act), 0.0)
            for d in range(PIECES):
                h_stage[slot, d] = h_wide[pl.ds(16 - RIM + d, pairs, stride=2), :].astype(BF16)
            h_store(i).start()

    def dw2_copy():
        return pltpu.make_async_copy(q_core if scatter else dw2, dw2_out, misc_sem.at[2])

    for m in range(micro_count):
        forward(m)
    product(dwp, diff, lg)
    for copy in p_sends:
        copy.start()
    for m in range(micro_count):
        pool_back(m)
    if scatter:
        add_core(dwp, p_core, p_sends)
        for zz in range(far_count):
            pool_x(zz).start()
    product(dw2, hid, branch)
    for copy in q_sends:
        copy.start()
    if not scatter:
        dw2_copy().start()
    for m in range(micro_count):
        act_back(m)
    reduce.start(0)
    xa_local().wait()
    xa_remote().wait_recv()
    for s in range(2):
        rim_up(s).wait_recv()
    h_load(0).start()
    quarter = h_count // 4
    hidden_blocks(0, quarter)
    reduce.start(1)
    if scatter:
        add_core(dw2, q_core, q_sends)
        dw2_copy().start()
    hidden_blocks(quarter, 2 * quarter)
    reduce.start(2)
    hidden_blocks(2 * quarter, 3 * quarter)
    reduce.start(3)
    hidden_blocks(3 * quarter, h_count)
    reduce.wait(3)
    sum_out[...] = r_result[...]

    scale = 1.0 / total_rows

    def first_low(m, e, c, n, at):
        plain = r_result[3 * m : 3 * m + 1, n] * scale
        cross = r_result[3 * m + 1 : 3 * m + 2, n] * scale
        normed = (first[e, m, at, c] - vec_ref[m, 0:1, c]) * vec_ref[m, 1:2, c]
        grad = so[m, e, at, c] + vec_ref[m, 1:2, c] * vec_ref[m, 2:3, c] * (
            a2g[m, e, at, c] - plain - normed * cross
        )
        return grad.astype(BF16).astype(F32)

    edge_out[...] = jnp.zeros_like(edge_out)
    for q in range(2):
        c = slice(q * half, (q + 1) * half)
        n = pl.ds(pl.multiple_of(lax.rem(q + ch, 2) * half, 128), half)
        for m in range(micro_count):
            for e in range(2):
                row = 2 * m + e
                top = first_low(m, e, c, n, slice(0, 8))
                bottom = first_low(m, e, c, n, slice(pairs - 8, pairs))
                edge_out[0, row : row + 1, n] = top[0:1]
                edge_out[1, row : row + 1, n] = bottom[7:8]

    def edge_copy(side):
        return remote(
            edge_out.at[side], edge_in.at[1 - side], edge_send.at[side], edge_recv.at[1 - side], (left, right)[side]
        )

    for side in range(2):
        edge_copy(side).start()
    line = pos * 2 + ch
    edge_copy(1).wait_send()
    edge_copy(0).wait_send()
    for side in range(2):
        edge_copy(side).wait_recv()
    keep_before = jnp.where(line > 0, 1.0, 0.0)
    keep_after = jnp.where(line < 2 * pos_count - 1, 1.0, 0.0)
    slots = 2

    def gp_copies(slot, c):
        return [
            pltpu.make_async_copy(
                w2_ref.at[slot * micro_count * pairs : (slot + 1) * micro_count * pairs, d * tile : (d + 1) * tile],
                gp.at[d, :, c],
                gp_sem.at[slot, d],
            )
            for d in range(PIECES)
        ]

    extra[...] = jnp.zeros_like(extra)
    for j in range(tiles):
        c = columns(j)
        n = natural(j)
        slot = j % slots
        if j >= slots:
            for copy in gp_copies(slot, columns(j - slots)):
                copy.wait()
        for m in range(micro_count):
            total = 0.0
            for e in range(2):
                row = 2 * m + e
                low = first_low(m, e, c, n, slice(0, pairs))
                low32[e, 8 : 8 + pairs, :] = low
                low32[e, 7:8, :] = edge_in[0, row : row + 1, n] * keep_before
                low32[e, 8 + pairs : 9 + pairs, :] = edge_in[1, row : row + 1, n] * keep_after
                total += jnp.sum(low, axis=0, keepdims=True)
            extra[2 * micro_count + m : 2 * micro_count + m + 1, n] = total
            begin = slot * micro_count * pairs + m * pairs
            for d in range(PIECES):
                shift = 7 + d // 2
                w2_ref[begin : begin + pairs, d * tile : (d + 1) * tile] = low32[
                    d % 2, shift : shift + pairs, :
                ].astype(BF16)
        for copy in gp_copies(slot, c):
            copy.start()
        if j == 2:
            if scatter:
                for zz in range(far_count):
                    pool_sum(zz)
            dwp_copy().start()
    for j in range(tiles - slots, tiles):
        for copy in gp_copies(j % slots, columns(j)):
            copy.wait()
    for i in range(h_count - 2, h_count):
        h_store(i).wait()
    xa_remote().wait_send()
    rim_up(0).wait_send()
    rim_down(0).wait_send()
    for m in range(micro_count):
        pooled_local(m).wait()
        pooled_remote(m).wait()
    dw2_copy().wait()
    dwp_copy().wait()
    if scatter:
        for zz in range(far_count):
            pool_x(zz).wait_send()
        for copy in p_sends + q_sends:
            copy.wait_send()


def middle(first_own, first_other, weights, og, x, vecs, vec1, limits, total_rows):
    _, micro_count, pairs, half = first_own.shape
    wide = 2 * half
    rows = 2 * pairs
    depth = micro_count * pairs
    local_rows, local_in = x.shape[1:]
    far = lax.axis_size("pos") // 2
    block = wide // (4 * far)
    scatter = block % 16 == 0
    land = block if scatter else 16
    tile = 256
    any_space = pl.BlockSpec(memory_space=pl.ANY)
    in_vmem = pl.BlockSpec(memory_space=pltpu.VMEM)
    dma = pltpu.SemaphoreType.DMA
    return pl.pallas_call(
        functools.partial(middle_kernel, scatter, total_rows),
        out_shape=(
            jax.ShapeDtypeStruct((micro_count, rows, half), BF16),
            jax.ShapeDtypeStruct((PIECES, depth, wide), BF16),
            jax.ShapeDtypeStruct((micro_count, local_rows // 2 + 32, 2 * local_in), BF16),
            jax.ShapeDtypeStruct((PIECES, depth, 2 * local_in), BF16),
            jax.ShapeDtypeStruct((2, far, block, wide) if scatter else (wide, wide), BF16),
            jax.ShapeDtypeStruct((far, block, wide) if scatter else (wide, wide), BF16),
            jax.ShapeDtypeStruct((8, wide), F32),
            jax.ShapeDtypeStruct((8, wide), F32),
        ),
        in_specs=[any_space] * 8 + [in_vmem] * 3,
        out_specs=(any_space,) * 6 + (in_vmem, in_vmem),
        scratch_shapes=[
            pltpu.VMEM((wide, wide), BF16),
            pltpu.VMEM((wide, wide), BF16),
            pltpu.VMEM((2, micro_count, pairs, wide), F32),
            pltpu.VMEM((micro_count, 2, pairs, wide), F32),
            pltpu.VMEM((micro_count, 2, pairs, wide), F32),
            pltpu.VMEM((micro_count, rows, wide), BF16),
            pltpu.VMEM((micro_count, rows, wide), BF16),
            pltpu.VMEM((micro_count, pairs, wide), BF16),
            pltpu.VMEM((micro_count, pairs, wide), BF16),
            pltpu.VMEM((micro_count, pairs, wide), BF16),
            pltpu.VMEM((micro_count, pairs, wide), BF16),
            pltpu.VMEM((wide, wide), BF16),
            pltpu.VMEM((wide, wide), BF16),
            pltpu.VMEM((2, far, land, wide), BF16),
            pltpu.VMEM((2, far, land, wide), BF16),
            pltpu.VMEM((2, pairs + 16, tile), F32),
            pltpu.VMEM((2, 8, wide), F32),
            pltpu.VMEM((2, 8, wide), F32),
            pltpu.VMEM((2, local_rows // 2 + 32, 128), BF16),
            pltpu.VMEM((local_rows // 2 + 32, 128), F32),
            pltpu.VMEM((2, PIECES, pairs, 128), BF16),
            dma((2,)),
            dma((2,)),
            dma((2, 2, 2)),
            dma((2,)),
            dma((4,)),
            dma((2, PIECES)),
            dma((micro_count,)),
            dma((micro_count,)),
            dma((micro_count,)),
            dma,
            dma,
            dma((2,)),
            dma((2,)),
            dma((2,)),
            dma((2,)),
            dma((2, far)),
            dma((2, far)),
            dma((2, far)),
            dma((2, far)),
        ]
        + Reduce.scratch(wide)
        + [pltpu.VMEM((far, land, wide), BF16), dma((far,)), dma((far,))],
        compiler_params=params(collective_id=7, has_side_effects=True),
        name="middle",
    )(first_own, first_other, *weights, og, x, vecs, vec1, limits)


def tail_kernel(
    scatter,
    total_rows,
    hp_own,
    hp_other,
    gp,
    wo,
    wx,
    xs_in,
    dw2,
    dwp,
    vec_ref,
    extra_ref,
    ig,
    dw_out,
    dw2_out,
    dwp_out,
    sum_out,
    g_buf,
    w_buf,
    a1g,
    xs,
    h_buf,
    f_buf,
    dw,
    core_in,
    x_in,
    z_in,
    weave,
    load_sem,
    w_sem,
    h_sem,
    low_send,
    low_recv,
    core_send,
    core_recv,
    x_send,
    x_recv,
    z_send,
    z_recv,
    ig_send,
    ig_recv,
    ig_sem,
    value,
    r_core,
    r_near,
    r_far,
    r_result,
    r_send,
    r_recv,
    k2_buf,
    x2_in,
    z2_in,
    y2_out,
    y2_in,
    z2_send,
    z2_recv,
    y2_send,
    y2_recv,
    x2_send,
    x2_recv,
    x3_in,
    z3_in,
    y3_out,
    y3_in,
    z3_send,
    z3_recv,
    y3_send,
    y3_recv,
):
    reduce = Reduce(value, r_core, r_near, r_far, r_result, (r_send, r_recv))
    batch, pos, ch, core, z = reduce.batch, reduce.pos, reduce.ch, reduce.core, reduce.z
    far_count = reduce.far_count
    chunks, rows_all, chunk = dw.shape
    rows, wide = xs.shape[1:]
    micro_count, pairs = vec_ref.shape[0], rows // vec_ref.shape[0]
    half_rows = 2 * pairs
    out = gp.shape[2]
    local_out = out // 2
    local_in = wide // 2
    tile = w_buf.shape[1]
    cut = h_buf.shape[3]
    per_half = rows_all // 2 // cut
    y_peer = (batch, pos, 1 - ch)
    x_peer = (1 - batch, pos, ch)
    core_peer = reduce.core_peer

    def loads():
        copies = [
            pltpu.make_async_copy(gp.at[2:4, :, 0:local_out], f_buf.at[0:2], load_sem.at[0]),
            pltpu.make_async_copy(xs_in, xs, load_sem.at[1]),
        ]
        for d in range(PIECES):
            copies.append(
                pltpu.make_async_copy(gp.at[d], g_buf.at[:, d * out : (d + 1) * out], load_sem.at[2 + d])
            )
        return copies

    def w_copies(j):
        s = j % 2
        at = slice(j * tile, (j + 1) * tile)
        copies = []
        for k in range(KW):
            for q, src in enumerate((wo, wx)):
                lanes = (KW - 1 - k) * out + q * local_out
                copies.append(
                    pltpu.make_async_copy(
                        src.at[k, at, :], w_buf.at[s, :, lanes : lanes + local_out], w_sem.at[s, 2 * k + q]
                    )
                )
        return copies

    def h_copies(side_half, t):
        number = side_half * per_half + t
        k = number // 2
        at = pl.ds(pl.multiple_of(lax.rem(number, 2) * cut, cut), cut)
        slot = lax.rem(t, 2)
        return [
            pltpu.make_async_copy((hp_own, hp_other)[s].at[k + e, :, at], h_buf.at[slot, 2 * s + e], h_sem.at[slot, 2 * s + e])
            for s in range(2)
            for e in range(2)
        ]

    def low_copy(c):
        return pltpu.make_async_remote_copy(
            gp.at[2:4, :, local_out + c * chunk : local_out + (c + 1) * chunk],
            f_buf.at[2:4, :, c * chunk : (c + 1) * chunk],
            low_send.at[c],
            low_recv.at[c],
            device_id=y_peer,
            device_id_type=MESH,
        )

    second = Scatter(
        reduce,
        lambda zz: k2_buf.at[zz],
        lambda zz: dw2.at[1 - batch, zz],
        x2_in,
        z2_in,
        y2_out,
        y2_in,
        (z2_send, z2_recv, y2_send, y2_recv, x2_send, x2_recv),
        round_steps(far_count),
    )
    third = Scatter(
        reduce,
        None,
        None,
        x3_in,
        z3_in,
        y3_out,
        y3_in,
        (z3_send, z3_recv, y3_send, y3_recv),
        round_steps(far_count),
    )

    def third_copy():
        return pltpu.make_async_copy(dwp, x3_in, load_sem.at[3 + PIECES])

    def k2_copy():
        return pltpu.make_async_copy(dw2.at[batch], k2_buf, load_sem.at[2 + PIECES])

    for copy in loads():
        copy.start()
    for copy in w_copies(0):
        copy.start()
    if scatter:
        k2_copy().start()
        third_copy().start()
    meet(reduce.peers())
    low_copy(0).start()
    if scatter:
        for r in range(far_count):
            second.send_x(r)
        third_copy().wait()
        for r in range(far_count - 1):
            third.send_z(r)
    for copy in h_copies(1 - batch, 0):
        copy.start()
    for copy in loads()[1:]:
        copy.wait()
    value[...] = extra_ref[...]

    tiles = wide // tile

    def back(j):
        s = j % 2
        if j + 1 < tiles:
            for copy in w_copies(j + 1):
                copy.start()
        for copy in w_copies(j):
            copy.wait()
        at = slice(j * tile, (j + 1) * tile)
        sums = [[0.0, 0.0] for _ in range(micro_count)]
        for e in range(2):
            acc = lax.dot_general(
                g_buf[:, e * out : (e + KW) * out], w_buf[s], NT, preferred_element_type=F32
            )
            for m in range(micro_count):
                x = xs[e, m * pairs : (m + 1) * pairs, at].astype(F32)
                moved = x - vec_ref[m, 0:1, at]
                normed = moved * vec_ref[m, 3:4, at]
                act = moved * vec_ref[m, 1:2, at] + vec_ref[m, 2:3, at]
                grad = acc[m * pairs : (m + 1) * pairs] * gelu_slope(act)
                a1g[e, m * pairs : (m + 1) * pairs, at] = grad
                sums[m][0] += jnp.sum(grad, axis=0, keepdims=True)
                sums[m][1] += jnp.sum(grad * normed, axis=0, keepdims=True)
        for m in range(micro_count):
            for i in range(2):
                value[2 * m + i : 2 * m + i + 1, at] = sums[m][i]

    block = rows_all // (2 * 2 * far_count)

    def block_rows(side_half, zz, cc):
        return pl.ds(pl.multiple_of(((side_half * far_count + zz) * 2 + cc) * block, 16), block)

    def core_copy(c, kind, side_half, zz):
        return pltpu.make_async_remote_copy(
            dw.at[c, block_rows(side_half, zz, 1 - core)],
            core_in.at[c, kind, zz],
            core_send.at[c, kind, zz],
            core_recv.at[c, kind, zz],
            device_id=core_peer,
            device_id_type=MESH,
        )

    def x_copy(c, zz):
        return pltpu.make_async_remote_copy(
            dw.at[c, block_rows(1 - batch, zz, core)],
            x_in.at[c, zz],
            x_send.at[c, zz],
            x_recv.at[c, zz],
            device_id=x_peer,
            device_id_type=MESH,
        )

    def z_copy(c, r, zz):
        return pltpu.make_async_remote_copy(
            dw.at[c, block_rows(batch, zz, core)],
            z_in.at[c, r],
            z_send.at[c, r],
            z_recv.at[c, r],
            device_id=(batch, zz * 2 + core, ch),
            device_id_type=MESH,
        )

    steps = round_steps(far_count)

    def away(r):
        return lax.rem(z + steps[r], far_count)

    def weigh(c, kind, side_half, following, hook=None, hook_at=2):
        lanes = slice(c * chunk, (c + 1) * chunk)

        @pl.loop(0, per_half)
        def _(t):
            @pl.when(t + 1 < per_half)
            def _():
                for copy in h_copies(side_half, t + 1):
                    copy.start()

            for copy in h_copies(side_half, t):
                copy.wait()
            slot = lax.rem(t, 2)
            grad = lax.dot_general(
                h_buf[slot].reshape(4 * rows, cut),
                f_buf[:, :, lanes].reshape(4 * rows, chunk),
                TN,
                preferred_element_type=F32,
            )
            at = pl.multiple_of((side_half * per_half + t) * cut, 16)
            dw[c, pl.ds(at, cut), :] = grad.astype(BF16)
            if hook is not None:
                pl.when(t == hook_at)(hook)

        if following is not None:
            for copy in h_copies(following, 0):
                copy.start()
        if scatter:
            for r in range(far_count):
                core_copy(c, kind, side_half, away(r)).start()

    def add_to(c, at, ref, *index):
        dw[c, at, :] = (dw[c, at, :].astype(F32) + ref[index].astype(F32)).astype(BF16)

    def send_x(c):
        if scatter:
            for r in range(far_count):
                zz = away(r)
                core_copy(c, 0, 1 - batch, zz).wait_recv()
                add_to(c, block_rows(1 - batch, zz, core), core_in, c, 0, zz)
                x_copy(c, zz).start()

    def send_z(c):
        if scatter:
            for r in range(far_count):
                zz = away(r)
                core_copy(c, 1, batch, zz).wait_recv()
                x_copy(c, zz).wait_recv()
                at = block_rows(batch, zz, core)
                total = dw[c, at, :].astype(F32) + core_in[c, 1, zz].astype(F32) + x_in[c, zz].astype(F32)
                lanes = slice(c * chunk, (c + 1) * chunk)
                if r < far_count - 1:
                    dw[c, at, :] = total.astype(BF16)
                    z_copy(c, r, zz).start()
                else:
                    dw_out[:, lanes] = total

    def finish(c):
        lanes = slice(c * chunk, (c + 1) * chunk)
        if scatter:
            for r in range(far_count - 1):
                z_copy(c, r, away(r)).wait_recv()
                dw_out[:, lanes] = dw_out[:, lanes] + z_in[c, r].astype(F32)
        else:
            copy = pltpu.make_async_copy(dw.at[c], dw_out.at[:, lanes], load_sem.at[4 + PIECES])
            copy.start()
            copy.wait()

    def ig_copies(m):
        copies = []
        for part in range(2):
            at = pl.ds(pl.multiple_of(ch * half_rows + part * pairs, 16), pairs)
            kept = pl.ds(pl.multiple_of(ch * local_in, 128), local_in)
            sent = pl.ds(pl.multiple_of((1 - ch) * local_in, 128), local_in)
            here = xs.at[part, m * pairs : (m + 1) * pairs]
            copies.append(pltpu.make_async_copy(here.at[:, kept], ig.at[m, at], ig_sem.at[m, part]))
            copies.append(
                pltpu.make_async_remote_copy(
                    here.at[:, sent],
                    ig.at[m, at],
                    ig_send.at[m, part],
                    ig_recv.at[m, part],
                    device_id=y_peer,
                    device_id_type=MESH,
                )
            )
        return copies

    def input_grad(m):
        scale = 1.0 / total_rows

        @pl.loop(0, wide // 128)
        def _(b):
            at = pl.ds(pl.multiple_of(b * 128, 128), 128)
            plain = r_result[2 * m : 2 * m + 1, at] * scale
            cross = r_result[2 * m + 1 : 2 * m + 2, at] * scale
            inverse = vec_ref[m, 3:4, at]
            for e in range(2):
                x = xs[e, m * pairs : (m + 1) * pairs, at].astype(F32)
                normed = (x - vec_ref[m, 0:1, at]) * inverse
                grad = a1g[e, m * pairs : (m + 1) * pairs, at]
                weave[pl.ds(e, pairs, stride=2), :] = vec_ref[m, 1:2, at] * (grad - plain - normed * cross)
            for part in range(2):
                xs[part, m * pairs : (m + 1) * pairs, at] = weave[part * pairs : (part + 1) * pairs, :].astype(BF16)

        for copy in ig_copies(m):
            copy.start()

    for j in range(3):
        back(j)
    loads()[0].wait()
    low_copy(0).wait_recv()
    low_copy(1).start()
    weigh(0, 0, 1 - batch, 1 - batch)
    send_x(0)
    back(3)
    if scatter:
        k2_copy().wait()
        for r in range(far_count):
            second.send_z(r)
    back(4)
    reduce.start(0)
    low_copy(1).wait_recv()
    low_copy(2).start()
    weigh(1, 0, 1 - batch, batch, lambda: reduce.start(1))
    reduce.start(2)
    send_x(1)
    weigh(0, 1, batch, 1 - batch, lambda: reduce.start(3))
    send_z(0)
    reduce.wait(3)
    sum_out[...] = r_result[...]
    for m in range(micro_count):
        input_grad(m)
    low_copy(2).wait_recv()
    weigh(2, 0, 1 - batch, batch)
    send_x(2)
    weigh(1, 1, batch, batch)
    send_z(1)
    if scatter:
        dw2_out[...] = second.send_y()
        dwp_out[...] = third.send_y()
    weigh(2, 1, batch, None)
    finish(0)
    send_z(2)
    finish(1)
    finish(2)
    for m in range(micro_count):
        for copy in ig_copies(m):
            copy.wait()
    if scatter:
        dw2_out[...] += second.finish()
        dwp_out[...] += third.finish()
        second.drain()
        third.drain()
    else:
        dw2_out[...] = jnp.zeros_like(dw2_out)
        dwp_out[...] = jnp.zeros_like(dwp_out)
    for c in range(chunks):
        low_copy(c).wait_send()
        if scatter:
            for r in range(far_count):
                zz = away(r)
                core_copy(c, 0, 1 - batch, zz).wait_send()
                core_copy(c, 1, batch, zz).wait_send()
                x_copy(c, zz).wait_send()
                if r < far_count - 1:
                    z_copy(c, r, zz).wait_send()


def tail(pieces, other_pieces, grad_pieces, own, other, x_split, dw2, dwp, vecs, extra, total_rows):
    _, rows, wide = pieces.shape
    micro_count = vecs.shape[0]
    pairs = rows // micro_count
    out = grad_pieces.shape[-1]
    local_out = out // 2
    chunks = 3
    chunk = local_out // chunks
    far = lax.axis_size("pos") // 2
    rows_all = KW * wide
    block = rows_all // (4 * far)
    scatter = block % 16 == 0
    tile = 256
    land = block if scatter else 16
    block2 = dw2.shape[2] if scatter else 16
    any_space = pl.BlockSpec(memory_space=pl.ANY)
    in_vmem = pl.BlockSpec(memory_space=pltpu.VMEM)
    dma = pltpu.SemaphoreType.DMA
    return pl.pallas_call(
        functools.partial(tail_kernel, scatter, total_rows),
        out_shape=(
            jax.ShapeDtypeStruct((micro_count, 4 * pairs, wide // 2), BF16),
            jax.ShapeDtypeStruct((block, local_out) if scatter else (rows_all, local_out), F32 if scatter else BF16),
            jax.ShapeDtypeStruct((block2, local_out), F32),
            jax.ShapeDtypeStruct((block2, local_out), F32),
            jax.ShapeDtypeStruct((8, out), F32),
        ),
        in_specs=[any_space] * 8 + [in_vmem] * 2,
        out_specs=(any_space, in_vmem if scatter else any_space, in_vmem, in_vmem, in_vmem),
        scratch_shapes=[
            pltpu.VMEM((rows, PIECES * out), BF16),
            pltpu.VMEM((2, tile, KW * out), BF16),
            pltpu.VMEM((2, rows, wide), F32),
            pltpu.VMEM((2, rows, wide), BF16),
            pltpu.VMEM((2, 4, rows, wide // 2), BF16),
            pltpu.VMEM((4, rows, local_out), BF16),
            pltpu.VMEM((chunks, rows_all, chunk), BF16),
            pltpu.VMEM((chunks, 2, far, land, chunk), BF16),
            pltpu.VMEM((chunks, far, land, chunk), BF16),
            pltpu.VMEM((chunks, far - 1, land, chunk), BF16),
            pltpu.VMEM((2 * pairs, 128), F32),
            dma((5 + PIECES,)),
            dma((2, 2 * KW)),
            dma((2, 4)),
            dma((chunks,)),
            dma((chunks,)),
            dma((chunks, 2, far)),
            dma((chunks, 2, far)),
            dma((chunks, far)),
            dma((chunks, far)),
            dma((chunks, far - 1)),
            dma((chunks, far - 1)),
            dma((micro_count, 2)),
            dma((micro_count, 2)),
            dma((micro_count, 2)),
        ]
        + Reduce.scratch(out)
        + [pltpu.VMEM((far, block2, out), BF16)]
        + Scatter.scratch(block2, out)
        + [dma((far,)), dma((far,))]
        + Scatter.scratch(block2, out),
        compiler_params=params(collective_id=5, has_side_effects=True),
        name="tail",
    )(
        pieces,
        other_pieces,
        grad_pieces,
        own.reshape(KW, wide, local_out),
        other.reshape(KW, wide, local_out),
        x_split,
        dw2,
        dwp,
        vecs,
        extra,
    )


def collect_kernel(part, sums3, *refs):
    count = 5
    sources, targets, vectors = refs[:count], refs[count : 2 * count], refs[2 * count : 2 * count + 6]
    held, sems = refs[2 * count + 6 : -1], refs[-1]
    loads = [pltpu.make_async_copy(a, h, sems.at[0, i]) for i, (a, h) in enumerate(zip(sources, held))]
    copies = [pltpu.make_async_copy(h, b, sems.at[1, i]) for i, (h, b) in enumerate(zip(held, targets))]
    for load in loads:
        load.start()
    for load, copy in zip(loads, copies):
        load.wait()
        copy.start()
    ch = lax.axis_index("ch")
    micro_count = 2

    def put(dst, ref, rows):
        width = dst.shape[0]
        at = pl.ds(pl.multiple_of(ch * width, 128), width)
        total = ref[rows[0] : rows[0] + 1, at]
        for r in rows[1:]:
            total = total + ref[r : r + 1, at]
        dst[...] = total.reshape(width)

    ms = range(micro_count)
    put(vectors[0], part, [2 * m + 1 for m in ms])
    put(vectors[1], part, [2 * m for m in ms])
    put(vectors[2], part, [2 * micro_count + m for m in ms])
    put(vectors[3], sums3, [3 * m + 1 for m in ms])
    put(vectors[4], sums3, [3 * m for m in ms])
    put(vectors[5], sums3, [3 * m + 2 for m in ms])
    for copy in copies:
        copy.wait()


def collect(arrays, part, sums3, local_in, local_out):
    any_space = pl.BlockSpec(memory_space=pl.ANY)
    in_vmem = pl.BlockSpec(memory_space=pltpu.VMEM)
    widths = [local_in, local_in] + [local_out] * 4
    return pl.pallas_call(
        collect_kernel,
        out_shape=tuple(jax.ShapeDtypeStruct(v.shape, v.dtype) for v in arrays)
        + tuple(jax.ShapeDtypeStruct((w,), F32) for w in widths),
        in_specs=[in_vmem] * 2 + [any_space] * 5,
        out_specs=(any_space,) * 5 + (in_vmem,) * 6,
        scratch_shapes=[pltpu.VMEM(v.shape, v.dtype) for v in arrays] + [pltpu.SemaphoreType.DMA((2, 5))],
        compiler_params=params(),
        name="collect",
    )(part, sums3, *arrays)


def local(
    section_input,
    norm1_gain,
    norm1_bias,
    conv1_weight,
    conv1_bias,
    norm2_gain,
    norm2_bias,
    conv2_weight,
    conv2_bias,
    pool_weight,
    out_grad,
    clip_table,
    clip_index,
):
    micro_count, seq_count, local_rows, local_in = section_input.shape
    batch_count, pos_count, ch_count = (lax.axis_size(a) for a in ("batch", "pos", "ch"))
    batch, pos, ch = (lax.axis_index(a) for a in ("batch", "pos", "ch"))
    total_rows = seq_count * local_rows * batch_count * pos_count
    wide_in = 2 * local_in
    local_out = conv1_weight.shape[1]
    wide_out = 2 * local_out
    half = local_rows // 2
    pairs = half // 2
    plane = batch_count * pos_count
    spot = batch * pos_count + pos
    swap = [(0, 1), (1, 0)]
    is_low = ch == 0

    def other_ch(v):
        return lax.ppermute(v, "ch", swap)

    def natural(own, other, axis):
        return jnp.where(
            is_low,
            jnp.concatenate([own, other], axis=axis),
            jnp.concatenate([other, own], axis=axis),
        )

    x = section_input.reshape(micro_count, local_rows, local_in)

    def own_first(v):
        return jnp.where(
            is_low, v, jnp.concatenate([v[..., local_out:], v[..., :local_out]], axis=-1)
        )

    to_natural = own_first
    bins = local_rows // 2
    mine = bins // 2
    small = jnp.stack([conv1_bias, norm2_gain, norm2_bias, conv2_bias])
    small = jnp.concatenate(
        [small, jnp.pad(jnp.stack([norm1_gain, norm1_bias]), ((0, 2), (0, local_out - local_in)))]
    )
    (
        pieces,
        x_split,
        first_own,
        first_other,
        w1_other,
        w2_other,
        wp_other,
        og_full,
        vec1,
        vec2,
    ) = head(
        x,
        conv1_weight,
        conv2_weight,
        pool_weight,
        out_grad.reshape(micro_count, bins, local_out),
        small,
        total_rows,
    )
    first_own = first_own.reshape(2, micro_count, pairs, local_out)
    first_other = first_other.reshape(2, micro_count, pairs, local_out)
    table_pos = jnp.arange(clip_table.shape[0], dtype=jnp.int32)
    limit = jnp.sum(jnp.where(table_pos[None] == clip_index[:, None], clip_table[None], 0.0), axis=1)
    limits = jnp.broadcast_to(limit[:, None, None], (micro_count, 8, 128))

    section_output, grad_pieces, _, other_pieces, dw2, dwp, sums3, extra = middle(
        first_own,
        first_other,
        (conv2_weight, w2_other, pool_weight, wp_other),
        og_full,
        x,
        vec2,
        vec1,
        limits,
        total_rows,
    )
    whole_two, whole_pool = dw2, dwp
    input_grad, dw1, dw2, dwp, part = tail(
        pieces, other_pieces, grad_pieces, conv1_weight, w1_other, x_split, dw2, dwp, vec1, extra, total_rows
    )

    def scatter(v):
        return lax.psum_scatter(v, ("batch", "pos"), scatter_dimension=0, tiled=True).astype(F32)

    def fold(v):
        v = jnp.where(is_low, v, jnp.concatenate([v[local_out:], v[:local_out]], axis=0))
        away = other_ch(v[:, local_out:])
        return scatter((v[:, :local_out].astype(F32) + away.astype(F32)).astype(BF16))

    if whole_pool.ndim == 2:
        dw2, dwp = fold(whole_two), fold(whole_pool)
    if dw1.shape[0] != KW * wide_in // plane:
        dw1 = scatter(dw1)
    section_output, input_grad, dw1, dw2, dwp, *vectors = collect(
        (section_output, input_grad, dw1, dw2, dwp), part, sums3, local_in, local_out
    )
    return (
        section_output.reshape(micro_count, seq_count, bins, local_out),
        input_grad.reshape(section_input.shape),
        vectors[0],
        vectors[1],
        dw1,
        vectors[2],
        vectors[3],
        vectors[4],
        dw2,
        vectors[5],
        dwp,
    )


def solution(mesh):
    placed = (
        P(None, "batch", "pos", "ch"),
        P("ch"),
        P("ch"),
        P(None, "ch"),
        P("ch"),
        P("ch"),
        P("ch"),
        P(None, "ch"),
        P("ch"),
        P(None, "ch"),
        P(None, "batch", "pos", "ch"),
        P(),
        P(),
    )
    return jax.shard_map(
        local,
        mesh=mesh,
        in_specs=placed,
        out_specs=(
            P(None, "batch", "pos", "ch"),
            P(None, "batch", "pos", "ch"),
            P("ch"),
            P("ch"),
            P(("batch", "pos"), "ch"),
            P("ch"),
            P("ch"),
            P("ch"),
            P(("batch", "pos"), "ch"),
            P("ch"),
            P(("batch", "pos"), "ch"),
        ),
        check_vma=False,
    )
```

```python
import functools

import jax
import jax.numpy as jnp
from jax import lax
from jax.experimental import pallas as pl
from jax.experimental.pallas import tpu as pltpu
from jax.sharding import PartitionSpec as P

KW = 5
RIM = KW // 2
PIECES = KW + 1
EPS = 1e-05
MESH = pl.DeviceIdType.MESH
C0 = 0.7978845608028654
C1 = 0.044715
F32 = jnp.float32
BF16 = jnp.bfloat16
VMEM_LIMIT = 60 * 1024 * 1024

NT = (((1,), (1,)), ((), ()))
TN = (((0,), (0,)), ((), ()))


def params(**kw):
    return pltpu.CompilerParams(vmem_limit_bytes=VMEM_LIMIT, **kw)


def gelu(u):
    return 0.5 * u * (1.0 + jnp.tanh(C0 * (u + C1 * u * u * u)))


def gelu_slope(u):
    square = u * u
    t = jnp.tanh(C0 * (u + C1 * square * u))
    return 0.5 * (1.0 + t) + 0.5 * u * (1.0 - t * t) * (C0 + (3.0 * C0 * C1) * square)


class Reduce:
    def __init__(self, value, core_in, near, far, result, sems):
        self.value, self.core_in, self.near, self.far, self.result = value, core_in, near, far, result
        self.send, self.recv = sems
        self.batch, self.pos, self.ch = (lax.axis_index(a) for a in ("batch", "pos", "ch"))
        self.core = lax.rem(self.pos, 2)
        self.z = self.pos // 2
        self.far_count = lax.axis_size("pos") // 2
        half = value.shape[1] // 2
        self.mine = pl.ds(pl.multiple_of(self.core * half, half), half)
        self.away = pl.ds(pl.multiple_of((1 - self.core) * half, half), half)
        self.me = self.batch * 2 + self.ch
        self.core_peer = (self.batch, self.z * 2 + 1 - self.core, self.ch)
        self.near_peers = []
        for step in range(1, 4):
            other = lax.rem(self.me + step, 4)
            self.near_peers.append((other // 2, self.pos, lax.rem(other, 2)))
        self.far_peers = []
        for step in range(1, self.far_count):
            other = lax.rem(self.z + step, self.far_count)
            self.far_peers.append((self.batch, other * 2 + self.core, self.ch))

    @staticmethod
    def scratch(width):
        far = lax.axis_size("pos") // 2
        count = 2 + 3 + far - 1
        return [
            pltpu.VMEM((8, width), F32),
            pltpu.VMEM((8, width // 2), F32),
            pltpu.VMEM((4, 8, width // 2), F32),
            pltpu.VMEM((far, 8, width // 2), F32),
            pltpu.VMEM((8, width), F32),
            pltpu.SemaphoreType.DMA((count,)),
            pltpu.SemaphoreType.DMA((count,)),
        ]

    def peers(self):
        return [self.core_peer] + self.near_peers + self.far_peers

    def copy(self, i, src, dst, peer):
        return pltpu.make_async_remote_copy(
            src, dst, self.send.at[i], self.recv.at[i], device_id=peer, device_id_type=MESH
        )

    def copies(self, stage):
        if stage == 0:
            return [self.copy(0, self.value.at[:, self.away], self.core_in, self.core_peer)]
        if stage == 1:
            slot = self.near.at[self.me]
            return [self.copy(1 + i, slot, slot, p) for i, p in enumerate(self.near_peers)]
        if stage == 2:
            slot = self.far.at[self.z]
            return [self.copy(4 + i, slot, slot, p) for i, p in enumerate(self.far_peers)]
        part = self.result.at[:, self.mine]
        return [self.copy(3 + self.far_count, part, part, self.core_peer)]

    def wait(self, stage):
        for copy in self.copies(stage):
            copy.wait()

    def start(self, stage):
        if stage == 1:
            self.wait(0)
            self.near[pl.ds(self.me, 1)] = (self.value[:, self.mine] + self.core_in[...])[None]
        if stage == 2:
            self.wait(1)
            total = (self.near[0] + self.near[1]) + (self.near[2] + self.near[3])
            self.far[pl.ds(self.z, 1)] = total[None]
        if stage == 3:
            self.wait(2)
            total = self.far[0]
            for i in range(1, self.far_count):
                total = total + self.far[i]
            self.result[:, self.mine] = total
        for copy in self.copies(stage):
            copy.start()


def meet(peers):
    barrier = pltpu.get_barrier_semaphore()
    for peer in peers:
        pl.semaphore_signal(barrier, inc=1, device_id=peer, device_id_type=MESH)
    pl.semaphore_wait(barrier, len(peers))


def reduce_kernel(v_ref, o_ref, *scratch):
    value, core_in, near, far, result, send, recv = scratch
    reduce = Reduce(value, core_in, near, far, result, (send, recv))
    value[...] = v_ref[...]
    meet(reduce.peers())
    for stage in range(4):
        reduce.start(stage)
    reduce.wait(3)
    o_ref[...] = result[...]


def reduce_all(values, collective_id):
    rows, width = values.shape
    total = pl.pallas_call(
        reduce_kernel,
        out_shape=jax.ShapeDtypeStruct((8, width), F32),
        in_specs=[pl.BlockSpec(memory_space=pltpu.VMEM)],
        out_specs=pl.BlockSpec(memory_space=pltpu.VMEM),
        scratch_shapes=Reduce.scratch(width),
        compiler_params=params(collective_id=collective_id, has_side_effects=True),
        name="reduce",
    )(jnp.pad(values, ((0, 8 - rows), (0, 0))))
    return total[:rows]


def head_kernel(
    total_rows,
    x,
    w1,
    w2,
    wp,
    og,
    small_ref,
    hp,
    xs_out,
    f_own,
    f_other,
    w1x,
    w2x,
    wpx,
    ogx,
    vec1,
    vec2,
    small_x,
    x_loc,
    x_ext,
    scr,
    raw,
    h_cat,
    xs,
    w_buf,
    f_buf,
    load_sem,
    w_sem,
    f_sem,
    out_sem,
    in_send,
    in_recv,
    halo_send,
    halo_recv,
    y1_send,
    y1_recv,
    z1_send,
    z1_recv,
    x1_send,
    x1_recv,
    c1_send,
    c1_recv,
    y2_send,
    y2_recv,
    c2_send,
    c2_recv,
    og_send,
    og_recv,
    small_send,
    small_recv,
    value,
    r_core,
    r_near,
    r_far,
    r_result,
    r_send,
    r_recv,
    value2,
    s_core,
    s_near,
    s_far,
    s_result,
    s_send,
    s_recv,
):
    first = Reduce(value, r_core, r_near, r_far, r_result, (r_send, r_recv))
    second = Reduce(value2, s_core, s_near, s_far, s_result, (s_send, s_recv))
    batch, pos, ch, core, z = first.batch, first.pos, first.ch, first.core, first.z
    far_count = first.far_count
    pos_count = 2 * far_count
    plane = 2 * pos_count
    micro_count, local_rows, local_in = x.shape
    wide = 2 * local_in
    half = local_rows // 2
    pairs = half // 2
    rows = micro_count * pairs
    ext = half + 32
    main = half + 16
    local_out = w1.shape[1]
    parts, chunk = w_buf.shape[0], w_buf.shape[2]
    lanes_count = wide // 128
    y_peer = (batch, pos, 1 - ch)
    x_peer = (1 - batch, pos, ch)
    up_pos = lax.rem(pos + 1, pos_count)
    down_pos = lax.rem(pos + pos_count - 1, pos_count)

    def remote(src, dst, send, recv, peer):
        return pltpu.make_async_remote_copy(src, dst, send, recv, device_id=peer, device_id_type=MESH)

    my_lanes = pl.ds(pl.multiple_of(ch * local_in, 128), local_in)

    def own_input():
        begin = pl.multiple_of(ch * (half - 16), 16)
        return pltpu.make_async_copy(
            x.at[:, pl.ds(begin, main), :],
            x_ext.at[:, pl.ds(pl.multiple_of(16 - 16 * ch, 16), main), my_lanes],
            load_sem.at[0],
        )

    def main_input():
        begin = pl.multiple_of((1 - ch) * (half - 16), 16)
        return remote(
            x.at[:, pl.ds(begin, main), :],
            x_ext.at[:, pl.ds(pl.multiple_of(16 * ch, 16), main), my_lanes],
            in_send,
            in_recv,
            y_peer,
        )

    def halo_up(s):
        return remote(
            x.at[:, local_rows - 16 : local_rows, :],
            x_ext.at[:, 0:16, my_lanes],
            halo_send.at[0],
            halo_recv.at[s],
            (batch, up_pos, 0),
        )

    def halo_down(s):
        return remote(
            x.at[:, 0:16, :],
            x_ext.at[:, ext - 16 : ext, my_lanes],
            halo_send.at[1],
            halo_recv.at[s],
            (batch, down_pos, 1),
        )

    def piece_rows(count):
        return -(-(count // plane) // 16) * 16

    def piece_at(count, bb, zz, cc):
        size = piece_rows(count)
        start = ((bb * far_count + zz) * 2 + cc) * size
        if size * plane != count:
            start = jnp.minimum(start, count - size)
        return pl.ds(pl.multiple_of(start, 16), size)

    class Fetch:
        def __init__(self, number, src, dst, lanes):
            self.number, self.src, self.dst, self.lanes = number, src, dst, lanes
            self.count = src.shape[0]

        def at(self, ref, bb, zz, cc):
            return ref.at[piece_at(self.count, bb, zz, cc), self.lanes]

        def over_y(self):
            return remote(
                self.at(self.src, batch, z, core),
                self.at(self.dst, batch, z, core),
                y1_send.at[self.number],
                y1_recv.at[self.number],
                y_peer,
            )

        def over_z(self, r):
            there = lax.rem(z + order[r], far_count)
            part = self.at(self.dst, batch, z, core)
            return remote(
                part, part, z1_send.at[self.number, r], z1_recv.at[self.number, r], (batch, there * 2 + core, ch)
            )

        def source(self, r):
            if r == 0:
                return z
            return lax.rem(z + far_count - order[r - 1], far_count)

        def over_x(self, r):
            part = self.at(self.dst, batch, self.source(r), core)
            return remote(part, part, x1_send.at[self.number, r], x1_recv.at[self.number, r], x_peer)

        def over_core(self, r, bb):
            part = self.at(self.dst, batch if bb == 0 else 1 - batch, self.source(r), core)
            return remote(
                part, part, c1_send.at[self.number, bb, r], c1_recv.at[self.number, bb, r], first.core_peer
            )

        def begin(self):
            self.over_x(0).start()
            for r in range(min(2, far_count - 1)):
                self.over_z(r).start()
            self.over_core(0, 0).start()

        def step(self, r):
            self.over_z(r).wait_recv()
            if r + 2 < far_count - 1:
                self.over_z(r + 2).start()
            self.over_x(r + 1).start()
            self.over_core(r + 1, 0).start()

        def end(self):
            for r in range(far_count):
                self.over_x(r).wait_recv()
                self.over_core(r, 1).start()

        def done(self):
            for r in range(far_count):
                for bb in range(2):
                    self.over_core(r, bb).wait_recv()

        def drain(self):
            self.over_y().wait_send()
            for r in range(far_count - 1):
                self.over_z(r).wait_send()
            for r in range(far_count):
                self.over_x(r).wait_send()
                for bb in range(2):
                    self.over_core(r, bb).wait_send()

    order = [1, 3, 2] if far_count == 4 else list(range(1, far_count))
    fetch1 = [
        Fetch(c, w1, w1x, slice(c * chunk, (c + 1) * chunk)) for c in range(local_out // chunk)
    ]
    fetch_p = Fetch(len(fetch1), wp, wpx, slice(0, local_out))

    half2 = w2.shape[0] // 2
    part2 = pl.ds(pl.multiple_of(core * half2, 16), half2)

    def second_y():
        return remote(w2.at[part2], w2x.at[part2], y2_send, y2_recv, y_peer)

    def second_core():
        return remote(w2x.at[part2], w2x.at[part2], c2_send, c2_recv, first.core_peer)

    bins = og.shape[1] // 2

    def og_local():
        at = pl.ds(pl.multiple_of(ch * bins, 16), bins)
        return pltpu.make_async_copy(og.at[:, at, :], ogx.at[:, :, 0:local_out], load_sem.at[1])

    def og_remote():
        at = pl.ds(pl.multiple_of((1 - ch) * bins, 16), bins)
        return remote(og.at[:, at, :], ogx.at[:, :, local_out : 2 * local_out], og_send, og_recv, y_peer)

    def small_copy():
        return remote(small_ref, small_x, small_send, small_recv, y_peer)

    def x_load():
        return pltpu.make_async_copy(x, x_loc, load_sem.at[2])

    tiles = local_out // chunk

    def w_load(i):
        src = w1 if i < tiles else w1x
        c = i % tiles
        return pltpu.make_async_copy(
            src.at[:, c * chunk : (c + 1) * chunk], w_buf.at[i % parts], w_sem.at[i % parts]
        )

    x_load().start()
    own_input().start()
    og_local().start()
    w_load(0).start()
    w_load(1).start()
    meet_peers = first.peers() + [
        (batch, lax.rem(pos + pos_count + 2 * ch - 1, pos_count), 0),
        (batch, lax.rem(pos + pos_count + 2 * ch - 1, pos_count), 1),
    ]
    meet(meet_peers)
    small_copy().start()
    fetch1[0].over_y().start()
    halo_up(ch).start()
    halo_down(ch).start()

    value[...] = jnp.zeros_like(value)
    x_load().wait()
    for m in range(micro_count):

        def add(i, sums):
            part = x_loc[m, pl.ds(pl.multiple_of(i * 64, 64), 64), :].astype(F32).reshape(8, 8, local_in)
            return sums[0] + jnp.sum(part, axis=0), sums[1] + jnp.sum(part * part, axis=0)

        zero = jnp.zeros((8, local_in), F32)
        plain, square = lax.fori_loop(0, local_rows // 64, add, (zero, zero))
        value[2 * m : 2 * m + 1, my_lanes] = jnp.sum(plain, axis=0, keepdims=True)
        value[2 * m + 1 : 2 * m + 2, my_lanes] = jnp.sum(square, axis=0, keepdims=True)
    first.start(0)
    first.start(1)
    fetch1[0].over_y().wait_recv()
    fetch1[0].begin()
    fetch1[1].over_y().start()
    first.start(2)
    fetch1[0].step(0)
    fetch1[1].over_y().wait_recv()
    main_input().start()
    first.start(3)
    for r in range(1, far_count - 2):
        fetch1[0].step(r)
    fetch1[1].begin()
    small_copy().wait_recv()
    first.wait(3)
    scale = 1.0 / total_rows
    for m in range(micro_count):
        center = r_result[2 * m : 2 * m + 1, :] * scale
        square = r_result[2 * m + 1 : 2 * m + 2, :] * scale
        inverse = lax.rsqrt(square - center * center + EPS)
        vec1[m, 0:1, :] = center
        vec1[m, 3:4, :] = inverse
        for source, lanes in ((small_ref, ch), (small_x, 1 - ch)):
            at = pl.ds(pl.multiple_of(lanes * local_in, 128), local_in)
            vec1[m, 1:2, at] = vec1[m, 3:4, at] * source[4:5, 0:local_in]
            vec1[m, 2:3, at] = source[5:6, 0:local_in]
        vec1[m, 4:8, :] = jnp.zeros((4, wide), F32)

    fetch1[0].step(far_count - 2)
    main_input().wait_recv()
    own_input().wait()
    for s in range(2):
        halo_up(s).wait_recv()
    fetch_p.over_y().start()
    second_y().start()
    for r in range(far_count - 3):
        fetch1[1].step(r)

    begin = pos * local_rows + ch * half - 16
    for m in range(micro_count):
        if m == 1:
            fetch1[1].step(far_count - 3)

        @pl.loop(0, ext // 16)
        def _(i):
            at = pl.multiple_of(i * 16, 16)
            v = x_ext[m, pl.ds(at, 16), :].astype(F32)
            act = (v - vec1[m, 0:1, :]) * vec1[m, 1:2, :] + vec1[m, 2:3, :]
            row = begin + at + lax.broadcasted_iota(jnp.int32, v.shape, 0)
            inside = jnp.logical_and(row >= 0, row < pos_count * local_rows)
            hidden = jnp.where(inside, gelu(act), 0.0)
            for b in range(lanes_count):
                scr[b, pl.ds(at, 16), :] = hidden[:, b * 128 : (b + 1) * 128]
                raw[b, pl.ds(at, 16), :] = v[:, b * 128 : (b + 1) * 128]

        @pl.loop(0, pairs // 16)
        def _(i):
            at = pl.multiple_of(i * 16, 16)
            to = pl.ds(pl.multiple_of(m * pairs + at, 16), 16)
            for b in range(lanes_count):
                for d in range(PIECES):
                    h_cat[to, d * wide + b * 128 : d * wide + (b + 1) * 128] = scr[
                        b, pl.ds(16 - RIM + d + 2 * at, 16, stride=2), :
                    ].astype(BF16)
                for e in range(2):
                    xs[e, to, b * 128 : (b + 1) * 128] = raw[
                        b, pl.ds(16 + e + 2 * at, 16, stride=2), :
                    ].astype(BF16)

    def pieces_out():
        copies = [
            pltpu.make_async_copy(h_cat.at[:, d * wide : (d + 1) * wide], hp.at[d], out_sem.at[d])
            for d in range(PIECES)
        ]
        return copies + [pltpu.make_async_copy(xs, xs_out, out_sem.at[PIECES])]

    for copy in pieces_out():
        copy.start()

    def f_copy(i):
        dst = f_own if i < tiles else f_other
        c = i % tiles
        return pltpu.make_async_copy(
            f_buf.at[i % 2], dst.at[:, :, c * chunk : (c + 1) * chunk], f_sem.at[i % 2]
        )

    value2[...] = jnp.zeros_like(value2)

    def conv(i):
        w_load(i).wait()
        if i >= 2:
            f_copy(i - 2).wait()
        c = i % tiles
        source, side = (small_ref, ch) if i < tiles else (small_x, 1 - ch)
        bias = source[0:1, c * chunk : (c + 1) * chunk]
        at = pl.ds(pl.multiple_of(side * local_out + c * chunk, 128), chunk)
        sums = [[0.0, 0.0] for _ in range(micro_count)]
        for e in range(2):
            acc = jnp.dot(
                h_cat[:, e * wide : (e + KW) * wide], w_buf[i % parts], preferred_element_type=F32
            )
            acc += bias
            f_buf[i % 2, e] = acc
            for m in range(micro_count):
                part = acc[m * pairs : (m + 1) * pairs]
                sums[m][0] += jnp.sum(part, axis=0, keepdims=True)
                sums[m][1] += jnp.sum(part * part, axis=0, keepdims=True)
        for m in range(micro_count):
            for k in range(2):
                value2[2 * m + k : 2 * m + k + 1, at] = sums[m][k]
        f_copy(i).start()

    fetch1[0].end()
    conv(0)
    fetch1[0].done()
    w_load(2).start()
    conv(1)
    og_remote().start()
    fetch1[1].step(far_count - 2)
    fetch_p.over_y().wait_recv()
    fetch_p.begin()
    conv(2)
    fetch1[1].end()
    fetch1[1].done()
    w_load(3).start()
    for r in range(far_count - 3):
        fetch_p.step(r)
    conv(3)
    second.start(0)
    fetch_p.step(far_count - 3)
    second.start(1)
    fetch_p.step(far_count - 2)
    second.start(2)
    second_y().wait_recv()
    second_core().start()
    fetch_p.end()
    second.start(3)
    for copy in pieces_out():
        copy.wait()
    fetch_p.done()
    second_core().wait()
    og_local().wait()
    og_remote().wait()
    for f in fetch1 + [fetch_p]:
        f.drain()
    second_y().wait_send()
    main_input().wait_send()
    halo_up(0).wait_send()
    halo_down(0).wait_send()
    small_copy().wait_send()
    f_copy(2).wait()
    f_copy(3).wait()
    second.wait(3)
    for m in range(micro_count):
        for q, (source, side) in enumerate(((small_ref, ch), (small_x, 1 - ch))):
            at = pl.ds(pl.multiple_of(side * local_out, 128), local_out)
            to = slice(q * local_out, (q + 1) * local_out)
            center = s_result[2 * m : 2 * m + 1, at] * scale
            square = s_result[2 * m + 1 : 2 * m + 2, at] * scale
            vec2[m, 0:1, to] = center
            vec2[m, 1:2, to] = lax.rsqrt(square - center * center + EPS)
            vec2[m, 2:5, to] = source[1:4, :]
            vec2[m, 5:8, to] = jnp.zeros((3, local_out), F32)


def head(x, w1, w2, wp, og, small, total_rows):
    micro_count, local_rows, local_in = x.shape
    wide = 2 * local_in
    half = local_rows // 2
    pairs = half // 2
    rows = micro_count * pairs
    ext = half + 32
    local_out = w1.shape[1]
    out = 2 * local_out
    chunk = local_out // 2
    far = lax.axis_size("pos") // 2
    any_space = pl.BlockSpec(memory_space=pl.ANY)
    in_vmem = pl.BlockSpec(memory_space=pltpu.VMEM)
    dma = pltpu.SemaphoreType.DMA
    fetches = local_out // chunk + 1
    return pl.pallas_call(
        functools.partial(head_kernel, total_rows),
        out_shape=(
            jax.ShapeDtypeStruct((PIECES, rows, wide), BF16),
            jax.ShapeDtypeStruct((2, rows, wide), BF16),
            jax.ShapeDtypeStruct((2, rows, local_out), F32),
            jax.ShapeDtypeStruct((2, rows, local_out), F32),
            jax.ShapeDtypeStruct(w1.shape, BF16),
            jax.ShapeDtypeStruct(w2.shape, BF16),
            jax.ShapeDtypeStruct(wp.shape, BF16),
            jax.ShapeDtypeStruct((micro_count, og.shape[1] // 2, out), BF16),
            jax.ShapeDtypeStruct((micro_count, 8, wide), F32),
            jax.ShapeDtypeStruct((micro_count, 8, out), F32),
        ),
        in_specs=[any_space] * 5 + [in_vmem],
        out_specs=(any_space,) * 8 + (in_vmem,) * 2,
        scratch_shapes=[
            pltpu.VMEM((8, local_out), F32),
            pltpu.VMEM((micro_count, local_rows, local_in), BF16),
            pltpu.VMEM((micro_count, ext, wide), BF16),
            pltpu.VMEM((wide // 128, ext, 128), F32),
            pltpu.VMEM((wide // 128, ext, 128), F32),
            pltpu.VMEM((rows, PIECES * wide), BF16),
            pltpu.VMEM((2, rows, wide), BF16),
            pltpu.VMEM((2, KW * wide, chunk), BF16),
            pltpu.VMEM((2, 2, rows, chunk), F32),
            dma((3,)),
            dma((2,)),
            dma((2,)),
            dma((PIECES + 1,)),
            dma,
            dma,
            dma((2,)),
            dma((2,)),
            dma((fetches,)),
            dma((fetches,)),
            dma((fetches, far - 1)),
            dma((fetches, far - 1)),
            dma((fetches, far)),
            dma((fetches, far)),
            dma((fetches, 2, far)),
            dma((fetches, 2, far)),
            dma,
            dma,
            dma,
            dma,
            dma,
            dma,
            dma,
            dma,
        ]
        + Reduce.scratch(wide)
        + Reduce.scratch(out),
        compiler_params=params(collective_id=6, has_side_effects=True),
        name="head",
    )(x, w1, w2, wp, og, small)


class Scatter:
    def __init__(self, reduce, kept, sent, x_in, z_in, y_out, y_in, sems):
        self.reduce, self.kept, self.sent = reduce, kept, sent
        self.x_in, self.z_in, self.y_out, self.y_in = x_in, z_in, y_out, y_in
        self.z_send, self.z_recv, self.y_send, self.y_recv, *self.x_sems = sems
        self.count = reduce.far_count
        self.half = y_in.shape[1]

    @staticmethod
    def scratch(block, width):
        far = lax.axis_size("pos") // 2
        dma = pltpu.SemaphoreType.DMA
        return [
            pltpu.VMEM((far, block, width), BF16),
            pltpu.VMEM((far - 1, block, width), BF16),
            pltpu.VMEM((block, width // 2), BF16),
            pltpu.VMEM((block, width // 2), BF16),
            dma((far - 1,)),
            dma((far - 1,)),
            dma,
            dma,
        ]

    def away(self, r):
        return far_order(self.reduce.z)[r]

    def copy(self, src, dst, send, recv, peer):
        return pltpu.make_async_remote_copy(src, dst, send, recv, device_id=peer, device_id_type=MESH)

    def over_x(self, r):
        zz, me = self.away(r), self.reduce
        peer = (1 - me.batch, me.pos, me.ch)
        return self.copy(self.sent(zz), self.x_in.at[zz], self.x_sems[0].at[zz], self.x_sems[1].at[zz], peer)

    def over_z(self, r):
        zz, me = self.away(r), self.reduce
        peer = (me.batch, self.away(max(r, 1)) * 2 + me.core, me.ch)
        return self.copy(self.x_in.at[zz], self.z_in.at[r], self.z_send.at[r], self.z_recv.at[r], peer)

    def over_y(self):
        me = self.reduce
        return self.copy(self.y_out, self.y_in, self.y_send, self.y_recv, (me.batch, me.pos, 1 - me.ch))

    def send_x(self, r):
        self.over_x(r).start()

    def send_z(self, r):
        zz = self.away(r)
        if self.x_sems:
            self.over_x(r).wait_recv()
            self.x_in[zz] = (self.x_in[zz].astype(F32) + self.kept(zz)[...].astype(F32)).astype(BF16)
        if r < 2:
            self.over_z(r).start()

    def relay(self):
        zz = self.away(2)
        self.over_z(0).wait_recv()
        self.x_in[zz] = (self.x_in[zz].astype(F32) + self.z_in[0].astype(F32)).astype(BF16)
        self.over_z(2).start()

    def send_y(self):
        zz = self.away(3)
        total = self.x_in[zz].astype(F32)
        for r in range(1, 3):
            self.over_z(r).wait_recv()
            total = total + self.z_in[r].astype(F32)
        self.y_out[...] = total[:, self.half :].astype(BF16)
        self.over_y().start()
        return total[:, : self.half]

    def finish(self):
        self.over_y().wait_recv()
        return self.y_in[...].astype(F32)

    def drain(self):
        for r in range(self.count):
            if self.x_sems:
                self.over_x(r).wait_send()
            if r < self.count - 1:
                self.over_z(r).wait_send()
        self.over_y().wait_send()


def far_order(z):
    near = z + 1 - 2 * lax.rem(z, 2)
    return [lax.rem(near + 2, 4), near, lax.rem(z + 2, 4), z]


def middle_kernel(
    scatter,
    total_rows,
    f_own,
    f_other,
    w2_own,
    w2_other,
    wp_own,
    wp_other,
    ogx,
    x,
    vec_ref,
    vec1_ref,
    lim_ref,
    pooled_out,
    gp,
    xa,
    h_other,
    dw2_out,
    dwp_out,
    sum_out,
    extra,
    w2_ref,
    wp_ref,
    first,
    so,
    a2g,
    hid,
    branch,
    diff,
    lg,
    og,
    pooled,
    dwp,
    dw2,
    p_core,
    q_core,
    low32,
    edge_out,
    edge_in,
    h_in,
    h_wide,
    h_stage,
    h_in_sem,
    h_out_sem,
    w_sem,
    f_sem,
    misc_sem,
    gp_sem,
    pooled_sem,
    pooled_send,
    pooled_recv,
    xa_send,
    xa_recv,
    rim_send,
    rim_recv,
    edge_send,
    edge_recv,
    pc_send,
    pc_recv,
    qc_send,
    qc_recv,
    value,
    r_core,
    r_near,
    r_far,
    r_result,
    r_send,
    r_recv,
    x_in,
    x_send,
    x_recv,
):
    reduce = Reduce(value, r_core, r_near, r_far, r_result, (r_send, r_recv))
    batch, pos, ch, core, z = reduce.batch, reduce.pos, reduce.ch, reduce.core, reduce.z
    far_count = reduce.far_count
    pos_count = 2 * far_count
    _, micro_count, pairs, wide = first.shape
    rows = 2 * pairs
    half = wide // 2
    tile = 256
    tiles = wide // tile
    y_peer = (batch, pos, 1 - ch)
    local_rows, local_in = x.shape[1:]
    half_rows = local_rows // 2
    ext = xa.shape[1]
    main = half_rows + 16

    def columns(j):
        return pl.ds(pl.multiple_of(j * tile, tile), tile)

    def natural(j):
        at = lax.rem(j * tile + ch * half, wide)
        return pl.ds(pl.multiple_of(at, tile), tile)

    def remote(src, dst, send, recv, peer):
        return pltpu.make_async_remote_copy(src, dst, send, recv, device_id=peer, device_id_type=MESH)

    def w_copies(kind):
        copies = []
        dst = (w2_ref, wp_ref)[kind]
        for q, src in enumerate(((w2_own, w2_other), (wp_own, wp_other))[kind]):
            for r in range(2):
                at = pl.ds(pl.multiple_of(lax.rem(ch + r, 2) * half, 16), half)
                copies.append(
                    pltpu.make_async_copy(
                        src.at[at, :],
                        dst.at[r * half : (r + 1) * half, q * half : (q + 1) * half],
                        w_sem.at[kind, q, r],
                    )
                )
        return copies

    def f_copies():
        return [
            pltpu.make_async_copy(src, first.at[:, :, :, q * half : (q + 1) * half], f_sem.at[q])
            for q, src in enumerate((f_own, f_other))
        ]

    def og_copy():
        return pltpu.make_async_copy(ogx, og, misc_sem.at[0])

    lanes_in = pl.ds(pl.multiple_of(ch * local_in, 128), local_in)

    def xa_local():
        begin = pl.multiple_of((1 - ch) * (half_rows - 16), 16)
        return pltpu.make_async_copy(
            x.at[:, pl.ds(begin, main), :],
            xa.at[:, pl.ds(pl.multiple_of(16 * ch, 16), main), lanes_in],
            misc_sem.at[1],
        )

    def xa_remote():
        begin = pl.multiple_of(ch * (half_rows - 16), 16)
        return remote(
            x.at[:, pl.ds(begin, main), :],
            xa.at[:, pl.ds(pl.multiple_of(16 * (1 - ch), 16), main), lanes_in],
            xa_send,
            xa_recv,
            y_peer,
        )

    def rim_up(s):
        return remote(
            x.at[:, local_rows - 16 : local_rows, :],
            xa.at[:, 0:16, lanes_in],
            rim_send.at[0],
            rim_recv.at[s],
            (batch, lax.rem(pos + 1, pos_count), 1),
        )

    def rim_down(s):
        return remote(
            x.at[:, 0:16, :],
            xa.at[:, ext - 16 : ext, lanes_in],
            rim_send.at[1],
            rim_recv.at[s],
            (batch, lax.rem(pos + pos_count - 1, pos_count), 0),
        )

    right = (batch, lax.rem(pos + ch, pos_count), 1 - ch)
    left = (batch, lax.rem(pos + pos_count - 1 + ch, pos_count), 1 - ch)
    rim_from = lax.rem(pos + pos_count + 1 - 2 * ch, pos_count)

    for copy in f_copies():
        copy.start()
    for kind in range(2):
        for copy in w_copies(kind):
            copy.start()
    og_copy().start()
    xa_local().start()
    meet(reduce.peers() + [right, left, (batch, rim_from, 0), (batch, rim_from, 1)])
    xa_remote().start()
    rim_up(ch).start()
    rim_down(ch).start()
    value[...] = jnp.zeros_like(value)
    for copy in f_copies():
        copy.wait()

    def normal(m, e, c):
        return (first[e, m, :, c] - vec_ref[m, 0:1, c]) * vec_ref[m, 1:2, c]

    def forward(m):
        @pl.loop(0, tiles)
        def _(j):
            c = columns(j)
            for e in range(2):
                act = normal(m, e, c) * vec_ref[m, 2:3, c] + vec_ref[m, 3:4, c]
                hid[m, e * pairs : (e + 1) * pairs, c] = gelu(act).astype(BF16)

        if m == 0:
            for copy in w_copies(0):
                copy.wait()

        @pl.loop(0, tiles)
        def _(j):
            c = columns(j)
            step = jnp.dot(hid[m], w2_ref[:, c], preferred_element_type=F32)
            even = step[:pairs] + (first[0, m, :, c] + vec_ref[m, 4:5, c])
            odd = step[pairs:] + (first[1, m, :, c] + vec_ref[m, 4:5, c])
            so[m, 0, :, c] = even
            so[m, 1, :, c] = odd
            diff[m, :, c] = (even - odd).astype(BF16)

        if m == 0:
            for copy in w_copies(1):
                copy.wait()
            og_copy().wait()
        limit = lim_ref[m, 0:1, 0:1]
        inverse_limit = 1.0 / limit

        @pl.loop(0, tiles)
        def _(j):
            c = columns(j)
            d = jnp.dot(diff[m], wp_ref[:, c], preferred_element_type=F32)
            t = jnp.tanh(0.5 * d)
            weight_even = 0.5 + 0.5 * t
            weight_odd = 0.5 - 0.5 * t
            even, odd = so[m, 0, :, c], so[m, 1, :, c]
            pooled[m, :, c] = (weight_even * even + weight_odd * odd).astype(BF16)
            clipped = limit * jnp.tanh(og[m, :, c].astype(F32) * inverse_limit)
            lg[m, :, c] = (weight_even * weight_odd * (even - odd) * clipped).astype(BF16)
            so[m, 0, :, c] = weight_even * clipped
            so[m, 1, :, c] = weight_odd * clipped

        pooled_local(m).start()
        pooled_remote(m).start()

    bins_at = pl.ds(pl.multiple_of(ch * pairs, 16), pairs)

    def pooled_local(m):
        return pltpu.make_async_copy(pooled.at[m, :, 0:half], pooled_out.at[m, bins_at], pooled_sem.at[m])

    def pooled_remote(m):
        return remote(
            pooled.at[m, :, half:wide], pooled_out.at[m, bins_at], pooled_send.at[m], pooled_recv.at[m], y_peer
        )

    def pool_back(m):
        @pl.loop(0, tiles)
        def _(j):
            c = columns(j)
            g = lax.dot_general(lg[m], wp_ref[c, :], NT, preferred_element_type=F32)
            even = so[m, 0, :, c] + g
            odd = so[m, 1, :, c] - g
            so[m, 0, :, c] = even
            so[m, 1, :, c] = odd
            low_even, low_odd = even.astype(BF16), odd.astype(BF16)
            branch[m, 0:pairs, c] = low_even
            branch[m, pairs:rows, c] = low_odd
            both = low_even.astype(F32) + low_odd.astype(F32)
            value[3 * m + 2 : 3 * m + 3, natural(j)] = jnp.sum(both, axis=0, keepdims=True)

    def act_back(m):
        @pl.loop(0, tiles)
        def _(j):
            c = columns(j)
            hg = lax.dot_general(branch[m], w2_ref[c, :], NT, preferred_element_type=F32)
            plain, cross = 0.0, 0.0
            for e in range(2):
                normed = normal(m, e, c)
                act = normed * vec_ref[m, 2:3, c] + vec_ref[m, 3:4, c]
                grad = hg[e * pairs : (e + 1) * pairs] * gelu_slope(act)
                a2g[m, e, :, c] = grad
                plain += jnp.sum(grad, axis=0, keepdims=True)
                cross += jnp.sum(grad * normed, axis=0, keepdims=True)
            value[3 * m : 3 * m + 1, natural(j)] = plain
            value[3 * m + 1 : 3 * m + 2, natural(j)] = cross

    blocks = 4 * far_count
    block = wide // blocks

    def product(dst, left, right_side):
        depth = left.shape[0] * left.shape[1]

        @pl.loop(0, tiles)
        def _(j):
            c = columns(j)
            dst[c, :] = lax.dot_general(
                left[:, :, c].reshape(depth, tile),
                right_side[...].reshape(depth, wide),
                TN,
                preferred_element_type=F32,
            ).astype(BF16)

    def block_rows(bb, zz, cc):
        number = lax.rem((bb * far_count + zz) * 2 + cc + ch * (blocks // 2), blocks)
        return pl.ds(pl.multiple_of(number * block, 16), block)

    def core_copies(src, dst, send, recv):
        return [
            remote(
                src.at[block_rows(bb, zz, 1 - core)], dst.at[bb, zz], send.at[bb, zz], recv.at[bb, zz], reduce.core_peer
            )
            for bb in range(2)
            for zz in range(far_count)
        ]

    def add_core(src, dst, sends):
        i = 0
        for bb in range(2):
            for zz in range(far_count):
                sends[i].wait_recv()
                i += 1
                mine = src[block_rows(bb, zz, core), :].astype(F32)
                dst[bb, zz] = (dst[bb, zz].astype(F32) + mine).astype(BF16)

    p_sends = core_copies(dwp, p_core, pc_send, pc_recv) if scatter else []
    q_sends = core_copies(dw2, q_core, qc_send, qc_recv) if scatter else []
    def pool_x(zz):
        return remote(
            p_core.at[1 - batch, zz], x_in.at[zz], x_send.at[zz], x_recv.at[zz], (1 - batch, pos, ch)
        )

    def pool_sum(zz):
        pool_x(zz).wait_recv()
        x_in[zz] = (x_in[zz].astype(F32) + p_core[batch, zz].astype(F32)).astype(BF16)

    def dwp_copy():
        return pltpu.make_async_copy(x_in if scatter else dwp, dwp_out, misc_sem.at[3])

    lanes_count = h_other.shape[2] // 128
    h_count = micro_count * lanes_count
    ext_half = ext // 2
    h_begin = pos * local_rows + (1 - ch) * half_rows - 16

    def h_load(i):
        at = pl.ds(pl.multiple_of(lax.rem(i, lanes_count) * 128, 128), 128)
        slot = lax.rem(i, 2)
        return pltpu.make_async_copy(xa.at[i // lanes_count, :, at], h_in.at[slot], h_in_sem.at[slot])

    def h_store(i):
        at = pl.ds(pl.multiple_of(lax.rem(i, lanes_count) * 128, 128), 128)
        to = pl.ds(pl.multiple_of((i // lanes_count) * pairs, 16), pairs)
        slot = lax.rem(i, 2)
        return pltpu.make_async_copy(h_stage.at[slot], h_other.at[:, to, at], h_out_sem.at[slot])

    def hidden_blocks(low, high):
        @pl.loop(low, high)
        def _(i):
            slot = lax.rem(i, 2)
            m = i // lanes_count
            at = pl.ds(pl.multiple_of(lax.rem(i, lanes_count) * 128, 128), 128)

            @pl.when(i + 1 < h_count)
            def _():
                h_load(i + 1).start()

            h_load(i).wait()

            @pl.when(i >= 2)
            def _():
                h_store(i - 2).wait()

            for part in range(2):
                v = h_in[slot, part * ext_half : (part + 1) * ext_half, :].astype(F32)
                act = (v - vec1_ref[m, 0:1, at]) * vec1_ref[m, 1:2, at] + vec1_ref[m, 2:3, at]
                row = h_begin + part * ext_half + lax.broadcasted_iota(jnp.int32, v.shape, 0)
                inside = jnp.logical_and(row >= 0, row < pos_count * local_rows)
                h_wide[part * ext_half : (part + 1) * ext_half, :] = jnp.where(inside, gelu(act), 0.0)
            for d in range(PIECES):
                h_stage[slot, d] = h_wide[pl.ds(16 - RIM + d, pairs, stride=2), :].astype(BF16)
            h_store(i).start()

    def dw2_copy():
        return pltpu.make_async_copy(q_core if scatter else dw2, dw2_out, misc_sem.at[2])

    for m in range(micro_count):
        forward(m)
    product(dwp, diff, lg)
    for copy in p_sends:
        copy.start()
    for m in range(micro_count):
        pool_back(m)
    if scatter:
        add_core(dwp, p_core, p_sends)
        for zz in range(far_count):
            pool_x(zz).start()
    product(dw2, hid, branch)
    for copy in q_sends:
        copy.start()
    if not scatter:
        dw2_copy().start()
    for m in range(micro_count):
        act_back(m)
    reduce.start(0)
    xa_local().wait()
    xa_remote().wait_recv()
    for s in range(2):
        rim_up(s).wait_recv()
    h_load(0).start()
    quarter = h_count // 4
    hidden_blocks(0, quarter)
    reduce.start(1)
    if scatter:
        add_core(dw2, q_core, q_sends)
        dw2_copy().start()
    hidden_blocks(quarter, 2 * quarter)
    reduce.start(2)
    hidden_blocks(2 * quarter, 3 * quarter)
    reduce.start(3)
    hidden_blocks(3 * quarter, h_count)
    reduce.wait(3)
    sum_out[...] = r_result[...]

    scale = 1.0 / total_rows

    def first_low(m, e, c, n, at):
        plain = r_result[3 * m : 3 * m + 1, n] * scale
        cross = r_result[3 * m + 1 : 3 * m + 2, n] * scale
        normed = (first[e, m, at, c] - vec_ref[m, 0:1, c]) * vec_ref[m, 1:2, c]
        grad = so[m, e, at, c] + vec_ref[m, 1:2, c] * vec_ref[m, 2:3, c] * (
            a2g[m, e, at, c] - plain - normed * cross
        )
        return grad.astype(BF16).astype(F32)

    edge_out[...] = jnp.zeros_like(edge_out)
    for q in range(2):
        c = slice(q * half, (q + 1) * half)
        n = pl.ds(pl.multiple_of(lax.rem(q + ch, 2) * half, 128), half)
        for m in range(micro_count):
            for e in range(2):
                row = 2 * m + e
                top = first_low(m, e, c, n, slice(0, 8))
                bottom = first_low(m, e, c, n, slice(pairs - 8, pairs))
                edge_out[0, row : row + 1, n] = top[0:1]
                edge_out[1, row : row + 1, n] = bottom[7:8]

    def edge_copy(side):
        return remote(
            edge_out.at[side], edge_in.at[1 - side], edge_send.at[side], edge_recv.at[1 - side], (left, right)[side]
        )

    for side in range(2):
        edge_copy(side).start()
    line = pos * 2 + ch
    edge_copy(1).wait_send()
    edge_copy(0).wait_send()
    for side in range(2):
        edge_copy(side).wait_recv()
    keep_before = jnp.where(line > 0, 1.0, 0.0)
    keep_after = jnp.where(line < 2 * pos_count - 1, 1.0, 0.0)
    slots = 2

    def gp_copies(slot, c):
        return [
            pltpu.make_async_copy(
                w2_ref.at[slot * micro_count * pairs : (slot + 1) * micro_count * pairs, d * tile : (d + 1) * tile],
                gp.at[d, :, c],
                gp_sem.at[slot, d],
            )
            for d in range(PIECES)
        ]

    extra[...] = jnp.zeros_like(extra)
    for j in range(tiles):
        c = columns(j)
        n = natural(j)
        slot = j % slots
        if j >= slots:
            for copy in gp_copies(slot, columns(j - slots)):
                copy.wait()
        for m in range(micro_count):
            total = 0.0
            for e in range(2):
                row = 2 * m + e
                low = first_low(m, e, c, n, slice(0, pairs))
                low32[e, 8 : 8 + pairs, :] = low
                low32[e, 7:8, :] = edge_in[0, row : row + 1, n] * keep_before
                low32[e, 8 + pairs : 9 + pairs, :] = edge_in[1, row : row + 1, n] * keep_after
                total += jnp.sum(low, axis=0, keepdims=True)
            extra[2 * micro_count + m : 2 * micro_count + m + 1, n] = total
            begin = slot * micro_count * pairs + m * pairs
            for d in range(PIECES):
                shift = 7 + d // 2
                w2_ref[begin : begin + pairs, d * tile : (d + 1) * tile] = low32[
                    d % 2, shift : shift + pairs, :
                ].astype(BF16)
        for copy in gp_copies(slot, c):
            copy.start()
        if j == 2:
            if scatter:
                for zz in range(far_count):
                    pool_sum(zz)
            dwp_copy().start()
    for j in range(tiles - slots, tiles):
        for copy in gp_copies(j % slots, columns(j)):
            copy.wait()
    for i in range(h_count - 2, h_count):
        h_store(i).wait()
    xa_remote().wait_send()
    rim_up(0).wait_send()
    rim_down(0).wait_send()
    for m in range(micro_count):
        pooled_local(m).wait()
        pooled_remote(m).wait()
    dw2_copy().wait()
    dwp_copy().wait()
    if scatter:
        for zz in range(far_count):
            pool_x(zz).wait_send()
        for copy in p_sends + q_sends:
            copy.wait_send()


def middle(first_own, first_other, weights, og, x, vecs, vec1, limits, total_rows):
    _, micro_count, pairs, half = first_own.shape
    wide = 2 * half
    rows = 2 * pairs
    depth = micro_count * pairs
    local_rows, local_in = x.shape[1:]
    far = lax.axis_size("pos") // 2
    block = wide // (4 * far)
    scatter = block % 16 == 0 and far == 4
    land = block if scatter else 16
    tile = 256
    any_space = pl.BlockSpec(memory_space=pl.ANY)
    in_vmem = pl.BlockSpec(memory_space=pltpu.VMEM)
    dma = pltpu.SemaphoreType.DMA
    return pl.pallas_call(
        functools.partial(middle_kernel, scatter, total_rows),
        out_shape=(
            jax.ShapeDtypeStruct((micro_count, rows, half), BF16),
            jax.ShapeDtypeStruct((PIECES, depth, wide), BF16),
            jax.ShapeDtypeStruct((micro_count, local_rows // 2 + 32, 2 * local_in), BF16),
            jax.ShapeDtypeStruct((PIECES, depth, 2 * local_in), BF16),
            jax.ShapeDtypeStruct((2, far, block, wide) if scatter else (wide, wide), BF16),
            jax.ShapeDtypeStruct((far, block, wide) if scatter else (wide, wide), BF16),
            jax.ShapeDtypeStruct((8, wide), F32),
            jax.ShapeDtypeStruct((8, wide), F32),
        ),
        in_specs=[any_space] * 8 + [in_vmem] * 3,
        out_specs=(any_space,) * 6 + (in_vmem, in_vmem),
        scratch_shapes=[
            pltpu.VMEM((wide, wide), BF16),
            pltpu.VMEM((wide, wide), BF16),
            pltpu.VMEM((2, micro_count, pairs, wide), F32),
            pltpu.VMEM((micro_count, 2, pairs, wide), F32),
            pltpu.VMEM((micro_count, 2, pairs, wide), F32),
            pltpu.VMEM((micro_count, rows, wide), BF16),
            pltpu.VMEM((micro_count, rows, wide), BF16),
            pltpu.VMEM((micro_count, pairs, wide), BF16),
            pltpu.VMEM((micro_count, pairs, wide), BF16),
            pltpu.VMEM((micro_count, pairs, wide), BF16),
            pltpu.VMEM((micro_count, pairs, wide), BF16),
            pltpu.VMEM((wide, wide), BF16),
            pltpu.VMEM((wide, wide), BF16),
            pltpu.VMEM((2, far, land, wide), BF16),
            pltpu.VMEM((2, far, land, wide), BF16),
            pltpu.VMEM((2, pairs + 16, tile), F32),
            pltpu.VMEM((2, 8, wide), F32),
            pltpu.VMEM((2, 8, wide), F32),
            pltpu.VMEM((2, local_rows // 2 + 32, 128), BF16),
            pltpu.VMEM((local_rows // 2 + 32, 128), F32),
            pltpu.VMEM((2, PIECES, pairs, 128), BF16),
            dma((2,)),
            dma((2,)),
            dma((2, 2, 2)),
            dma((2,)),
            dma((4,)),
            dma((2, PIECES)),
            dma((micro_count,)),
            dma((micro_count,)),
            dma((micro_count,)),
            dma,
            dma,
            dma((2,)),
            dma((2,)),
            dma((2,)),
            dma((2,)),
            dma((2, far)),
            dma((2, far)),
            dma((2, far)),
            dma((2, far)),
        ]
        + Reduce.scratch(wide)
        + [pltpu.VMEM((far, land, wide), BF16), dma((far,)), dma((far,))],
        compiler_params=params(collective_id=7, has_side_effects=True),
        name="middle",
    )(first_own, first_other, *weights, og, x, vecs, vec1, limits)


def tail_kernel(
    scatter,
    total_rows,
    hp_own,
    hp_other,
    gp,
    wo,
    wx,
    xs_in,
    dw2,
    dwp,
    vec_ref,
    extra_ref,
    ig,
    dw_out,
    dw2_out,
    dwp_out,
    sum_out,
    g_buf,
    w_buf,
    a1g,
    xs,
    h_buf,
    f_buf,
    dw,
    core_in,
    x_in,
    z_in,
    weave,
    load_sem,
    w_sem,
    h_sem,
    low_send,
    low_recv,
    core_send,
    core_recv,
    x_send,
    x_recv,
    z_send,
    z_recv,
    ig_send,
    ig_recv,
    ig_sem,
    value,
    r_core,
    r_near,
    r_far,
    r_result,
    r_send,
    r_recv,
    k2_buf,
    x2_in,
    z2_in,
    y2_out,
    y2_in,
    z2_send,
    z2_recv,
    y2_send,
    y2_recv,
    x2_send,
    x2_recv,
    x3_in,
    z3_in,
    y3_out,
    y3_in,
    z3_send,
    z3_recv,
    y3_send,
    y3_recv,
):
    reduce = Reduce(value, r_core, r_near, r_far, r_result, (r_send, r_recv))
    batch, pos, ch, core, z = reduce.batch, reduce.pos, reduce.ch, reduce.core, reduce.z
    far_count = reduce.far_count
    chunks, rows_all, chunk = dw.shape
    rows, wide = xs.shape[1:]
    micro_count, pairs = vec_ref.shape[0], rows // vec_ref.shape[0]
    half_rows = 2 * pairs
    out = gp.shape[2]
    local_out = out // 2
    local_in = wide // 2
    tile = w_buf.shape[1]
    cut = h_buf.shape[3]
    per_half = rows_all // 2 // cut
    y_peer = (batch, pos, 1 - ch)
    x_peer = (1 - batch, pos, ch)
    core_peer = reduce.core_peer

    def loads():
        copies = [
            pltpu.make_async_copy(gp.at[2:4, :, 0:local_out], f_buf.at[0:2], load_sem.at[0]),
            pltpu.make_async_copy(xs_in, xs, load_sem.at[1]),
        ]
        for d in range(PIECES):
            copies.append(
                pltpu.make_async_copy(gp.at[d], g_buf.at[:, d * out : (d + 1) * out], load_sem.at[2 + d])
            )
        return copies

    def w_copies(j):
        s = j % 2
        at = slice(j * tile, (j + 1) * tile)
        copies = []
        for k in range(KW):
            for q, src in enumerate((wo, wx)):
                lanes = (KW - 1 - k) * out + q * local_out
                copies.append(
                    pltpu.make_async_copy(
                        src.at[k, at, :], w_buf.at[s, :, lanes : lanes + local_out], w_sem.at[s, 2 * k + q]
                    )
                )
        return copies

    def h_copies(side_half, t):
        number = side_half * per_half + t
        k = number // 2
        at = pl.ds(pl.multiple_of(lax.rem(number, 2) * cut, cut), cut)
        slot = lax.rem(t, 2)
        return [
            pltpu.make_async_copy((hp_own, hp_other)[s].at[k + e, :, at], h_buf.at[slot, 2 * s + e], h_sem.at[slot, 2 * s + e])
            for s in range(2)
            for e in range(2)
        ]

    def low_copy(c):
        return pltpu.make_async_remote_copy(
            gp.at[2:4, :, local_out + c * chunk : local_out + (c + 1) * chunk],
            f_buf.at[2:4, :, c * chunk : (c + 1) * chunk],
            low_send.at[c],
            low_recv.at[c],
            device_id=y_peer,
            device_id_type=MESH,
        )

    second = Scatter(
        reduce,
        lambda zz: k2_buf.at[zz],
        lambda zz: dw2.at[1 - batch, zz],
        x2_in,
        z2_in,
        y2_out,
        y2_in,
        (z2_send, z2_recv, y2_send, y2_recv, x2_send, x2_recv),
    )
    third = Scatter(
        reduce,
        None,
        None,
        x3_in,
        z3_in,
        y3_out,
        y3_in,
        (z3_send, z3_recv, y3_send, y3_recv),
    )

    def third_copy():
        return pltpu.make_async_copy(dwp, x3_in, load_sem.at[3 + PIECES])

    def k2_copy():
        return pltpu.make_async_copy(dw2.at[batch], k2_buf, load_sem.at[2 + PIECES])

    for copy in loads():
        copy.start()
    for copy in w_copies(0):
        copy.start()
    if scatter:
        k2_copy().start()
        third_copy().start()
    meet(reduce.peers())
    low_copy(0).start()
    if scatter:
        for r in range(far_count):
            second.send_x(r)
        third_copy().wait()
        for r in range(far_count):
            third.send_z(r)
    for copy in h_copies(1 - batch, 0):
        copy.start()
    for copy in loads()[1:]:
        copy.wait()
    value[...] = extra_ref[...]

    tiles = wide // tile

    def back(j):
        s = j % 2
        if j + 1 < tiles:
            for copy in w_copies(j + 1):
                copy.start()
        for copy in w_copies(j):
            copy.wait()
        at = slice(j * tile, (j + 1) * tile)
        sums = [[0.0, 0.0] for _ in range(micro_count)]
        for e in range(2):
            acc = lax.dot_general(
                g_buf[:, e * out : (e + KW) * out], w_buf[s], NT, preferred_element_type=F32
            )
            for m in range(micro_count):
                x = xs[e, m * pairs : (m + 1) * pairs, at].astype(F32)
                moved = x - vec_ref[m, 0:1, at]
                normed = moved * vec_ref[m, 3:4, at]
                act = moved * vec_ref[m, 1:2, at] + vec_ref[m, 2:3, at]
                grad = acc[m * pairs : (m + 1) * pairs] * gelu_slope(act)
                a1g[e, m * pairs : (m + 1) * pairs, at] = grad
                sums[m][0] += jnp.sum(grad, axis=0, keepdims=True)
                sums[m][1] += jnp.sum(grad * normed, axis=0, keepdims=True)
        for m in range(micro_count):
            for i in range(2):
                value[2 * m + i : 2 * m + i + 1, at] = sums[m][i]

    block = rows_all // (2 * 2 * far_count)

    def block_rows(side_half, zz, cc):
        return pl.ds(pl.multiple_of(((side_half * far_count + zz) * 2 + cc) * block, 16), block)

    def core_copy(c, kind, side_half, zz):
        return pltpu.make_async_remote_copy(
            dw.at[c, block_rows(side_half, zz, 1 - core)],
            core_in.at[c, kind, zz],
            core_send.at[c, kind, zz],
            core_recv.at[c, kind, zz],
            device_id=core_peer,
            device_id_type=MESH,
        )

    def x_copy(c, zz):
        return pltpu.make_async_remote_copy(
            dw.at[c, block_rows(1 - batch, zz, core)],
            x_in.at[c, zz],
            x_send.at[c, zz],
            x_recv.at[c, zz],
            device_id=x_peer,
            device_id_type=MESH,
        )

    def z_copy(c, r, zz):
        return pltpu.make_async_remote_copy(
            dw.at[c, block_rows(batch, zz, core)],
            z_in.at[c, r],
            z_send.at[c, r],
            z_recv.at[c, r],
            device_id=(batch, away(max(r, 1)) * 2 + core, ch),
            device_id_type=MESH,
        )

    def away(r):
        return far_order(z)[r]

    def weigh(c, kind, side_half, following, hook=None, hook_at=2):
        lanes = slice(c * chunk, (c + 1) * chunk)

        @pl.loop(0, per_half)
        def _(t):
            @pl.when(t + 1 < per_half)
            def _():
                for copy in h_copies(side_half, t + 1):
                    copy.start()

            for copy in h_copies(side_half, t):
                copy.wait()
            slot = lax.rem(t, 2)
            grad = lax.dot_general(
                h_buf[slot].reshape(4 * rows, cut),
                f_buf[:, :, lanes].reshape(4 * rows, chunk),
                TN,
                preferred_element_type=F32,
            )
            at = pl.multiple_of((side_half * per_half + t) * cut, 16)
            dw[c, pl.ds(at, cut), :] = grad.astype(BF16)
            if hook is not None:
                pl.when(t == hook_at)(hook)

        if following is not None:
            for copy in h_copies(following, 0):
                copy.start()
        if scatter:
            for r in range(far_count):
                core_copy(c, kind, side_half, away(r)).start()

    def add_to(c, at, ref, *index):
        dw[c, at, :] = (dw[c, at, :].astype(F32) + ref[index].astype(F32)).astype(BF16)

    def send_x(c):
        if scatter:
            for r in range(far_count):
                zz = away(r)
                core_copy(c, 0, 1 - batch, zz).wait_recv()
                add_to(c, block_rows(1 - batch, zz, core), core_in, c, 0, zz)
                x_copy(c, zz).start()

    def send_z(c):
        if scatter:
            for r in range(far_count):
                zz = away(r)
                core_copy(c, 1, batch, zz).wait_recv()
                x_copy(c, zz).wait_recv()
                at = block_rows(batch, zz, core)
                total = dw[c, at, :].astype(F32) + core_in[c, 1, zz].astype(F32) + x_in[c, zz].astype(F32)
                lanes = slice(c * chunk, (c + 1) * chunk)
                if r < 3:
                    dw[c, at, :] = total.astype(BF16)
                    if r < 2:
                        z_copy(c, r, zz).start()
                else:
                    dw_out[:, lanes] = total

    def relay_z(c):
        if scatter:
            zz = away(2)
            z_copy(c, 0, away(0)).wait_recv()
            add_to(c, block_rows(batch, zz, core), z_in, c, 0)
            z_copy(c, 2, zz).start()

    def finish(c):
        lanes = slice(c * chunk, (c + 1) * chunk)
        if scatter:
            for r in range(1, 3):
                z_copy(c, r, away(r)).wait_recv()
                dw_out[:, lanes] = dw_out[:, lanes] + z_in[c, r].astype(F32)
        else:
            copy = pltpu.make_async_copy(dw.at[c], dw_out.at[:, lanes], load_sem.at[4 + PIECES])
            copy.start()
            copy.wait()

    def ig_copies(m):
        copies = []
        for part in range(2):
            at = pl.ds(pl.multiple_of(ch * half_rows + part * pairs, 16), pairs)
            kept = pl.ds(pl.multiple_of(ch * local_in, 128), local_in)
            sent = pl.ds(pl.multiple_of((1 - ch) * local_in, 128), local_in)
            here = xs.at[part, m * pairs : (m + 1) * pairs]
            copies.append(pltpu.make_async_copy(here.at[:, kept], ig.at[m, at], ig_sem.at[m, part]))
            copies.append(
                pltpu.make_async_remote_copy(
                    here.at[:, sent],
                    ig.at[m, at],
                    ig_send.at[m, part],
                    ig_recv.at[m, part],
                    device_id=y_peer,
                    device_id_type=MESH,
                )
            )
        return copies

    def input_grad(m):
        scale = 1.0 / total_rows

        @pl.loop(0, wide // 128)
        def _(b):
            at = pl.ds(pl.multiple_of(b * 128, 128), 128)
            plain = r_result[2 * m : 2 * m + 1, at] * scale
            cross = r_result[2 * m + 1 : 2 * m + 2, at] * scale
            inverse = vec_ref[m, 3:4, at]
            for e in range(2):
                x = xs[e, m * pairs : (m + 1) * pairs, at].astype(F32)
                normed = (x - vec_ref[m, 0:1, at]) * inverse
                grad = a1g[e, m * pairs : (m + 1) * pairs, at]
                weave[pl.ds(e, pairs, stride=2), :] = vec_ref[m, 1:2, at] * (grad - plain - normed * cross)
            for part in range(2):
                xs[part, m * pairs : (m + 1) * pairs, at] = weave[part * pairs : (part + 1) * pairs, :].astype(BF16)

        for copy in ig_copies(m):
            copy.start()

    for j in range(3):
        back(j)
    if scatter:
        third.relay()
    loads()[0].wait()
    low_copy(0).wait_recv()
    low_copy(1).start()
    weigh(0, 0, 1 - batch, 1 - batch)
    send_x(0)
    back(3)
    if scatter:
        k2_copy().wait()
        for r in range(far_count):
            second.send_z(r)
    low_copy(1).wait_recv()
    low_copy(2).start()
    back(4)
    reduce.start(0)
    weigh(1, 0, 1 - batch, batch)
    reduce.start(1)
    send_x(1)
    if scatter:
        second.relay()
    weigh(0, 1, batch, 1 - batch)
    send_z(0)
    low_copy(2).wait_recv()
    weigh(2, 0, 1 - batch, batch)
    send_x(2)
    reduce.start(2)
    relay_z(0)
    weigh(1, 1, batch, batch)
    send_z(1)
    reduce.start(3)
    reduce.wait(3)
    sum_out[...] = r_result[...]
    for m in range(micro_count):
        input_grad(m)
    weigh(2, 1, batch, None)
    relay_z(1)
    if scatter:
        dw2_out[...] = second.send_y()
        dwp_out[...] = third.send_y()
    finish(0)
    send_z(2)
    finish(1)
    relay_z(2)
    finish(2)
    for m in range(micro_count):
        for copy in ig_copies(m):
            copy.wait()
    if scatter:
        dw2_out[...] += second.finish()
        dwp_out[...] += third.finish()
        second.drain()
        third.drain()
    else:
        dw2_out[...] = jnp.zeros_like(dw2_out)
        dwp_out[...] = jnp.zeros_like(dwp_out)
    for c in range(chunks):
        low_copy(c).wait_send()
        if scatter:
            for r in range(far_count):
                zz = away(r)
                core_copy(c, 0, 1 - batch, zz).wait_send()
                core_copy(c, 1, batch, zz).wait_send()
                x_copy(c, zz).wait_send()
                if r < far_count - 1:
                    z_copy(c, r, zz).wait_send()


def tail(pieces, other_pieces, grad_pieces, own, other, x_split, dw2, dwp, vecs, extra, total_rows):
    _, rows, wide = pieces.shape
    micro_count = vecs.shape[0]
    pairs = rows // micro_count
    out = grad_pieces.shape[-1]
    local_out = out // 2
    chunks = 3
    chunk = local_out // chunks
    far = lax.axis_size("pos") // 2
    rows_all = KW * wide
    block = rows_all // (4 * far)
    scatter = block % 16 == 0 and far == 4
    tile = 256
    land = block if scatter else 16
    block2 = dw2.shape[2] if scatter else 16
    any_space = pl.BlockSpec(memory_space=pl.ANY)
    in_vmem = pl.BlockSpec(memory_space=pltpu.VMEM)
    dma = pltpu.SemaphoreType.DMA
    return pl.pallas_call(
        functools.partial(tail_kernel, scatter, total_rows),
        out_shape=(
            jax.ShapeDtypeStruct((micro_count, 4 * pairs, wide // 2), BF16),
            jax.ShapeDtypeStruct((block, local_out) if scatter else (rows_all, local_out), F32 if scatter else BF16),
            jax.ShapeDtypeStruct((block2, local_out), F32),
            jax.ShapeDtypeStruct((block2, local_out), F32),
            jax.ShapeDtypeStruct((8, out), F32),
        ),
        in_specs=[any_space] * 8 + [in_vmem] * 2,
        out_specs=(any_space, in_vmem if scatter else any_space, in_vmem, in_vmem, in_vmem),
        scratch_shapes=[
            pltpu.VMEM((rows, PIECES * out), BF16),
            pltpu.VMEM((2, tile, KW * out), BF16),
            pltpu.VMEM((2, rows, wide), F32),
            pltpu.VMEM((2, rows, wide), BF16),
            pltpu.VMEM((2, 4, rows, wide // 2), BF16),
            pltpu.VMEM((4, rows, local_out), BF16),
            pltpu.VMEM((chunks, rows_all, chunk), BF16),
            pltpu.VMEM((chunks, 2, far, land, chunk), BF16),
            pltpu.VMEM((chunks, far, land, chunk), BF16),
            pltpu.VMEM((chunks, far - 1, land, chunk), BF16),
            pltpu.VMEM((2 * pairs, 128), F32),
            dma((5 + PIECES,)),
            dma((2, 2 * KW)),
            dma((2, 4)),
            dma((chunks,)),
            dma((chunks,)),
            dma((chunks, 2, far)),
            dma((chunks, 2, far)),
            dma((chunks, far)),
            dma((chunks, far)),
            dma((chunks, far - 1)),
            dma((chunks, far - 1)),
            dma((micro_count, 2)),
            dma((micro_count, 2)),
            dma((micro_count, 2)),
        ]
        + Reduce.scratch(out)
        + [pltpu.VMEM((far, block2, out), BF16)]
        + Scatter.scratch(block2, out)
        + [dma((far,)), dma((far,))]
        + Scatter.scratch(block2, out),
        compiler_params=params(collective_id=5, has_side_effects=True),
        name="tail",
    )(
        pieces,
        other_pieces,
        grad_pieces,
        own.reshape(KW, wide, local_out),
        other.reshape(KW, wide, local_out),
        x_split,
        dw2,
        dwp,
        vecs,
        extra,
    )


def collect_kernel(part, sums3, *refs):
    count = 5
    sources, targets, vectors = refs[:count], refs[count : 2 * count], refs[2 * count : 2 * count + 6]
    held, sems = refs[2 * count + 6 : -1], refs[-1]
    loads = [pltpu.make_async_copy(a, h, sems.at[0, i]) for i, (a, h) in enumerate(zip(sources, held))]
    copies = [pltpu.make_async_copy(h, b, sems.at[1, i]) for i, (h, b) in enumerate(zip(held, targets))]
    for load in loads:
        load.start()
    for load, copy in zip(loads, copies):
        load.wait()
        copy.start()
    ch = lax.axis_index("ch")
    micro_count = 2

    def put(dst, ref, rows):
        width = dst.shape[0]
        at = pl.ds(pl.multiple_of(ch * width, 128), width)
        total = ref[rows[0] : rows[0] + 1, at]
        for r in rows[1:]:
            total = total + ref[r : r + 1, at]
        dst[...] = total.reshape(width)

    ms = range(micro_count)
    put(vectors[0], part, [2 * m + 1 for m in ms])
    put(vectors[1], part, [2 * m for m in ms])
    put(vectors[2], part, [2 * micro_count + m for m in ms])
    put(vectors[3], sums3, [3 * m + 1 for m in ms])
    put(vectors[4], sums3, [3 * m for m in ms])
    put(vectors[5], sums3, [3 * m + 2 for m in ms])
    for copy in copies:
        copy.wait()


def collect(arrays, part, sums3, local_in, local_out):
    any_space = pl.BlockSpec(memory_space=pl.ANY)
    in_vmem = pl.BlockSpec(memory_space=pltpu.VMEM)
    widths = [local_in, local_in] + [local_out] * 4
    return pl.pallas_call(
        collect_kernel,
        out_shape=tuple(jax.ShapeDtypeStruct(v.shape, v.dtype) for v in arrays)
        + tuple(jax.ShapeDtypeStruct((w,), F32) for w in widths),
        in_specs=[in_vmem] * 2 + [any_space] * 5,
        out_specs=(any_space,) * 5 + (in_vmem,) * 6,
        scratch_shapes=[pltpu.VMEM(v.shape, v.dtype) for v in arrays] + [pltpu.SemaphoreType.DMA((2, 5))],
        compiler_params=params(),
        name="collect",
    )(part, sums3, *arrays)


def local(
    section_input,
    norm1_gain,
    norm1_bias,
    conv1_weight,
    conv1_bias,
    norm2_gain,
    norm2_bias,
    conv2_weight,
    conv2_bias,
    pool_weight,
    out_grad,
    clip_table,
    clip_index,
):
    micro_count, seq_count, local_rows, local_in = section_input.shape
    batch_count, pos_count, ch_count = (lax.axis_size(a) for a in ("batch", "pos", "ch"))
    batch, pos, ch = (lax.axis_index(a) for a in ("batch", "pos", "ch"))
    total_rows = seq_count * local_rows * batch_count * pos_count
    wide_in = 2 * local_in
    local_out = conv1_weight.shape[1]
    wide_out = 2 * local_out
    half = local_rows // 2
    pairs = half // 2
    plane = batch_count * pos_count
    spot = batch * pos_count + pos
    swap = [(0, 1), (1, 0)]
    is_low = ch == 0

    def other_ch(v):
        return lax.ppermute(v, "ch", swap)

    def natural(own, other, axis):
        return jnp.where(
            is_low,
            jnp.concatenate([own, other], axis=axis),
            jnp.concatenate([other, own], axis=axis),
        )

    x = section_input.reshape(micro_count, local_rows, local_in)

    def own_first(v):
        return jnp.where(
            is_low, v, jnp.concatenate([v[..., local_out:], v[..., :local_out]], axis=-1)
        )

    to_natural = own_first
    bins = local_rows // 2
    mine = bins // 2
    small = jnp.stack([conv1_bias, norm2_gain, norm2_bias, conv2_bias])
    small = jnp.concatenate(
        [small, jnp.pad(jnp.stack([norm1_gain, norm1_bias]), ((0, 2), (0, local_out - local_in)))]
    )
    (
        pieces,
        x_split,
        first_own,
        first_other,
        w1_other,
        w2_other,
        wp_other,
        og_full,
        vec1,
        vec2,
    ) = head(
        x,
        conv1_weight,
        conv2_weight,
        pool_weight,
        out_grad.reshape(micro_count, bins, local_out),
        small,
        total_rows,
    )
    first_own = first_own.reshape(2, micro_count, pairs, local_out)
    first_other = first_other.reshape(2, micro_count, pairs, local_out)
    table_pos = jnp.arange(clip_table.shape[0], dtype=jnp.int32)
    limit = jnp.sum(jnp.where(table_pos[None] == clip_index[:, None], clip_table[None], 0.0), axis=1)
    limits = jnp.broadcast_to(limit[:, None, None], (micro_count, 8, 128))

    section_output, grad_pieces, _, other_pieces, dw2, dwp, sums3, extra = middle(
        first_own,
        first_other,
        (conv2_weight, w2_other, pool_weight, wp_other),
        og_full,
        x,
        vec2,
        vec1,
        limits,
        total_rows,
    )
    whole_two, whole_pool = dw2, dwp
    input_grad, dw1, dw2, dwp, part = tail(
        pieces, other_pieces, grad_pieces, conv1_weight, w1_other, x_split, dw2, dwp, vec1, extra, total_rows
    )

    def scatter(v):
        return lax.psum_scatter(v, ("batch", "pos"), scatter_dimension=0, tiled=True).astype(F32)

    def fold(v):
        v = jnp.where(is_low, v, jnp.concatenate([v[local_out:], v[:local_out]], axis=0))
        away = other_ch(v[:, local_out:])
        return scatter((v[:, :local_out].astype(F32) + away.astype(F32)).astype(BF16))

    if whole_pool.ndim == 2:
        dw2, dwp = fold(whole_two), fold(whole_pool)
    if dw1.shape[0] != KW * wide_in // plane:
        dw1 = scatter(dw1)
    section_output, input_grad, dw1, dw2, dwp, *vectors = collect(
        (section_output, input_grad, dw1, dw2, dwp), part, sums3, local_in, local_out
    )
    return (
        section_output.reshape(micro_count, seq_count, bins, local_out),
        input_grad.reshape(section_input.shape),
        vectors[0],
        vectors[1],
        dw1,
        vectors[2],
        vectors[3],
        vectors[4],
        dw2,
        vectors[5],
        dwp,
    )


def solution(mesh):
    placed = (
        P(None, "batch", "pos", "ch"),
        P("ch"),
        P("ch"),
        P(None, "ch"),
        P("ch"),
        P("ch"),
        P("ch"),
        P(None, "ch"),
        P("ch"),
        P(None, "ch"),
        P(None, "batch", "pos", "ch"),
        P(),
        P(),
    )
    return jax.shard_map(
        local,
        mesh=mesh,
        in_specs=placed,
        out_specs=(
            P(None, "batch", "pos", "ch"),
            P(None, "batch", "pos", "ch"),
            P("ch"),
            P("ch"),
            P(("batch", "pos"), "ch"),
            P("ch"),
            P("ch"),
            P("ch"),
            P(("batch", "pos"), "ch"),
            P("ch"),
            P(("batch", "pos"), "ch"),
        ),
        check_vma=False,
    )
```

```python
import functools

import jax
import jax.numpy as jnp
from jax import lax
from jax.experimental import pallas as pl
from jax.experimental.pallas import tpu as pltpu
from jax.sharding import PartitionSpec as P

KW = 5
RIM = KW // 2
PIECES = KW + 1
EPS = 1e-05
MESH = pl.DeviceIdType.MESH
C0 = 0.7978845608028654
C1 = 0.044715
F32 = jnp.float32
BF16 = jnp.bfloat16
VMEM_LIMIT = 60 * 1024 * 1024

NT = (((1,), (1,)), ((), ()))
TN = (((0,), (0,)), ((), ()))


def params(**kw):
    return pltpu.CompilerParams(vmem_limit_bytes=VMEM_LIMIT, **kw)


def gelu(u):
    return 0.5 * u * (1.0 + jnp.tanh(C0 * (u + C1 * u * u * u)))


def gelu_slope(u):
    square = u * u
    t = jnp.tanh(C0 * (u + C1 * square * u))
    return 0.5 * (1.0 + t) + 0.5 * u * (1.0 - t * t) * (C0 + (3.0 * C0 * C1) * square)


class Reduce:
    def __init__(self, value, core_in, near, far, result, sems):
        self.value, self.core_in, self.near, self.far, self.result = value, core_in, near, far, result
        self.send, self.recv = sems
        self.batch, self.pos, self.ch = (lax.axis_index(a) for a in ("batch", "pos", "ch"))
        self.core = lax.rem(self.pos, 2)
        self.z = self.pos // 2
        self.far_count = lax.axis_size("pos") // 2
        half = value.shape[1] // 2
        self.mine = pl.ds(pl.multiple_of(self.core * half, half), half)
        self.away = pl.ds(pl.multiple_of((1 - self.core) * half, half), half)
        self.me = self.batch * 2 + self.ch
        self.core_peer = (self.batch, self.z * 2 + 1 - self.core, self.ch)
        self.near_peers = []
        for step in range(1, 4):
            other = lax.rem(self.me + step, 4)
            self.near_peers.append((other // 2, self.pos, lax.rem(other, 2)))
        self.far_peers = []
        for step in range(1, self.far_count):
            other = lax.rem(self.z + step, self.far_count)
            self.far_peers.append((self.batch, other * 2 + self.core, self.ch))

    @staticmethod
    def scratch(width):
        far = lax.axis_size("pos") // 2
        count = 2 + 3 + far - 1
        return [
            pltpu.VMEM((8, width), F32),
            pltpu.VMEM((8, width // 2), F32),
            pltpu.VMEM((4, 8, width // 2), F32),
            pltpu.VMEM((far, 8, width // 2), F32),
            pltpu.VMEM((8, width), F32),
            pltpu.SemaphoreType.DMA((count,)),
            pltpu.SemaphoreType.DMA((count,)),
        ]

    def peers(self):
        return [self.core_peer] + self.near_peers + self.far_peers

    def copy(self, i, src, dst, peer):
        return pltpu.make_async_remote_copy(
            src, dst, self.send.at[i], self.recv.at[i], device_id=peer, device_id_type=MESH
        )

    def copies(self, stage):
        if stage == 0:
            return [self.copy(0, self.value.at[:, self.away], self.core_in, self.core_peer)]
        if stage == 1:
            slot = self.near.at[self.me]
            return [self.copy(1 + i, slot, slot, p) for i, p in enumerate(self.near_peers)]
        if stage == 2:
            slot = self.far.at[self.z]
            return [self.copy(4 + i, slot, slot, p) for i, p in enumerate(self.far_peers)]
        part = self.result.at[:, self.mine]
        return [self.copy(3 + self.far_count, part, part, self.core_peer)]

    def wait(self, stage):
        for copy in self.copies(stage):
            copy.wait()

    def start(self, stage):
        if stage == 1:
            self.wait(0)
            self.near[pl.ds(self.me, 1)] = (self.value[:, self.mine] + self.core_in[...])[None]
        if stage == 2:
            self.wait(1)
            total = (self.near[0] + self.near[1]) + (self.near[2] + self.near[3])
            self.far[pl.ds(self.z, 1)] = total[None]
        if stage == 3:
            self.wait(2)
            total = self.far[0]
            for i in range(1, self.far_count):
                total = total + self.far[i]
            self.result[:, self.mine] = total
        for copy in self.copies(stage):
            copy.start()


def meet(peers):
    barrier = pltpu.get_barrier_semaphore()
    for peer in peers:
        pl.semaphore_signal(barrier, inc=1, device_id=peer, device_id_type=MESH)
    pl.semaphore_wait(barrier, len(peers))


def reduce_kernel(v_ref, o_ref, *scratch):
    value, core_in, near, far, result, send, recv = scratch
    reduce = Reduce(value, core_in, near, far, result, (send, recv))
    value[...] = v_ref[...]
    meet(reduce.peers())
    for stage in range(4):
        reduce.start(stage)
    reduce.wait(3)
    o_ref[...] = result[...]


def reduce_all(values, collective_id):
    rows, width = values.shape
    total = pl.pallas_call(
        reduce_kernel,
        out_shape=jax.ShapeDtypeStruct((8, width), F32),
        in_specs=[pl.BlockSpec(memory_space=pltpu.VMEM)],
        out_specs=pl.BlockSpec(memory_space=pltpu.VMEM),
        scratch_shapes=Reduce.scratch(width),
        compiler_params=params(collective_id=collective_id, has_side_effects=True),
        name="reduce",
    )(jnp.pad(values, ((0, 8 - rows), (0, 0))))
    return total[:rows]


def head_kernel(
    total_rows,
    x,
    w1,
    w2,
    wp,
    og,
    small_ref,
    hp,
    xs_out,
    f_own,
    f_other,
    w1x,
    w2x,
    wpx,
    ogx,
    vec1,
    vec2,
    small_x,
    x_loc,
    x_ext,
    scr,
    raw,
    h_cat,
    xs,
    w_buf,
    f_buf,
    load_sem,
    w_sem,
    f_sem,
    out_sem,
    in_send,
    in_recv,
    halo_send,
    halo_recv,
    y1_send,
    y1_recv,
    z1_send,
    z1_recv,
    x1_send,
    x1_recv,
    c1_send,
    c1_recv,
    y2_send,
    y2_recv,
    c2_send,
    c2_recv,
    og_send,
    og_recv,
    small_send,
    small_recv,
    value,
    r_core,
    r_near,
    r_far,
    r_result,
    r_send,
    r_recv,
    value2,
    s_core,
    s_near,
    s_far,
    s_result,
    s_send,
    s_recv,
):
    first = Reduce(value, r_core, r_near, r_far, r_result, (r_send, r_recv))
    second = Reduce(value2, s_core, s_near, s_far, s_result, (s_send, s_recv))
    batch, pos, ch, core, z = first.batch, first.pos, first.ch, first.core, first.z
    far_count = first.far_count
    pos_count = 2 * far_count
    plane = 2 * pos_count
    micro_count, local_rows, local_in = x.shape
    wide = 2 * local_in
    half = local_rows // 2
    pairs = half // 2
    rows = micro_count * pairs
    ext = half + 32
    main = half + 16
    local_out = w1.shape[1]
    parts, chunk = w_buf.shape[0], w_buf.shape[2]
    lanes_count = wide // 128
    y_peer = (batch, pos, 1 - ch)
    x_peer = (1 - batch, pos, ch)
    up_pos = lax.rem(pos + 1, pos_count)
    down_pos = lax.rem(pos + pos_count - 1, pos_count)

    def remote(src, dst, send, recv, peer):
        return pltpu.make_async_remote_copy(src, dst, send, recv, device_id=peer, device_id_type=MESH)

    my_lanes = pl.ds(pl.multiple_of(ch * local_in, 128), local_in)

    def own_input():
        begin = pl.multiple_of(ch * (half - 16), 16)
        return pltpu.make_async_copy(
            x.at[:, pl.ds(begin, main), :],
            x_ext.at[:, pl.ds(pl.multiple_of(16 - 16 * ch, 16), main), my_lanes],
            load_sem.at[0],
        )

    def main_input():
        begin = pl.multiple_of((1 - ch) * (half - 16), 16)
        return remote(
            x.at[:, pl.ds(begin, main), :],
            x_ext.at[:, pl.ds(pl.multiple_of(16 * ch, 16), main), my_lanes],
            in_send,
            in_recv,
            y_peer,
        )

    def halo_up(s):
        return remote(
            x.at[:, local_rows - 16 : local_rows, :],
            x_ext.at[:, 0:16, my_lanes],
            halo_send.at[0],
            halo_recv.at[s],
            (batch, up_pos, 0),
        )

    def halo_down(s):
        return remote(
            x.at[:, 0:16, :],
            x_ext.at[:, ext - 16 : ext, my_lanes],
            halo_send.at[1],
            halo_recv.at[s],
            (batch, down_pos, 1),
        )

    def piece_rows(count):
        return -(-(count // plane) // 16) * 16

    def piece_at(count, bb, zz, cc):
        size = piece_rows(count)
        start = ((bb * far_count + zz) * 2 + cc) * size
        if size * plane != count:
            start = jnp.minimum(start, count - size)
        return pl.ds(pl.multiple_of(start, 16), size)

    class Fetch:
        def __init__(self, number, src, dst, lanes):
            self.number, self.src, self.dst, self.lanes = number, src, dst, lanes
            self.count = src.shape[0]

        def at(self, ref, bb, zz, cc):
            return ref.at[piece_at(self.count, bb, zz, cc), self.lanes]

        def over_y(self):
            return remote(
                self.at(self.src, batch, z, core),
                self.at(self.dst, batch, z, core),
                y1_send.at[self.number],
                y1_recv.at[self.number],
                y_peer,
            )

        def over_z(self, r):
            there = lax.rem(z + order[r], far_count)
            part = self.at(self.dst, batch, z, core)
            return remote(
                part, part, z1_send.at[self.number, r], z1_recv.at[self.number, r], (batch, there * 2 + core, ch)
            )

        def source(self, r):
            if r == 0:
                return z
            return lax.rem(z + far_count - order[r - 1], far_count)

        def over_x(self, r):
            part = self.at(self.dst, batch, self.source(r), core)
            return remote(part, part, x1_send.at[self.number, r], x1_recv.at[self.number, r], x_peer)

        def over_core(self, r, bb):
            part = self.at(self.dst, batch if bb == 0 else 1 - batch, self.source(r), core)
            return remote(
                part, part, c1_send.at[self.number, bb, r], c1_recv.at[self.number, bb, r], first.core_peer
            )

        def begin(self):
            self.over_x(0).start()
            for r in range(min(2, far_count - 1)):
                self.over_z(r).start()
            self.over_core(0, 0).start()

        def step(self, r):
            self.over_z(r).wait_recv()
            if r + 2 < far_count - 1:
                self.over_z(r + 2).start()
            self.over_x(r + 1).start()
            self.over_core(r + 1, 0).start()

        def end(self):
            for r in range(far_count):
                self.over_x(r).wait_recv()
                self.over_core(r, 1).start()

        def done(self):
            for r in range(far_count):
                for bb in range(2):
                    self.over_core(r, bb).wait_recv()

        def drain(self):
            self.over_y().wait_send()
            for r in range(far_count - 1):
                self.over_z(r).wait_send()
            for r in range(far_count):
                self.over_x(r).wait_send()
                for bb in range(2):
                    self.over_core(r, bb).wait_send()

    order = [1, 3, 2] if far_count == 4 else list(range(1, far_count))
    fetch1 = [
        Fetch(c, w1, w1x, slice(c * chunk, (c + 1) * chunk)) for c in range(local_out // chunk)
    ]
    fetch_p = Fetch(len(fetch1), wp, wpx, slice(0, local_out))

    half2 = w2.shape[0] // 2
    part2 = pl.ds(pl.multiple_of(core * half2, 16), half2)

    def second_y():
        return remote(w2.at[part2], w2x.at[part2], y2_send, y2_recv, y_peer)

    def second_core():
        return remote(w2x.at[part2], w2x.at[part2], c2_send, c2_recv, first.core_peer)

    bins = og.shape[1] // 2

    def og_local():
        at = pl.ds(pl.multiple_of(ch * bins, 16), bins)
        return pltpu.make_async_copy(og.at[:, at, :], ogx.at[:, :, 0:local_out], load_sem.at[1])

    def og_remote():
        at = pl.ds(pl.multiple_of((1 - ch) * bins, 16), bins)
        return remote(og.at[:, at, :], ogx.at[:, :, local_out : 2 * local_out], og_send, og_recv, y_peer)

    def small_copy():
        return remote(small_ref, small_x, small_send, small_recv, y_peer)

    def x_load():
        return pltpu.make_async_copy(x, x_loc, load_sem.at[2])

    tiles = local_out // chunk

    def w_load(i):
        src = w1 if i < tiles else w1x
        c = i % tiles
        return pltpu.make_async_copy(
            src.at[:, c * chunk : (c + 1) * chunk], w_buf.at[i % parts], w_sem.at[i % parts]
        )

    x_load().start()
    own_input().start()
    og_local().start()
    w_load(0).start()
    w_load(1).start()
    meet_peers = first.peers() + [
        (batch, lax.rem(pos + pos_count + 2 * ch - 1, pos_count), 0),
        (batch, lax.rem(pos + pos_count + 2 * ch - 1, pos_count), 1),
    ]
    meet(meet_peers)
    small_copy().start()
    fetch1[0].over_y().start()
    halo_up(ch).start()
    halo_down(ch).start()

    value[...] = jnp.zeros_like(value)
    x_load().wait()
    for m in range(micro_count):

        def add(i, sums):
            part = x_loc[m, pl.ds(pl.multiple_of(i * 64, 64), 64), :].astype(F32).reshape(8, 8, local_in)
            return sums[0] + jnp.sum(part, axis=0), sums[1] + jnp.sum(part * part, axis=0)

        zero = jnp.zeros((8, local_in), F32)
        plain, square = lax.fori_loop(0, local_rows // 64, add, (zero, zero))
        value[2 * m : 2 * m + 1, my_lanes] = jnp.sum(plain, axis=0, keepdims=True)
        value[2 * m + 1 : 2 * m + 2, my_lanes] = jnp.sum(square, axis=0, keepdims=True)
    first.start(0)
    first.start(1)
    fetch1[0].over_y().wait_recv()
    fetch1[0].begin()
    fetch1[1].over_y().start()
    first.start(2)
    fetch1[0].step(0)
    fetch1[1].over_y().wait_recv()
    main_input().start()
    first.start(3)
    for r in range(1, far_count - 2):
        fetch1[0].step(r)
    fetch1[1].begin()
    small_copy().wait_recv()
    first.wait(3)
    scale = 1.0 / total_rows
    for m in range(micro_count):
        center = r_result[2 * m : 2 * m + 1, :] * scale
        square = r_result[2 * m + 1 : 2 * m + 2, :] * scale
        inverse = lax.rsqrt(square - center * center + EPS)
        vec1[m, 0:1, :] = center
        vec1[m, 3:4, :] = inverse
        for source, lanes in ((small_ref, ch), (small_x, 1 - ch)):
            at = pl.ds(pl.multiple_of(lanes * local_in, 128), local_in)
            vec1[m, 1:2, at] = vec1[m, 3:4, at] * source[4:5, 0:local_in]
            vec1[m, 2:3, at] = source[5:6, 0:local_in]
        vec1[m, 4:8, :] = jnp.zeros((4, wide), F32)

    fetch1[0].step(far_count - 2)
    main_input().wait_recv()
    own_input().wait()
    for s in range(2):
        halo_up(s).wait_recv()
    fetch_p.over_y().start()
    second_y().start()
    for r in range(far_count - 3):
        fetch1[1].step(r)

    begin = pos * local_rows + ch * half - 16
    for m in range(micro_count):
        if m == 1:
            fetch1[1].step(far_count - 3)

        @pl.loop(0, ext // 16)
        def _(i):
            at = pl.multiple_of(i * 16, 16)
            v = x_ext[m, pl.ds(at, 16), :].astype(F32)
            act = (v - vec1[m, 0:1, :]) * vec1[m, 1:2, :] + vec1[m, 2:3, :]
            row = begin + at + lax.broadcasted_iota(jnp.int32, v.shape, 0)
            inside = jnp.logical_and(row >= 0, row < pos_count * local_rows)
            hidden = jnp.where(inside, gelu(act), 0.0)
            for b in range(lanes_count):
                scr[b, pl.ds(at, 16), :] = hidden[:, b * 128 : (b + 1) * 128]
                raw[b, pl.ds(at, 16), :] = v[:, b * 128 : (b + 1) * 128]

        @pl.loop(0, pairs // 16)
        def _(i):
            at = pl.multiple_of(i * 16, 16)
            to = pl.ds(pl.multiple_of(m * pairs + at, 16), 16)
            for b in range(lanes_count):
                for d in range(PIECES):
                    h_cat[to, d * wide + b * 128 : d * wide + (b + 1) * 128] = scr[
                        b, pl.ds(16 - RIM + d + 2 * at, 16, stride=2), :
                    ].astype(BF16)
                for e in range(2):
                    xs[e, to, b * 128 : (b + 1) * 128] = raw[
                        b, pl.ds(16 + e + 2 * at, 16, stride=2), :
                    ].astype(BF16)

    def pieces_out():
        copies = [
            pltpu.make_async_copy(h_cat.at[:, d * wide : (d + 1) * wide], hp.at[d], out_sem.at[d])
            for d in range(PIECES)
        ]
        return copies + [pltpu.make_async_copy(xs, xs_out, out_sem.at[PIECES])]

    for copy in pieces_out():
        copy.start()

    def f_copy(i):
        dst = f_own if i < tiles else f_other
        c = i % tiles
        return pltpu.make_async_copy(
            f_buf.at[i % 2], dst.at[:, :, c * chunk : (c + 1) * chunk], f_sem.at[i % 2]
        )

    value2[...] = jnp.zeros_like(value2)

    def conv(i):
        w_load(i).wait()
        if i >= 2:
            f_copy(i - 2).wait()
        c = i % tiles
        source, side = (small_ref, ch) if i < tiles else (small_x, 1 - ch)
        bias = source[0:1, c * chunk : (c + 1) * chunk]
        at = pl.ds(pl.multiple_of(side * local_out + c * chunk, 128), chunk)
        sums = [[0.0, 0.0] for _ in range(micro_count)]
        for e in range(2):
            acc = jnp.dot(
                h_cat[:, e * wide : (e + KW) * wide], w_buf[i % parts], preferred_element_type=F32
            )
            acc += bias
            f_buf[i % 2, e] = acc
            for m in range(micro_count):
                part = acc[m * pairs : (m + 1) * pairs]
                sums[m][0] += jnp.sum(part, axis=0, keepdims=True)
                sums[m][1] += jnp.sum(part * part, axis=0, keepdims=True)
        for m in range(micro_count):
            for k in range(2):
                value2[2 * m + k : 2 * m + k + 1, at] = sums[m][k]
        f_copy(i).start()

    fetch1[0].end()
    conv(0)
    fetch1[0].done()
    w_load(2).start()
    conv(1)
    og_remote().start()
    fetch1[1].step(far_count - 2)
    fetch_p.over_y().wait_recv()
    fetch_p.begin()
    conv(2)
    fetch1[1].end()
    fetch1[1].done()
    w_load(3).start()
    for r in range(far_count - 3):
        fetch_p.step(r)
    conv(3)
    second.start(0)
    fetch_p.step(far_count - 3)
    second.start(1)
    fetch_p.step(far_count - 2)
    second.start(2)
    second_y().wait_recv()
    second_core().start()
    fetch_p.end()
    second.start(3)
    for copy in pieces_out():
        copy.wait()
    fetch_p.done()
    second_core().wait()
    og_local().wait()
    og_remote().wait()
    for f in fetch1 + [fetch_p]:
        f.drain()
    second_y().wait_send()
    main_input().wait_send()
    halo_up(0).wait_send()
    halo_down(0).wait_send()
    small_copy().wait_send()
    f_copy(2).wait()
    f_copy(3).wait()
    second.wait(3)
    for m in range(micro_count):
        for q, (source, side) in enumerate(((small_ref, ch), (small_x, 1 - ch))):
            at = pl.ds(pl.multiple_of(side * local_out, 128), local_out)
            to = slice(q * local_out, (q + 1) * local_out)
            center = s_result[2 * m : 2 * m + 1, at] * scale
            square = s_result[2 * m + 1 : 2 * m + 2, at] * scale
            vec2[m, 0:1, to] = center
            vec2[m, 1:2, to] = lax.rsqrt(square - center * center + EPS)
            vec2[m, 2:5, to] = source[1:4, :]
            vec2[m, 5:8, to] = jnp.zeros((3, local_out), F32)


def head(x, w1, w2, wp, og, small, total_rows):
    micro_count, local_rows, local_in = x.shape
    wide = 2 * local_in
    half = local_rows // 2
    pairs = half // 2
    rows = micro_count * pairs
    ext = half + 32
    local_out = w1.shape[1]
    out = 2 * local_out
    chunk = local_out // 2
    far = lax.axis_size("pos") // 2
    any_space = pl.BlockSpec(memory_space=pl.ANY)
    in_vmem = pl.BlockSpec(memory_space=pltpu.VMEM)
    dma = pltpu.SemaphoreType.DMA
    fetches = local_out // chunk + 1
    return pl.pallas_call(
        functools.partial(head_kernel, total_rows),
        out_shape=(
            jax.ShapeDtypeStruct((PIECES, rows, wide), BF16),
            jax.ShapeDtypeStruct((2, rows, wide), BF16),
            jax.ShapeDtypeStruct((2, rows, local_out), F32),
            jax.ShapeDtypeStruct((2, rows, local_out), F32),
            jax.ShapeDtypeStruct(w1.shape, BF16),
            jax.ShapeDtypeStruct(w2.shape, BF16),
            jax.ShapeDtypeStruct(wp.shape, BF16),
            jax.ShapeDtypeStruct((micro_count, og.shape[1] // 2, out), BF16),
            jax.ShapeDtypeStruct((micro_count, 8, wide), F32),
            jax.ShapeDtypeStruct((micro_count, 8, out), F32),
        ),
        in_specs=[any_space] * 5 + [in_vmem],
        out_specs=(any_space,) * 8 + (in_vmem,) * 2,
        scratch_shapes=[
            pltpu.VMEM((8, local_out), F32),
            pltpu.VMEM((micro_count, local_rows, local_in), BF16),
            pltpu.VMEM((micro_count, ext, wide), BF16),
            pltpu.VMEM((wide // 128, ext, 128), F32),
            pltpu.VMEM((wide // 128, ext, 128), F32),
            pltpu.VMEM((rows, PIECES * wide), BF16),
            pltpu.VMEM((2, rows, wide), BF16),
            pltpu.VMEM((2, KW * wide, chunk), BF16),
            pltpu.VMEM((2, 2, rows, chunk), F32),
            dma((3,)),
            dma((2,)),
            dma((2,)),
            dma((PIECES + 1,)),
            dma,
            dma,
            dma((2,)),
            dma((2,)),
            dma((fetches,)),
            dma((fetches,)),
            dma((fetches, far - 1)),
            dma((fetches, far - 1)),
            dma((fetches, far)),
            dma((fetches, far)),
            dma((fetches, 2, far)),
            dma((fetches, 2, far)),
            dma,
            dma,
            dma,
            dma,
            dma,
            dma,
            dma,
            dma,
        ]
        + Reduce.scratch(wide)
        + Reduce.scratch(out),
        compiler_params=params(collective_id=6, has_side_effects=True),
        name="head",
    )(x, w1, w2, wp, og, small)


class Scatter:
    def __init__(self, reduce, kept, sent, x_in, z_in, y_out, y_in, sems):
        self.reduce, self.kept, self.sent = reduce, kept, sent
        self.x_in, self.z_in, self.y_out, self.y_in = x_in, z_in, y_out, y_in
        self.z_send, self.z_recv, self.y_send, self.y_recv, *self.x_sems = sems
        self.count = reduce.far_count
        self.half = y_in.shape[1]

    @staticmethod
    def scratch(block, width):
        far = lax.axis_size("pos") // 2
        dma = pltpu.SemaphoreType.DMA
        return [
            pltpu.VMEM((far, block, width), BF16),
            pltpu.VMEM((far - 1, block, width), BF16),
            pltpu.VMEM((block, width // 2), BF16),
            pltpu.VMEM((block, width // 2), BF16),
            dma((far - 1,)),
            dma((far - 1,)),
            dma,
            dma,
        ]

    def away(self, r):
        return far_order(self.reduce.z)[r]

    def copy(self, src, dst, send, recv, peer):
        return pltpu.make_async_remote_copy(src, dst, send, recv, device_id=peer, device_id_type=MESH)

    def over_x(self, r):
        zz, me = self.away(r), self.reduce
        peer = (1 - me.batch, me.pos, me.ch)
        return self.copy(self.sent(zz), self.x_in.at[zz], self.x_sems[0].at[zz], self.x_sems[1].at[zz], peer)

    def over_z(self, r):
        zz, me = self.away(r), self.reduce
        peer = (me.batch, self.away(max(r, 1)) * 2 + me.core, me.ch)
        return self.copy(self.x_in.at[zz], self.z_in.at[r], self.z_send.at[r], self.z_recv.at[r], peer)

    def over_y(self):
        me = self.reduce
        return self.copy(self.y_out, self.y_in, self.y_send, self.y_recv, (me.batch, me.pos, 1 - me.ch))

    def send_x(self, r):
        self.over_x(r).start()

    def send_z(self, r):
        zz = self.away(r)
        if self.x_sems:
            self.over_x(r).wait_recv()
            self.x_in[zz] = (self.x_in[zz].astype(F32) + self.kept(zz)[...].astype(F32)).astype(BF16)
        if r < 2:
            self.over_z(r).start()

    def relay(self):
        zz = self.away(2)
        self.over_z(0).wait_recv()
        self.x_in[zz] = (self.x_in[zz].astype(F32) + self.z_in[0].astype(F32)).astype(BF16)
        self.over_z(2).start()

    def send_y(self):
        zz = self.away(3)
        total = self.x_in[zz].astype(F32)
        for r in range(1, 3):
            self.over_z(r).wait_recv()
            total = total + self.z_in[r].astype(F32)
        self.y_out[...] = total[:, self.half :].astype(BF16)
        self.over_y().start()
        return total[:, : self.half]

    def finish(self):
        self.over_y().wait_recv()
        return self.y_in[...].astype(F32)

    def drain(self):
        for r in range(self.count):
            if self.x_sems:
                self.over_x(r).wait_send()
            if r < self.count - 1:
                self.over_z(r).wait_send()
        self.over_y().wait_send()


def far_order(z):
    near = z + 1 - 2 * lax.rem(z, 2)
    return [lax.rem(near + 2, 4), near, lax.rem(z + 2, 4), z]


def middle_kernel(
    scatter,
    total_rows,
    f_own,
    f_other,
    w2_own,
    w2_other,
    wp_own,
    wp_other,
    ogx,
    x,
    vec_ref,
    vec1_ref,
    lim_ref,
    pooled_out,
    gp,
    xa,
    h_other,
    dw2_out,
    dwp_out,
    sum_out,
    extra,
    w2_ref,
    wp_ref,
    first,
    so,
    a2g,
    hid,
    branch,
    diff,
    lg,
    og,
    pooled,
    dwp,
    dw2,
    p_core,
    q_core,
    low32,
    edge_out,
    edge_in,
    h_in,
    h_wide,
    h_stage,
    h_in_sem,
    h_out_sem,
    w_sem,
    f_sem,
    misc_sem,
    gp_sem,
    pooled_sem,
    pooled_send,
    pooled_recv,
    xa_send,
    xa_recv,
    rim_send,
    rim_recv,
    edge_send,
    edge_recv,
    pc_send,
    pc_recv,
    qc_send,
    qc_recv,
    value,
    r_core,
    r_near,
    r_far,
    r_result,
    r_send,
    r_recv,
    x_in,
    x_send,
    x_recv,
):
    reduce = Reduce(value, r_core, r_near, r_far, r_result, (r_send, r_recv))
    batch, pos, ch, core, z = reduce.batch, reduce.pos, reduce.ch, reduce.core, reduce.z
    far_count = reduce.far_count
    pos_count = 2 * far_count
    _, micro_count, pairs, wide = first.shape
    rows = 2 * pairs
    half = wide // 2
    tile = 256
    tiles = wide // tile
    y_peer = (batch, pos, 1 - ch)
    local_rows, local_in = x.shape[1:]
    half_rows = local_rows // 2
    ext = xa.shape[1]
    main = half_rows + 16

    def columns(j):
        return pl.ds(pl.multiple_of(j * tile, tile), tile)

    def natural(j):
        at = lax.rem(j * tile + ch * half, wide)
        return pl.ds(pl.multiple_of(at, tile), tile)

    def remote(src, dst, send, recv, peer):
        return pltpu.make_async_remote_copy(src, dst, send, recv, device_id=peer, device_id_type=MESH)

    def w_copies(kind):
        copies = []
        dst = (w2_ref, wp_ref)[kind]
        for q, src in enumerate(((w2_own, w2_other), (wp_own, wp_other))[kind]):
            for r in range(2):
                at = pl.ds(pl.multiple_of(lax.rem(ch + r, 2) * half, 16), half)
                copies.append(
                    pltpu.make_async_copy(
                        src.at[at, :],
                        dst.at[r * half : (r + 1) * half, q * half : (q + 1) * half],
                        w_sem.at[kind, q, r],
                    )
                )
        return copies

    def f_copies():
        return [
            pltpu.make_async_copy(src, first.at[:, :, :, q * half : (q + 1) * half], f_sem.at[q])
            for q, src in enumerate((f_own, f_other))
        ]

    def og_copy():
        return pltpu.make_async_copy(ogx, og, misc_sem.at[0])

    lanes_in = pl.ds(pl.multiple_of(ch * local_in, 128), local_in)

    def xa_local():
        begin = pl.multiple_of((1 - ch) * (half_rows - 16), 16)
        return pltpu.make_async_copy(
            x.at[:, pl.ds(begin, main), :],
            xa.at[:, pl.ds(pl.multiple_of(16 * ch, 16), main), lanes_in],
            misc_sem.at[1],
        )

    def xa_remote():
        begin = pl.multiple_of(ch * (half_rows - 16), 16)
        return remote(
            x.at[:, pl.ds(begin, main), :],
            xa.at[:, pl.ds(pl.multiple_of(16 * (1 - ch), 16), main), lanes_in],
            xa_send,
            xa_recv,
            y_peer,
        )

    def rim_up(s):
        return remote(
            x.at[:, local_rows - 16 : local_rows, :],
            xa.at[:, 0:16, lanes_in],
            rim_send.at[0],
            rim_recv.at[s],
            (batch, lax.rem(pos + 1, pos_count), 1),
        )

    def rim_down(s):
        return remote(
            x.at[:, 0:16, :],
            xa.at[:, ext - 16 : ext, lanes_in],
            rim_send.at[1],
            rim_recv.at[s],
            (batch, lax.rem(pos + pos_count - 1, pos_count), 0),
        )

    right = (batch, lax.rem(pos + ch, pos_count), 1 - ch)
    left = (batch, lax.rem(pos + pos_count - 1 + ch, pos_count), 1 - ch)
    rim_from = lax.rem(pos + pos_count + 1 - 2 * ch, pos_count)

    for copy in f_copies():
        copy.start()
    for kind in range(2):
        for copy in w_copies(kind):
            copy.start()
    og_copy().start()
    xa_local().start()
    meet(reduce.peers() + [right, left, (batch, rim_from, 0), (batch, rim_from, 1)])
    xa_remote().start()
    rim_up(ch).start()
    rim_down(ch).start()
    value[...] = jnp.zeros_like(value)
    for copy in f_copies():
        copy.wait()

    def normal(m, e, c):
        return (first[e, m, :, c] - vec_ref[m, 0:1, c]) * vec_ref[m, 1:2, c]

    def forward(m):
        @pl.loop(0, tiles)
        def _(j):
            c = columns(j)
            for e in range(2):
                act = normal(m, e, c) * vec_ref[m, 2:3, c] + vec_ref[m, 3:4, c]
                hid[m, e * pairs : (e + 1) * pairs, c] = gelu(act).astype(BF16)

        if m == 0:
            for copy in w_copies(0):
                copy.wait()

        @pl.loop(0, tiles)
        def _(j):
            c = columns(j)
            step = jnp.dot(hid[m], w2_ref[:, c], preferred_element_type=F32)
            even = step[:pairs] + (first[0, m, :, c] + vec_ref[m, 4:5, c])
            odd = step[pairs:] + (first[1, m, :, c] + vec_ref[m, 4:5, c])
            so[m, 0, :, c] = even
            so[m, 1, :, c] = odd
            diff[m, :, c] = (even - odd).astype(BF16)

        if m == 0:
            for copy in w_copies(1):
                copy.wait()
            og_copy().wait()
        limit = lim_ref[m, 0:1, 0:1]
        inverse_limit = 1.0 / limit

        @pl.loop(0, tiles)
        def _(j):
            c = columns(j)
            d = jnp.dot(diff[m], wp_ref[:, c], preferred_element_type=F32)
            t = jnp.tanh(0.5 * d)
            weight_even = 0.5 + 0.5 * t
            weight_odd = 0.5 - 0.5 * t
            even, odd = so[m, 0, :, c], so[m, 1, :, c]
            pooled[m, :, c] = (weight_even * even + weight_odd * odd).astype(BF16)
            clipped = limit * jnp.tanh(og[m, :, c].astype(F32) * inverse_limit)
            lg[m, :, c] = (weight_even * weight_odd * (even - odd) * clipped).astype(BF16)
            so[m, 0, :, c] = weight_even * clipped
            so[m, 1, :, c] = weight_odd * clipped

        pooled_local(m).start()
        pooled_remote(m).start()

    bins_at = pl.ds(pl.multiple_of(ch * pairs, 16), pairs)

    def pooled_local(m):
        return pltpu.make_async_copy(pooled.at[m, :, 0:half], pooled_out.at[m, bins_at], pooled_sem.at[m])

    def pooled_remote(m):
        return remote(
            pooled.at[m, :, half:wide], pooled_out.at[m, bins_at], pooled_send.at[m], pooled_recv.at[m], y_peer
        )

    def pool_back(m):
        @pl.loop(0, tiles)
        def _(j):
            c = columns(j)
            g = lax.dot_general(lg[m], wp_ref[c, :], NT, preferred_element_type=F32)
            even = so[m, 0, :, c] + g
            odd = so[m, 1, :, c] - g
            so[m, 0, :, c] = even
            so[m, 1, :, c] = odd
            low_even, low_odd = even.astype(BF16), odd.astype(BF16)
            branch[m, 0:pairs, c] = low_even
            branch[m, pairs:rows, c] = low_odd
            both = low_even.astype(F32) + low_odd.astype(F32)
            value[3 * m + 2 : 3 * m + 3, natural(j)] = jnp.sum(both, axis=0, keepdims=True)

    def act_back(m):
        @pl.loop(0, tiles)
        def _(j):
            c = columns(j)
            hg = lax.dot_general(branch[m], w2_ref[c, :], NT, preferred_element_type=F32)
            plain, cross = 0.0, 0.0
            for e in range(2):
                normed = normal(m, e, c)
                act = normed * vec_ref[m, 2:3, c] + vec_ref[m, 3:4, c]
                grad = hg[e * pairs : (e + 1) * pairs] * gelu_slope(act)
                a2g[m, e, :, c] = grad
                plain += jnp.sum(grad, axis=0, keepdims=True)
                cross += jnp.sum(grad * normed, axis=0, keepdims=True)
            value[3 * m : 3 * m + 1, natural(j)] = plain
            value[3 * m + 1 : 3 * m + 2, natural(j)] = cross

    blocks = 4 * far_count
    block = wide // blocks

    def product(dst, left, right_side):
        depth = left.shape[0] * left.shape[1]

        @pl.loop(0, tiles)
        def _(j):
            c = columns(j)
            dst[c, :] = lax.dot_general(
                left[:, :, c].reshape(depth, tile),
                right_side[...].reshape(depth, wide),
                TN,
                preferred_element_type=F32,
            ).astype(BF16)

    def block_rows(bb, zz, cc):
        number = lax.rem((bb * far_count + zz) * 2 + cc + ch * (blocks // 2), blocks)
        return pl.ds(pl.multiple_of(number * block, 16), block)

    def core_copies(src, dst, send, recv):
        return [
            remote(
                src.at[block_rows(bb, zz, 1 - core)], dst.at[bb, zz], send.at[bb, zz], recv.at[bb, zz], reduce.core_peer
            )
            for bb in range(2)
            for zz in range(far_count)
        ]

    def add_core(src, dst, sends):
        i = 0
        for bb in range(2):
            for zz in range(far_count):
                sends[i].wait_recv()
                i += 1
                mine = src[block_rows(bb, zz, core), :].astype(F32)
                dst[bb, zz] = (dst[bb, zz].astype(F32) + mine).astype(BF16)

    p_sends = core_copies(dwp, p_core, pc_send, pc_recv) if scatter else []
    q_sends = core_copies(dw2, q_core, qc_send, qc_recv) if scatter else []
    def pool_x(zz):
        return remote(
            p_core.at[1 - batch, zz], x_in.at[zz], x_send.at[zz], x_recv.at[zz], (1 - batch, pos, ch)
        )

    def pool_sum(zz):
        pool_x(zz).wait_recv()
        x_in[zz] = (x_in[zz].astype(F32) + p_core[batch, zz].astype(F32)).astype(BF16)

    def dwp_copy():
        return pltpu.make_async_copy(x_in if scatter else dwp, dwp_out, misc_sem.at[3])

    lanes_count = h_other.shape[2] // 128
    h_count = micro_count * lanes_count
    ext_half = ext // 2
    h_begin = pos * local_rows + (1 - ch) * half_rows - 16

    def h_load(i):
        at = pl.ds(pl.multiple_of(lax.rem(i, lanes_count) * 128, 128), 128)
        slot = lax.rem(i, 2)
        return pltpu.make_async_copy(xa.at[i // lanes_count, :, at], h_in.at[slot], h_in_sem.at[slot])

    def h_store(i):
        at = pl.ds(pl.multiple_of(lax.rem(i, lanes_count) * 128, 128), 128)
        to = pl.ds(pl.multiple_of((i // lanes_count) * pairs, 16), pairs)
        slot = lax.rem(i, 2)
        return pltpu.make_async_copy(h_stage.at[slot], h_other.at[:, to, at], h_out_sem.at[slot])

    def hidden_blocks(low, high):
        @pl.loop(low, high)
        def _(i):
            slot = lax.rem(i, 2)
            m = i // lanes_count
            at = pl.ds(pl.multiple_of(lax.rem(i, lanes_count) * 128, 128), 128)

            @pl.when(i + 1 < h_count)
            def _():
                h_load(i + 1).start()

            h_load(i).wait()

            @pl.when(i >= 2)
            def _():
                h_store(i - 2).wait()

            for part in range(2):
                v = h_in[slot, part * ext_half : (part + 1) * ext_half, :].astype(F32)
                act = (v - vec1_ref[m, 0:1, at]) * vec1_ref[m, 1:2, at] + vec1_ref[m, 2:3, at]
                row = h_begin + part * ext_half + lax.broadcasted_iota(jnp.int32, v.shape, 0)
                inside = jnp.logical_and(row >= 0, row < pos_count * local_rows)
                h_wide[part * ext_half : (part + 1) * ext_half, :] = jnp.where(inside, gelu(act), 0.0)
            for d in range(PIECES):
                h_stage[slot, d] = h_wide[pl.ds(16 - RIM + d, pairs, stride=2), :].astype(BF16)
            h_store(i).start()

    def dw2_copy():
        return pltpu.make_async_copy(q_core if scatter else dw2, dw2_out, misc_sem.at[2])

    for m in range(micro_count):
        forward(m)
    product(dwp, diff, lg)
    for copy in p_sends:
        copy.start()
    for m in range(micro_count):
        pool_back(m)
    if scatter:
        add_core(dwp, p_core, p_sends)
        for zz in range(far_count):
            pool_x(zz).start()
    product(dw2, hid, branch)
    for copy in q_sends:
        copy.start()
    if not scatter:
        dw2_copy().start()
    for m in range(micro_count):
        act_back(m)
    reduce.start(0)
    xa_local().wait()
    xa_remote().wait_recv()
    for s in range(2):
        rim_up(s).wait_recv()
    h_load(0).start()
    quarter = h_count // 4
    hidden_blocks(0, quarter)
    reduce.start(1)
    if scatter:
        add_core(dw2, q_core, q_sends)
        dw2_copy().start()
    hidden_blocks(quarter, 2 * quarter)
    reduce.start(2)
    hidden_blocks(2 * quarter, 3 * quarter)
    reduce.start(3)
    hidden_blocks(3 * quarter, h_count)
    reduce.wait(3)
    sum_out[...] = r_result[...]

    scale = 1.0 / total_rows

    def first_low(m, e, c, n, at):
        plain = r_result[3 * m : 3 * m + 1, n] * scale
        cross = r_result[3 * m + 1 : 3 * m + 2, n] * scale
        normed = (first[e, m, at, c] - vec_ref[m, 0:1, c]) * vec_ref[m, 1:2, c]
        grad = so[m, e, at, c] + vec_ref[m, 1:2, c] * vec_ref[m, 2:3, c] * (
            a2g[m, e, at, c] - plain - normed * cross
        )
        return grad.astype(BF16).astype(F32)

    edge_out[...] = jnp.zeros_like(edge_out)
    for q in range(2):
        c = slice(q * half, (q + 1) * half)
        n = pl.ds(pl.multiple_of(lax.rem(q + ch, 2) * half, 128), half)
        for m in range(micro_count):
            for e in range(2):
                row = 2 * m + e
                top = first_low(m, e, c, n, slice(0, 8))
                bottom = first_low(m, e, c, n, slice(pairs - 8, pairs))
                edge_out[0, row : row + 1, n] = top[0:1]
                edge_out[1, row : row + 1, n] = bottom[7:8]

    def edge_copy(side):
        return remote(
            edge_out.at[side], edge_in.at[1 - side], edge_send.at[side], edge_recv.at[1 - side], (left, right)[side]
        )

    for side in range(2):
        edge_copy(side).start()
    line = pos * 2 + ch
    edge_copy(1).wait_send()
    edge_copy(0).wait_send()
    for side in range(2):
        edge_copy(side).wait_recv()
    keep_before = jnp.where(line > 0, 1.0, 0.0)
    keep_after = jnp.where(line < 2 * pos_count - 1, 1.0, 0.0)
    slots = 2

    def gp_copies(slot, c):
        return [
            pltpu.make_async_copy(
                w2_ref.at[slot * micro_count * pairs : (slot + 1) * micro_count * pairs, d * tile : (d + 1) * tile],
                gp.at[d, :, c],
                gp_sem.at[slot, d],
            )
            for d in range(PIECES)
        ]

    extra[...] = jnp.zeros_like(extra)
    for j in range(tiles):
        c = columns(j)
        n = natural(j)
        slot = j % slots
        if j >= slots:
            for copy in gp_copies(slot, columns(j - slots)):
                copy.wait()
        for m in range(micro_count):
            total = 0.0
            for e in range(2):
                row = 2 * m + e
                low = first_low(m, e, c, n, slice(0, pairs))
                low32[e, 8 : 8 + pairs, :] = low
                low32[e, 7:8, :] = edge_in[0, row : row + 1, n] * keep_before
                low32[e, 8 + pairs : 9 + pairs, :] = edge_in[1, row : row + 1, n] * keep_after
                total += jnp.sum(low, axis=0, keepdims=True)
            extra[2 * micro_count + m : 2 * micro_count + m + 1, n] = total
            begin = slot * micro_count * pairs + m * pairs
            for d in range(PIECES):
                shift = 7 + d // 2
                w2_ref[begin : begin + pairs, d * tile : (d + 1) * tile] = low32[
                    d % 2, shift : shift + pairs, :
                ].astype(BF16)
        for copy in gp_copies(slot, c):
            copy.start()
        if j == 2:
            if scatter:
                for zz in range(far_count):
                    pool_sum(zz)
            dwp_copy().start()
    for j in range(tiles - slots, tiles):
        for copy in gp_copies(j % slots, columns(j)):
            copy.wait()
    for i in range(h_count - 2, h_count):
        h_store(i).wait()
    xa_remote().wait_send()
    rim_up(0).wait_send()
    rim_down(0).wait_send()
    for m in range(micro_count):
        pooled_local(m).wait()
        pooled_remote(m).wait()
    dw2_copy().wait()
    dwp_copy().wait()
    if scatter:
        for zz in range(far_count):
            pool_x(zz).wait_send()
        for copy in p_sends + q_sends:
            copy.wait_send()


def middle(first_own, first_other, weights, og, x, vecs, vec1, limits, total_rows):
    _, micro_count, pairs, half = first_own.shape
    wide = 2 * half
    rows = 2 * pairs
    depth = micro_count * pairs
    local_rows, local_in = x.shape[1:]
    far = lax.axis_size("pos") // 2
    block = wide // (4 * far)
    scatter = block % 16 == 0 and far == 4
    land = block if scatter else 16
    tile = 256
    any_space = pl.BlockSpec(memory_space=pl.ANY)
    in_vmem = pl.BlockSpec(memory_space=pltpu.VMEM)
    dma = pltpu.SemaphoreType.DMA
    return pl.pallas_call(
        functools.partial(middle_kernel, scatter, total_rows),
        out_shape=(
            jax.ShapeDtypeStruct((micro_count, rows, half), BF16),
            jax.ShapeDtypeStruct((PIECES, depth, wide), BF16),
            jax.ShapeDtypeStruct((micro_count, local_rows // 2 + 32, 2 * local_in), BF16),
            jax.ShapeDtypeStruct((PIECES, depth, 2 * local_in), BF16),
            jax.ShapeDtypeStruct((2, far, block, wide) if scatter else (wide, wide), BF16),
            jax.ShapeDtypeStruct((far, block, wide) if scatter else (wide, wide), BF16),
            jax.ShapeDtypeStruct((8, wide), F32),
            jax.ShapeDtypeStruct((8, wide), F32),
        ),
        in_specs=[any_space] * 8 + [in_vmem] * 3,
        out_specs=(any_space,) * 6 + (in_vmem, in_vmem),
        scratch_shapes=[
            pltpu.VMEM((wide, wide), BF16),
            pltpu.VMEM((wide, wide), BF16),
            pltpu.VMEM((2, micro_count, pairs, wide), F32),
            pltpu.VMEM((micro_count, 2, pairs, wide), F32),
            pltpu.VMEM((micro_count, 2, pairs, wide), F32),
            pltpu.VMEM((micro_count, rows, wide), BF16),
            pltpu.VMEM((micro_count, rows, wide), BF16),
            pltpu.VMEM((micro_count, pairs, wide), BF16),
            pltpu.VMEM((micro_count, pairs, wide), BF16),
            pltpu.VMEM((micro_count, pairs, wide), BF16),
            pltpu.VMEM((micro_count, pairs, wide), BF16),
            pltpu.VMEM((wide, wide), BF16),
            pltpu.VMEM((wide, wide), BF16),
            pltpu.VMEM((2, far, land, wide), BF16),
            pltpu.VMEM((2, far, land, wide), BF16),
            pltpu.VMEM((2, pairs + 16, tile), F32),
            pltpu.VMEM((2, 8, wide), F32),
            pltpu.VMEM((2, 8, wide), F32),
            pltpu.VMEM((2, local_rows // 2 + 32, 128), BF16),
            pltpu.VMEM((local_rows // 2 + 32, 128), F32),
            pltpu.VMEM((2, PIECES, pairs, 128), BF16),
            dma((2,)),
            dma((2,)),
            dma((2, 2, 2)),
            dma((2,)),
            dma((4,)),
            dma((2, PIECES)),
            dma((micro_count,)),
            dma((micro_count,)),
            dma((micro_count,)),
            dma,
            dma,
            dma((2,)),
            dma((2,)),
            dma((2,)),
            dma((2,)),
            dma((2, far)),
            dma((2, far)),
            dma((2, far)),
            dma((2, far)),
        ]
        + Reduce.scratch(wide)
        + [pltpu.VMEM((far, land, wide), BF16), dma((far,)), dma((far,))],
        compiler_params=params(collective_id=7, has_side_effects=True),
        name="middle",
    )(first_own, first_other, *weights, og, x, vecs, vec1, limits)


def tail_kernel(
    scatter,
    total_rows,
    hp_own,
    hp_other,
    gp,
    wo,
    wx,
    xs_in,
    dw2,
    dwp,
    vec_ref,
    extra_ref,
    ig,
    dw_out,
    dw2_out,
    dwp_out,
    sum_out,
    g_buf,
    w_buf,
    a1g,
    xs,
    h_buf,
    f_buf,
    dw,
    core_in,
    x_in,
    z_in,
    weave,
    load_sem,
    w_sem,
    h_sem,
    low_send,
    low_recv,
    core_send,
    core_recv,
    x_send,
    x_recv,
    z_send,
    z_recv,
    ig_send,
    ig_recv,
    ig_sem,
    value,
    r_core,
    r_near,
    r_far,
    r_result,
    r_send,
    r_recv,
    k2_buf,
    x2_in,
    z2_in,
    y2_out,
    y2_in,
    z2_send,
    z2_recv,
    y2_send,
    y2_recv,
    x2_send,
    x2_recv,
    x3_in,
    z3_in,
    y3_out,
    y3_in,
    z3_send,
    z3_recv,
    y3_send,
    y3_recv,
):
    reduce = Reduce(value, r_core, r_near, r_far, r_result, (r_send, r_recv))
    batch, pos, ch, core, z = reduce.batch, reduce.pos, reduce.ch, reduce.core, reduce.z
    far_count = reduce.far_count
    chunks, rows_all, chunk = dw.shape
    rows, wide = xs.shape[1:]
    micro_count, pairs = vec_ref.shape[0], rows // vec_ref.shape[0]
    half_rows = 2 * pairs
    out = gp.shape[2]
    local_out = out // 2
    local_in = wide // 2
    tile = w_buf.shape[1]
    cut = h_buf.shape[3]
    per_half = rows_all // 2 // cut
    y_peer = (batch, pos, 1 - ch)
    x_peer = (1 - batch, pos, ch)
    core_peer = reduce.core_peer

    def loads():
        copies = [
            pltpu.make_async_copy(gp.at[2:4, :, 0:local_out], f_buf.at[0:2], load_sem.at[0]),
            pltpu.make_async_copy(xs_in, xs, load_sem.at[1]),
        ]
        for d in range(PIECES):
            copies.append(
                pltpu.make_async_copy(gp.at[d], g_buf.at[:, d * out : (d + 1) * out], load_sem.at[2 + d])
            )
        return copies

    def w_copies(j):
        s = j % 2
        at = slice(j * tile, (j + 1) * tile)
        copies = []
        for k in range(KW):
            for q, src in enumerate((wo, wx)):
                lanes = (KW - 1 - k) * out + q * local_out
                copies.append(
                    pltpu.make_async_copy(
                        src.at[k, at, :], w_buf.at[s, :, lanes : lanes + local_out], w_sem.at[s, 2 * k + q]
                    )
                )
        return copies

    def h_copies(side_half, t):
        number = side_half * per_half + t
        k = number // 2
        at = pl.ds(pl.multiple_of(lax.rem(number, 2) * cut, cut), cut)
        slot = lax.rem(t, 2)
        return [
            pltpu.make_async_copy((hp_own, hp_other)[s].at[k + e, :, at], h_buf.at[slot, 2 * s + e], h_sem.at[slot, 2 * s + e])
            for s in range(2)
            for e in range(2)
        ]

    def low_copy(c):
        return pltpu.make_async_remote_copy(
            gp.at[2:4, :, local_out + c * chunk : local_out + (c + 1) * chunk],
            f_buf.at[2:4, :, c * chunk : (c + 1) * chunk],
            low_send.at[c],
            low_recv.at[c],
            device_id=y_peer,
            device_id_type=MESH,
        )

    second = Scatter(
        reduce,
        lambda zz: k2_buf.at[zz],
        lambda zz: dw2.at[1 - batch, zz],
        x2_in,
        z2_in,
        y2_out,
        y2_in,
        (z2_send, z2_recv, y2_send, y2_recv, x2_send, x2_recv),
    )
    third = Scatter(
        reduce,
        None,
        None,
        x3_in,
        z3_in,
        y3_out,
        y3_in,
        (z3_send, z3_recv, y3_send, y3_recv),
    )

    def third_copy():
        return pltpu.make_async_copy(dwp, x3_in, load_sem.at[3 + PIECES])

    def k2_copy():
        return pltpu.make_async_copy(dw2.at[batch], k2_buf, load_sem.at[2 + PIECES])

    for copy in loads():
        copy.start()
    for copy in w_copies(0):
        copy.start()
    if scatter:
        k2_copy().start()
        third_copy().start()
    meet(reduce.peers())
    low_copy(0).start()
    if scatter:
        for r in range(far_count):
            second.send_x(r)
        third_copy().wait()
        for r in range(far_count):
            third.send_z(r)
    for copy in h_copies(1 - batch, 0):
        copy.start()
    for copy in loads()[1:]:
        copy.wait()
    value[...] = extra_ref[...]

    tiles = wide // tile

    def back(j):
        s = j % 2
        if j + 1 < tiles:
            for copy in w_copies(j + 1):
                copy.start()
        for copy in w_copies(j):
            copy.wait()
        at = slice(j * tile, (j + 1) * tile)
        sums = [[0.0, 0.0] for _ in range(micro_count)]
        for e in range(2):
            acc = lax.dot_general(
                g_buf[:, e * out : (e + KW) * out], w_buf[s], NT, preferred_element_type=F32
            )
            for m in range(micro_count):
                x = xs[e, m * pairs : (m + 1) * pairs, at].astype(F32)
                moved = x - vec_ref[m, 0:1, at]
                normed = moved * vec_ref[m, 3:4, at]
                act = moved * vec_ref[m, 1:2, at] + vec_ref[m, 2:3, at]
                grad = acc[m * pairs : (m + 1) * pairs] * gelu_slope(act)
                a1g[e, m * pairs : (m + 1) * pairs, at] = grad
                sums[m][0] += jnp.sum(grad, axis=0, keepdims=True)
                sums[m][1] += jnp.sum(grad * normed, axis=0, keepdims=True)
        for m in range(micro_count):
            for i in range(2):
                value[2 * m + i : 2 * m + i + 1, at] = sums[m][i]

    block = rows_all // (2 * 2 * far_count)

    def block_rows(side_half, zz, cc):
        return pl.ds(pl.multiple_of(((side_half * far_count + zz) * 2 + cc) * block, 16), block)

    def core_copy(c, kind, side_half, zz):
        return pltpu.make_async_remote_copy(
            dw.at[c, block_rows(side_half, zz, 1 - core)],
            core_in.at[c, kind, zz],
            core_send.at[c, kind, zz],
            core_recv.at[c, kind, zz],
            device_id=core_peer,
            device_id_type=MESH,
        )

    def x_copy(c, zz):
        return pltpu.make_async_remote_copy(
            dw.at[c, block_rows(1 - batch, zz, core)],
            x_in.at[c, zz],
            x_send.at[c, zz],
            x_recv.at[c, zz],
            device_id=x_peer,
            device_id_type=MESH,
        )

    def z_copy(c, r, zz):
        return pltpu.make_async_remote_copy(
            dw.at[c, block_rows(batch, zz, core)],
            z_in.at[c, r],
            z_send.at[c, r],
            z_recv.at[c, r],
            device_id=(batch, away(max(r, 1)) * 2 + core, ch),
            device_id_type=MESH,
        )

    def away(r):
        return far_order(z)[r]

    def weigh(c, kind, side_half, following, hook=None, hook_at=2):
        lanes = slice(c * chunk, (c + 1) * chunk)

        @pl.loop(0, per_half)
        def _(t):
            @pl.when(t + 1 < per_half)
            def _():
                for copy in h_copies(side_half, t + 1):
                    copy.start()

            for copy in h_copies(side_half, t):
                copy.wait()
            slot = lax.rem(t, 2)
            grad = lax.dot_general(
                h_buf[slot].reshape(4 * rows, cut),
                f_buf[:, :, lanes].reshape(4 * rows, chunk),
                TN,
                preferred_element_type=F32,
            )
            at = pl.multiple_of((side_half * per_half + t) * cut, 16)
            dw[c, pl.ds(at, cut), :] = grad.astype(BF16)
            if hook is not None:
                pl.when(t == hook_at)(hook)

        if following is not None:
            for copy in h_copies(following, 0):
                copy.start()
        if scatter:
            for r in range(far_count):
                core_copy(c, kind, side_half, away(r)).start()

    def add_to(c, at, ref, *index):
        dw[c, at, :] = (dw[c, at, :].astype(F32) + ref[index].astype(F32)).astype(BF16)

    def send_x(c):
        if scatter:
            for r in range(far_count):
                zz = away(r)
                core_copy(c, 0, 1 - batch, zz).wait_recv()
                add_to(c, block_rows(1 - batch, zz, core), core_in, c, 0, zz)
                x_copy(c, zz).start()

    def send_z(c):
        if scatter:
            for r in range(far_count):
                zz = away(r)
                core_copy(c, 1, batch, zz).wait_recv()
                x_copy(c, zz).wait_recv()
                at = block_rows(batch, zz, core)
                total = dw[c, at, :].astype(F32) + core_in[c, 1, zz].astype(F32) + x_in[c, zz].astype(F32)
                lanes = slice(c * chunk, (c + 1) * chunk)
                if r < 3:
                    dw[c, at, :] = total.astype(BF16)
                    if r < 2:
                        z_copy(c, r, zz).start()
                else:
                    dw_out[:, lanes] = total

    def relay_z(c):
        if scatter:
            zz = away(2)
            z_copy(c, 0, away(0)).wait_recv()
            add_to(c, block_rows(batch, zz, core), z_in, c, 0)
            z_copy(c, 2, zz).start()

    def finish(c):
        lanes = slice(c * chunk, (c + 1) * chunk)
        if scatter:
            for r in range(1, 3):
                z_copy(c, r, away(r)).wait_recv()
                dw_out[:, lanes] = dw_out[:, lanes] + z_in[c, r].astype(F32)
        else:
            copy = pltpu.make_async_copy(dw.at[c], dw_out.at[:, lanes], load_sem.at[4 + PIECES])
            copy.start()
            copy.wait()

    def ig_copies(m):
        copies = []
        for part in range(2):
            at = pl.ds(pl.multiple_of(ch * half_rows + part * pairs, 16), pairs)
            kept = pl.ds(pl.multiple_of(ch * local_in, 128), local_in)
            sent = pl.ds(pl.multiple_of((1 - ch) * local_in, 128), local_in)
            here = xs.at[part, m * pairs : (m + 1) * pairs]
            copies.append(pltpu.make_async_copy(here.at[:, kept], ig.at[m, at], ig_sem.at[m, part]))
            copies.append(
                pltpu.make_async_remote_copy(
                    here.at[:, sent],
                    ig.at[m, at],
                    ig_send.at[m, part],
                    ig_recv.at[m, part],
                    device_id=y_peer,
                    device_id_type=MESH,
                )
            )
        return copies

    def input_grad(m):
        scale = 1.0 / total_rows

        @pl.loop(0, wide // 128)
        def _(b):
            at = pl.ds(pl.multiple_of(b * 128, 128), 128)
            plain = r_result[2 * m : 2 * m + 1, at] * scale
            cross = r_result[2 * m + 1 : 2 * m + 2, at] * scale
            inverse = vec_ref[m, 3:4, at]
            for e in range(2):
                x = xs[e, m * pairs : (m + 1) * pairs, at].astype(F32)
                normed = (x - vec_ref[m, 0:1, at]) * inverse
                grad = a1g[e, m * pairs : (m + 1) * pairs, at]
                weave[pl.ds(e, pairs, stride=2), :] = vec_ref[m, 1:2, at] * (grad - plain - normed * cross)
            for part in range(2):
                xs[part, m * pairs : (m + 1) * pairs, at] = weave[part * pairs : (part + 1) * pairs, :].astype(BF16)

        for copy in ig_copies(m):
            copy.start()

    for j in range(3):
        back(j)
    if scatter:
        third.relay()
    loads()[0].wait()
    low_copy(0).wait_recv()
    low_copy(1).start()
    weigh(0, 0, 1 - batch, 1 - batch)
    send_x(0)
    back(3)
    if scatter:
        k2_copy().wait()
        for r in range(far_count):
            second.send_z(r)
    low_copy(1).wait_recv()
    low_copy(2).start()
    back(4)
    reduce.start(0)
    weigh(1, 0, 1 - batch, batch)
    reduce.start(1)
    send_x(1)
    if scatter:
        second.relay()
    weigh(0, 1, batch, 1 - batch)
    send_z(0)
    low_copy(2).wait_recv()
    weigh(2, 0, 1 - batch, batch)
    send_x(2)
    reduce.start(2)
    relay_z(0)
    weigh(1, 1, batch, batch)
    send_z(1)
    reduce.start(3)
    reduce.wait(3)
    sum_out[...] = r_result[...]
    for m in range(micro_count):
        input_grad(m)
    weigh(2, 1, batch, None)
    relay_z(1)
    if scatter:
        dw2_out[...] = second.send_y()
        dwp_out[...] = third.send_y()
    finish(0)
    send_z(2)
    finish(1)
    relay_z(2)
    finish(2)
    for m in range(micro_count):
        for copy in ig_copies(m):
            copy.wait()
    if scatter:
        dw2_out[...] += second.finish()
        dwp_out[...] += third.finish()
        second.drain()
        third.drain()
    else:
        dw2_out[...] = jnp.zeros_like(dw2_out)
        dwp_out[...] = jnp.zeros_like(dwp_out)
    for c in range(chunks):
        low_copy(c).wait_send()
        if scatter:
            for r in range(far_count):
                zz = away(r)
                core_copy(c, 0, 1 - batch, zz).wait_send()
                core_copy(c, 1, batch, zz).wait_send()
                x_copy(c, zz).wait_send()
                if r < far_count - 1:
                    z_copy(c, r, zz).wait_send()


def tail(pieces, other_pieces, grad_pieces, own, other, x_split, dw2, dwp, vecs, extra, total_rows):
    _, rows, wide = pieces.shape
    micro_count = vecs.shape[0]
    pairs = rows // micro_count
    out = grad_pieces.shape[-1]
    local_out = out // 2
    chunks = 3
    chunk = local_out // chunks
    far = lax.axis_size("pos") // 2
    rows_all = KW * wide
    block = rows_all // (4 * far)
    scatter = block % 16 == 0 and far == 4
    tile = 256
    land = block if scatter else 16
    block2 = dw2.shape[2] if scatter else 16
    any_space = pl.BlockSpec(memory_space=pl.ANY)
    in_vmem = pl.BlockSpec(memory_space=pltpu.VMEM)
    dma = pltpu.SemaphoreType.DMA
    return pl.pallas_call(
        functools.partial(tail_kernel, scatter, total_rows),
        out_shape=(
            jax.ShapeDtypeStruct((micro_count, 4 * pairs, wide // 2), BF16),
            jax.ShapeDtypeStruct((block, local_out) if scatter else (rows_all, local_out), F32 if scatter else BF16),
            jax.ShapeDtypeStruct((block2, local_out), F32),
            jax.ShapeDtypeStruct((block2, local_out), F32),
            jax.ShapeDtypeStruct((8, out), F32),
        ),
        in_specs=[any_space] * 8 + [in_vmem] * 2,
        out_specs=(any_space, in_vmem if scatter else any_space, in_vmem, in_vmem, in_vmem),
        scratch_shapes=[
            pltpu.VMEM((rows, PIECES * out), BF16),
            pltpu.VMEM((2, tile, KW * out), BF16),
            pltpu.VMEM((2, rows, wide), F32),
            pltpu.VMEM((2, rows, wide), BF16),
            pltpu.VMEM((2, 4, rows, wide // 2), BF16),
            pltpu.VMEM((4, rows, local_out), BF16),
            pltpu.VMEM((chunks, rows_all, chunk), BF16),
            pltpu.VMEM((chunks, 2, far, land, chunk), BF16),
            pltpu.VMEM((chunks, far, land, chunk), BF16),
            pltpu.VMEM((chunks, far - 1, land, chunk), BF16),
            pltpu.VMEM((2 * pairs, 128), F32),
            dma((5 + PIECES,)),
            dma((2, 2 * KW)),
            dma((2, 4)),
            dma((chunks,)),
            dma((chunks,)),
            dma((chunks, 2, far)),
            dma((chunks, 2, far)),
            dma((chunks, far)),
            dma((chunks, far)),
            dma((chunks, far - 1)),
            dma((chunks, far - 1)),
            dma((micro_count, 2)),
            dma((micro_count, 2)),
            dma((micro_count, 2)),
        ]
        + Reduce.scratch(out)
        + [pltpu.VMEM((far, block2, out), BF16)]
        + Scatter.scratch(block2, out)
        + [dma((far,)), dma((far,))]
        + Scatter.scratch(block2, out),
        compiler_params=params(collective_id=5, has_side_effects=True),
        name="tail",
    )(
        pieces,
        other_pieces,
        grad_pieces,
        own.reshape(KW, wide, local_out),
        other.reshape(KW, wide, local_out),
        x_split,
        dw2,
        dwp,
        vecs,
        extra,
    )


def rows_kernel(table, index, *refs):
    vectors, (rows, limits) = refs[:-2], refs[-2:]
    rows[...] = jnp.zeros_like(rows)
    for i, ref in enumerate(vectors):
        width = ref.shape[0]
        rows[i : i + 1, 0:width] = ref[...].reshape(1, width)
    for m in range(limits.shape[0]):
        limits[m] = jnp.full(limits.shape[1:], table[index[m]], F32)


def gather_rows(table, index, vectors, width):
    in_vmem = pl.BlockSpec(memory_space=pltpu.VMEM)
    in_smem = pl.BlockSpec(memory_space=pltpu.SMEM)
    return pl.pallas_call(
        rows_kernel,
        out_shape=(
            jax.ShapeDtypeStruct((8, width), F32),
            jax.ShapeDtypeStruct((index.shape[0], 8, 128), F32),
        ),
        in_specs=[in_smem] * 2 + [in_vmem] * len(vectors),
        out_specs=(in_vmem, in_vmem),
        name="rows",
    )(table, index, *vectors)


def collect_kernel(part, sums3, *refs):
    count = 5
    sources, targets, vectors = refs[:count], refs[count : 2 * count], refs[2 * count : 2 * count + 6]
    held, sems = refs[2 * count + 6 : -1], refs[-1]
    loads = [pltpu.make_async_copy(a, h, sems.at[0, i]) for i, (a, h) in enumerate(zip(sources, held))]
    copies = [pltpu.make_async_copy(h, b, sems.at[1, i]) for i, (h, b) in enumerate(zip(held, targets))]
    for load in loads:
        load.start()
    for load, copy in zip(loads, copies):
        load.wait()
        copy.start()
    ch = lax.axis_index("ch")
    micro_count = 2

    def put(dst, ref, rows):
        width = dst.shape[0]
        at = pl.ds(pl.multiple_of(ch * width, 128), width)
        total = ref[rows[0] : rows[0] + 1, at]
        for r in rows[1:]:
            total = total + ref[r : r + 1, at]
        dst[...] = total.reshape(width)

    ms = range(micro_count)
    put(vectors[0], part, [2 * m + 1 for m in ms])
    put(vectors[1], part, [2 * m for m in ms])
    put(vectors[2], part, [2 * micro_count + m for m in ms])
    put(vectors[3], sums3, [3 * m + 1 for m in ms])
    put(vectors[4], sums3, [3 * m for m in ms])
    put(vectors[5], sums3, [3 * m + 2 for m in ms])
    for copy in copies:
        copy.wait()


def collect(arrays, part, sums3, local_in, local_out):
    any_space = pl.BlockSpec(memory_space=pl.ANY)
    in_vmem = pl.BlockSpec(memory_space=pltpu.VMEM)
    widths = [local_in, local_in] + [local_out] * 4
    return pl.pallas_call(
        collect_kernel,
        out_shape=tuple(jax.ShapeDtypeStruct(v.shape, v.dtype) for v in arrays)
        + tuple(jax.ShapeDtypeStruct((w,), F32) for w in widths),
        in_specs=[in_vmem] * 2 + [any_space] * 5,
        out_specs=(any_space,) * 5 + (in_vmem,) * 6,
        scratch_shapes=[pltpu.VMEM(v.shape, v.dtype) for v in arrays] + [pltpu.SemaphoreType.DMA((2, 5))],
        compiler_params=params(),
        name="collect",
    )(part, sums3, *arrays)


def local(
    section_input,
    norm1_gain,
    norm1_bias,
    conv1_weight,
    conv1_bias,
    norm2_gain,
    norm2_bias,
    conv2_weight,
    conv2_bias,
    pool_weight,
    out_grad,
    clip_table,
    clip_index,
):
    micro_count, seq_count, local_rows, local_in = section_input.shape
    batch_count, pos_count, ch_count = (lax.axis_size(a) for a in ("batch", "pos", "ch"))
    batch, pos, ch = (lax.axis_index(a) for a in ("batch", "pos", "ch"))
    total_rows = seq_count * local_rows * batch_count * pos_count
    wide_in = 2 * local_in
    local_out = conv1_weight.shape[1]
    wide_out = 2 * local_out
    half = local_rows // 2
    pairs = half // 2
    plane = batch_count * pos_count
    spot = batch * pos_count + pos
    swap = [(0, 1), (1, 0)]
    is_low = ch == 0

    def other_ch(v):
        return lax.ppermute(v, "ch", swap)

    def natural(own, other, axis):
        return jnp.where(
            is_low,
            jnp.concatenate([own, other], axis=axis),
            jnp.concatenate([other, own], axis=axis),
        )

    x = section_input.reshape(micro_count, local_rows, local_in)

    def own_first(v):
        return jnp.where(
            is_low, v, jnp.concatenate([v[..., local_out:], v[..., :local_out]], axis=-1)
        )

    to_natural = own_first
    bins = local_rows // 2
    mine = bins // 2
    small, limits = gather_rows(
        clip_table,
        clip_index,
        (conv1_bias, norm2_gain, norm2_bias, conv2_bias, norm1_gain, norm1_bias),
        local_out,
    )
    (
        pieces,
        x_split,
        first_own,
        first_other,
        w1_other,
        w2_other,
        wp_other,
        og_full,
        vec1,
        vec2,
    ) = head(
        x,
        conv1_weight,
        conv2_weight,
        pool_weight,
        out_grad.reshape(micro_count, bins, local_out),
        small,
        total_rows,
    )
    first_own = first_own.reshape(2, micro_count, pairs, local_out)
    first_other = first_other.reshape(2, micro_count, pairs, local_out)
    section_output, grad_pieces, _, other_pieces, dw2, dwp, sums3, extra = middle(
        first_own,
        first_other,
        (conv2_weight, w2_other, pool_weight, wp_other),
        og_full,
        x,
        vec2,
        vec1,
        limits,
        total_rows,
    )
    whole_two, whole_pool = dw2, dwp
    input_grad, dw1, dw2, dwp, part = tail(
        pieces, other_pieces, grad_pieces, conv1_weight, w1_other, x_split, dw2, dwp, vec1, extra, total_rows
    )

    def scatter(v):
        return lax.psum_scatter(v, ("batch", "pos"), scatter_dimension=0, tiled=True).astype(F32)

    def fold(v):
        v = jnp.where(is_low, v, jnp.concatenate([v[local_out:], v[:local_out]], axis=0))
        away = other_ch(v[:, local_out:])
        return scatter((v[:, :local_out].astype(F32) + away.astype(F32)).astype(BF16))

    if whole_pool.ndim == 2:
        dw2, dwp = fold(whole_two), fold(whole_pool)
    if dw1.shape[0] != KW * wide_in // plane:
        dw1 = scatter(dw1)
    section_output, input_grad, dw1, dw2, dwp, *vectors = collect(
        (section_output, input_grad, dw1, dw2, dwp), part, sums3, local_in, local_out
    )
    return (
        section_output.reshape(micro_count, seq_count, bins, local_out),
        input_grad.reshape(section_input.shape),
        vectors[0],
        vectors[1],
        dw1,
        vectors[2],
        vectors[3],
        vectors[4],
        dw2,
        vectors[5],
        dwp,
    )


def solution(mesh):
    placed = (
        P(None, "batch", "pos", "ch"),
        P("ch"),
        P("ch"),
        P(None, "ch"),
        P("ch"),
        P("ch"),
        P("ch"),
        P(None, "ch"),
        P("ch"),
        P(None, "ch"),
        P(None, "batch", "pos", "ch"),
        P(),
        P(),
    )
    return jax.shard_map(
        local,
        mesh=mesh,
        in_specs=placed,
        out_specs=(
            P(None, "batch", "pos", "ch"),
            P(None, "batch", "pos", "ch"),
            P("ch"),
            P("ch"),
            P(("batch", "pos"), "ch"),
            P("ch"),
            P("ch"),
            P("ch"),
            P(("batch", "pos"), "ch"),
            P("ch"),
            P(("batch", "pos"), "ch"),
        ),
        check_vma=False,
    )
```
